32 devices in a mesh: dp: 8 (over z, x), tp: 4 (over y, core).
Axes of the slice: x: 2, y: 2, z: 4, core: 2. Of those that a mesh axis runs over, the one named last changes fastest.
Arguments:
- tokens: bfloat16 [2, 8192, 768], P(None, ('dp', 'tp')), may hold values from -6 to 6
- cotangent: bfloat16 [2, 8192, 768], P(None, ('dp', 'tp')), may hold values from -6 to 6
- doc_ends: int32 [2, 8, 4], P(None, 'dp'), may hold values from 1 to 1024, as said below
- pos_scale: int32 [2, 8, 4], P(None, 'dp'), may hold values from 1 to 4
- first_gain: float32 [768], replicated, may hold values from 0.5 to 1.5
- first_bias: float32 [768], replicated, may hold values from -1 to 1
- second_gain: float32 [768], replicated, may hold values from 0.5 to 1.5
- second_bias: float32 [768], replicated, may hold values from -1 to 1
- w_query: bfloat16 [768, 768], P(None, 'tp'), may hold values from -0.21875 to 0.21875
- query_bias: float32 [768], P('tp'), may hold values from -1.5 to 1.5
- w_shared: bfloat16 [768, 128], replicated, may hold values from -0.21875 to 0.21875
- shared_bias: float32 [128], replicated, may hold values from -1.5 to 1.5
- w_output: bfloat16 [768, 768], P('tp'), may hold values from -0.875 to 0.875
- w_expand: bfloat16 [768, 3072], P(None, 'tp'), may hold values from -0.21875 to 0.21875
- expand_bias: float32 [3072], P('tp'), may hold values from -1.5 to 1.5
- w_contract: bfloat16 [3072, 768], P('tp'), may hold values from -0.109375 to 0.109375
- output_bias: float32 [768], replicated, may hold values from -2.5 to 2.5
Outputs:
- layer_out: bfloat16 [2, 8192, 768], P(None, ('dp', 'tp'))
- input_grad: float32 [2, 8192, 768], P(None, ('dp', 'tp'))
- query_grad: float32 [768, 768], P(None, 'tp')
- query_bias_grad: float32 [768], P('tp')
- shared_grad: float32 [768, 128], replicated
- shared_bias_grad: float32 [128], replicated
- output_grad: float32 [768, 768], P('tp')
- expand_grad: float32 [768, 3072], P(None, 'tp')
- expand_bias_grad: float32 [3072], P('tp')
- contract_grad: float32 [3072, 768], P('tp')
- output_bias_grad: float32 [768], replicated
- first_gain_grad: float32 [768], replicated
- first_bias_grad: float32 [768], replicated
- second_gain_grad: float32 [768], replicated
- second_bias_grad: float32 [768], replicated
The draws below stay inside these ranges and needn't reach their ends.
Inputs may be any that keep to these rules, and one draw needn't show every extreme that they name: `doc_ends`: for each pack the 4 entries rise strictly and the last is 1024; document d holds the rows from the previous entry (0 for the first document) up to its own entry, exclusive.
All inputs are finite; a program needn't handle non-finite values.
Results may differ from the reference program's by a relative error of at most 0.012.
Values may be sent and summed in bfloat16 or wider, within the bound.
No kernel may reach another device: no remote copies, remote signals or barrier semaphores. Data moves between devices by JAX's collectives and lax.ppermute only.
A program may use at most 128 MiB of HBM per device.

```python
import jax
import jax.numpy as jnp
from jax import lax

D = 768
HEADS = 12
HD = 64
FF = 3072
ROT = 16
SEQ = 1024
MICRO = 2
DOCS = 4
ROWS = 8192
N_DP = 8


def draw_doc_ends(key, part):
    key = jax.random.fold_in(key, 7)
    subkeys = jax.random.split(key, 4)
    grid_shape = (MICRO, N_DP)
    first_end = jax.random.randint(subkeys[0], grid_shape, 1, SEQ // 4)
    second_end = jax.random.randint(subkeys[1], grid_shape, 3 * SEQ // 4 + 1, SEQ - 1)
    third_end = jax.random.randint(subkeys[2], grid_shape, second_end + 1, SEQ)
    lengths = jnp.stack([first_end, second_end - first_end, third_end - second_end, SEQ - third_end], -1)
    flipped = jax.random.randint(subkeys[3], grid_shape, 0, 2)
    lengths = jnp.where(flipped[..., None] == 1, lengths[..., ::-1], lengths)
    return jnp.cumsum(lengths, -1).astype(jnp.int32)


def plant(values, rng, smallest, high):
    longest = values.shape.index(max(values.shape))
    spots = []
    for shift in (0, 1):
        where = [jax.random.randint(jax.random.fold_in(rng, axis), (), 0, length) for axis, length in enumerate(values.shape)]
        where[longest] = (where[longest] + shift) % values.shape[longest]
        spots.append(tuple(where))
    return values.at[spots[0]].set(smallest).at[spots[1]].set(high)


def levels(stream_key, shape, cuts, smallest, top_value):
    loudness = 1.0
    for dim, parts in cuts:
        steps = jax.random.uniform(jax.random.fold_in(jax.random.fold_in(stream_key, 6), dim), (parts,), jnp.float32, smallest / len(cuts), top_value / len(cuts))
        loudness = loudness * jnp.repeat(jnp.exp(steps), shape[dim] // parts).reshape((-1,) + (1,) * (len(shape) - 1 - dim))
    return loudness


def bell_draw(key, extent, scale, reach, pieces=(), held_as=jnp.bfloat16):
    values = jax.random.normal(key, extent, jnp.float32) * scale
    if len(pieces) > 0:
        values = levels(key, extent, pieces, -0.22, 0.18) * values
    return jnp.clip(values, min=-reach, max=reach).astype(held_as)


def setup_inputs(seed: int = 0) -> dict:
    seeds = jax.random.split(jax.random.key(seed), 18)
    return {
        "tokens": bell_draw(seeds[0], (MICRO, ROWS, D), 1.0, 6.0, ((1, 32),)),
        "cotangent": bell_draw(seeds[1], (MICRO, ROWS, D), 1.0, 6.0, ((1, 32),)),
        "doc_ends": draw_doc_ends(jax.random.fold_in(seeds[17], 71), 0),
        "pos_scale": plant(jax.random.randint(seeds[3], (MICRO, N_DP, DOCS), 1, 5), jax.random.fold_in(seeds[3], 1), 1, 4).astype(jnp.int32),
        "first_gain": jnp.clip(1.0 + 0.1 * jax.random.normal(seeds[4], (D,), jnp.float32), 0.5, 1.5),
        "first_bias": bell_draw(seeds[5], (D,), 0.2, 1.0, (), jnp.float32),
        "second_gain": jnp.clip(1.0 + 0.1 * jax.random.normal(seeds[6], (D,), jnp.float32), 0.5, 1.5),
        "second_bias": bell_draw(seeds[7], (D,), 0.2, 1.0, (), jnp.float32),
        "w_query": bell_draw(seeds[8], (D, HEADS * HD), D ** -0.5, 0.21875, ((1, 4),)),
        "query_bias": bell_draw(seeds[9], (HEADS * HD,), 0.3, 1.5, ((0, 4),), jnp.float32),
        "w_shared": bell_draw(seeds[10], (D, 2 * HD), D ** -0.5, 0.21875),
        "shared_bias": bell_draw(seeds[11], (2 * HD,), 0.3, 1.5, (), jnp.float32),
        "w_output": bell_draw(seeds[12], (HEADS * HD, D), (HEADS * HD // 16) ** -0.5, 0.875, ((0, 4),)),
        "w_expand": bell_draw(seeds[13], (D, FF), D ** -0.5, 0.21875, ((1, 4),)),
        "expand_bias": bell_draw(seeds[14], (FF,), 0.3, 1.5, ((0, 4),), jnp.float32),
        "w_contract": bell_draw(seeds[15], (FF, D), FF ** -0.5, 0.109375, ((0, 4),)),
        "output_bias": bell_draw(seeds[16], (D,), 0.5, 2.5, (), jnp.float32),
    }


@jax.custom_vjp
def low(v):
    return lax.optimization_barrier(v.astype(jnp.bfloat16)).astype(jnp.float32)

@jax.custom_vjp
def low_back(v):
    return v

def low_keep(v):
    return (low(v), None)

def low_pass(kept, grad):
    return (grad,)

def back_keep(v):
    return (v, None)

def back_low(kept, grad):
    return (low(grad),)
low.defvjp(low_keep, low_pass)
low_back.defvjp(back_keep, back_low)

def norm_rows(values, gain, shift):
    centre = values - lax.optimization_barrier(jnp.mean(values, -1, keepdims=True))
    spread = lax.optimization_barrier(jnp.mean(centre * centre, -1, keepdims=True))
    return centre * lax.rsqrt(spread + 1e-05) * gain + shift

def rotate(values, cosine, sine):
    half = cosine.shape[-1]
    first = values[..., :half]
    second = values[..., half:2 * half]
    return jnp.concatenate([first * cosine - second * sine, second * cosine + first * sine, values[..., 2 * half:]], -1)

def doc_layout(ends, scales, length):
    row_ids = jnp.arange(length, dtype=jnp.int32)
    doc_ids = lax.optimization_barrier(jnp.sum((row_ids[:, None] >= ends[None, :]).astype(jnp.int32), 1)).astype(jnp.int32)
    starts = jnp.concatenate([jnp.zeros((1,), jnp.int32), ends[:-1].astype(jnp.int32)])
    onehot = doc_ids[:, None] == jnp.arange(ends.shape[0], dtype=jnp.int32)[None, :]
    begins = lax.optimization_barrier(jnp.sum(jnp.where(onehot, starts[None, :], 0), 1)).astype(jnp.int32)
    steps_of = lax.optimization_barrier(jnp.sum(jnp.where(onehot, scales[None, :].astype(jnp.int32), 0), 1)).astype(jnp.int32)
    return (doc_ids, ((row_ids - begins) * steps_of).astype(jnp.int32))

def angle_tables(placed):
    freqs = 10000.0 ** (-jnp.arange(ROT // 2, dtype=jnp.float32) * 2.0 / ROT)
    angles = placed.astype(jnp.float32)[:, None] * freqs[None, :]
    return (jnp.cos(angles), jnp.sin(angles))

def pack_forward(inputs, ends, scales, weights):
    first_gain, first_bias, second_gain, second_bias, w_query, query_bias, w_shared, shared_bias, w_output, w_expand, expand_bias, w_contract, output_bias = weights
    highest = lax.Precision.HIGHEST
    length = inputs.shape[0]
    doc_ids, placed = doc_layout(ends, scales, length)
    cosine, sine = angle_tables(placed)
    first_low = low(norm_rows(inputs, first_gain, first_bias))
    second_low = low(norm_rows(inputs, second_gain, second_bias))
    queries = low_back(jnp.dot(first_low, w_query, precision=highest) + query_bias).reshape(length, HEADS, HD)
    shared = low_back(jnp.dot(first_low, w_shared, precision=highest) + shared_bias)
    queries_rot = low(rotate(queries, cosine[:, None, :], sine[:, None, :]))
    keys_rot = low(rotate(shared[:, :HD], cosine, sine))
    values_low = low(shared[:, HD:])
    raw = jnp.einsum('qhd,kd->hqk', queries_rot, keys_rot, precision=highest) * 0.125
    row_ids = jnp.arange(length, dtype=jnp.int32)
    allowed = (row_ids[None, :] <= row_ids[:, None]) & (doc_ids[None, :] == doc_ids[:, None])
    scores = low_back(jnp.where(allowed[None], raw, -1e+30))
    row_max = lax.optimization_barrier(jnp.max(scores, -1, keepdims=True))
    exp_scores = jnp.exp(scores - row_max)
    attention = low(exp_scores / lax.optimization_barrier(jnp.sum(exp_scores, -1, keepdims=True)))
    context = jnp.einsum('hqk,kd->qhd', attention, values_low, precision=highest).reshape(length, HEADS * HD)
    context = low(low_back(context))
    expanded = low_back(jnp.dot(second_low, w_expand, precision=highest) + expand_bias)
    activated = low(jax.nn.gelu(expanded, approximate=False))
    return inputs + jnp.dot(context, w_output, precision=highest) + jnp.dot(activated, w_contract, precision=highest) + output_bias

def layer(inputs, *weights):
    packs = inputs.reshape(MICRO, N_DP, SEQ, D).transpose(1, 0, 2, 3)
    return (packs, weights)

def reference(tokens, cotangent, doc_ends, pos_scale, first_gain, first_bias, second_gain, second_bias, w_query, query_bias, w_shared, shared_bias, w_output, w_expand, expand_bias, w_contract, output_bias):
    floats = [a.astype(jnp.float32) for a in (tokens, first_gain, first_bias, second_gain, second_bias, w_query, query_bias, w_shared, shared_bias, w_output, w_expand, expand_bias, w_contract, output_bias)]
    ends_all = doc_ends.transpose(1, 0, 2)
    scales_all = pos_scale.transpose(1, 0, 2)

    def advance(weights, batch):
        packs, ends, scales = batch
        outputs = jax.vmap(lambda a, b, c: pack_forward(a, b, c, weights))(packs, ends, scales)
        return (weights, outputs)

    def whole(inputs, *weights):
        packs = inputs.reshape(MICRO, N_DP, SEQ, D).transpose(1, 0, 2, 3)
        _, outputs = lax.scan(jax.checkpoint(advance), tuple(weights), (packs, ends_all, scales_all))
        return outputs.transpose(1, 0, 2, 3).reshape(MICRO, N_DP * SEQ, D)
    result, pullback = jax.vjp(whole, *floats)
    grads = pullback(cotangent.astype(jnp.float32))
    return (result.astype(jnp.bfloat16), grads[0], grads[5], grads[6], grads[7], grads[8], grads[9], grads[10], grads[11], grads[12], grads[13], grads[1], grads[2], grads[3], grads[4])
```

```python
import functools

import jax
import jax.numpy as jnp
from jax import lax
from jax.experimental import pallas as pl
from jax.experimental.pallas import tpu as pltpu
from jax.sharding import PartitionSpec as P

ROT = 16
LANES = 128
QW = 256
SHRINK = 8
BF = jnp.bfloat16
F32 = jnp.float32
KEEP = (0, 4, 2, 6)
SEND = (1, 5, 3, 7)
NT = (((1,), (1,)), ((), ()))
TN = (((0,), (0,)), ((), ()))
ANY = pl.BlockSpec(memory_space=pl.ANY)
VMEM = pl.BlockSpec(memory_space=pltpu.VMEM)
SMEM = pl.BlockSpec(memory_space=pltpu.SMEM)


def dot(a, b):
    return jnp.dot(a, b, preferred_element_type=F32)


def dot_nt(a, b):
    return lax.dot_general(a, b, NT, preferred_element_type=F32)


def dot_tn(a, b):
    return lax.dot_general(a, b, TN, preferred_element_type=F32)


def shape(dims, dtype=BF):
    return jax.ShapeDtypeStruct(dims, dtype)


def call(kernel, name, ins, outs, scratch, copies, flops):
    specs = [s for _, s in ins]
    arrays = [a for a, _ in ins]
    nbytes = sum(a.size * a.dtype.itemsize for a in arrays)
    return pl.pallas_call(
        kernel,
        in_specs=specs,
        out_specs=[s for _, s in outs],
        out_shape=[o for o, _ in outs],
        scratch_shapes=list(scratch) + [pltpu.SemaphoreType.DMA((copies,))],
        compiler_params=pltpu.CompilerParams(vmem_limit_bytes=60 * 2**20),
        cost_estimate=pl.CostEstimate(
            flops=int(flops) // SHRINK, bytes_accessed=int(nbytes) // SHRINK, transcendentals=0
        ),
        name=name,
    )(*arrays)


class Copies:
    def __init__(self, sems):
        self.sems = sems
        self.count = 0

    def start(self, src, dst):
        copy = pltpu.make_async_copy(src, dst, self.sems.at[self.count])
        self.count += 1
        copy.start()
        return copy


def normalize(x):
    centre = x - jnp.mean(x, -1, keepdims=True)
    spread = jnp.mean(centre * centre, -1, keepdims=True)
    return centre * lax.rsqrt(spread + 1e-05)


def swap_halves(w):
    lane = lax.broadcasted_iota(jnp.int32, w.shape, 1)
    up = pltpu.roll(w, w.shape[1] - ROT // 2, 1)
    down = pltpu.roll(w, ROT // 2, 1)
    return jnp.where((lane % 64) < ROT // 2, up, down)


def spread_table(compact, filler, signs):
    fill = jnp.full((64 - ROT, compact.shape[1]), filler, F32)
    head = [signs * compact, compact, fill]
    return jnp.concatenate(head + head, 0).T


def hidden_kernel(xo, xc, xy, xd, gb, we, be, acto, slopeo, xs, wev, acts, slopes, sems):
    copies = Copies(sems)
    got = [copies.start(x, xs.at[r]) for r, x in enumerate((xo, xc))]
    gotw = copies.start(we, wev)
    got += [copies.start(x, xs.at[2 + r]) for r, x in enumerate((xy, xd))]
    out = []
    for r in range(4):
        got[r].wait()
        n = normalize(xs[r].astype(F32))
        h2 = (n * gb[2:3] + gb[3:4]).astype(BF)
        if r == 0:
            gotw.wait()
        u = dot(h2, wev[...]) + be[...]
        phi = 0.5 * (1.0 + lax.erf(u * 0.7071067811865476))
        acts[r] = (u * phi).astype(BF)
        slopes[r] = (phi + u * jnp.exp(-0.5 * u * u) * 0.3989422804014327).astype(BF)
        out.append(copies.start(acts.at[r], acto.at[r]))
        out.append(copies.start(slopes.at[r], slopeo.at[r]))
    for c in out:
        c.wait()


def hidden(xs, gb, we, be):
    rows, feat = xs[0].shape
    ff = we.shape[1]
    stack = (4, rows, ff)
    return call(
        hidden_kernel,
        "hidden",
        [(x, ANY) for x in xs] + [(gb, VMEM), (we, ANY), (be, VMEM)],
        [(shape(stack), ANY)] * 2,
        [
            pltpu.VMEM((4, rows, feat), BF),
            pltpu.VMEM(we.shape, BF),
            pltpu.VMEM(stack, BF),
            pltpu.VMEM(stack, BF),
        ],
        13,
        8 * rows * feat * ff,
    )


def doubled(kv):
    kv = kv.astype(F32)
    swapped = pltpu.roll(kv, 64, 1)
    low = lax.broadcasted_iota(jnp.int32, kv.shape, 1) < 64
    return jnp.where(low, kv, swapped).astype(BF), jnp.where(low, swapped, kv).astype(BF)


def stack_heads(block, heads):
    low = lax.broadcasted_iota(jnp.int32, (block.shape[0], LANES), 1) < 64
    zero = jnp.zeros((block.shape[0], LANES), block.dtype)
    parts = []
    for h in range(heads):
        part = block[:, LANES * (h // 2) : LANES * (h // 2 + 1)]
        parts.append(jnp.where(low, part, zero) if h % 2 == 0 else jnp.where(low, zero, part))
    return jnp.concatenate(parts, 0)


def join_heads(stacked, heads, rows):
    low = lax.broadcasted_iota(jnp.int32, (rows, LANES), 1) < 64
    part = lambda h: stacked[h * rows : (h + 1) * rows]
    zero = jnp.zeros((rows, LANES), stacked.dtype)
    cols = []
    for h in range(0, heads, 2):
        cols.append(jnp.where(low, part(h), part(h + 1) if h + 1 < heads else zero))
    return jnp.concatenate(cols, 1)


def attention_kernel(heads, first, *refs):
    refs = list(refs)
    take = lambda k: [refs.pop(0) for _ in range(k)]
    t_ref, ends = take(2)
    xpieces, gpieces = take(4), take(4)
    act, wt, bqkv, wo, wc, gb, cs, sn = take(8)
    if not first:
        e2, og_in, qs_in, vec_in = take(4)
    outm, outs, em, es, og, qs, vec = take(7)
    xs, gs, acts, wts, wos, wcs, h1s, ns, qrs, kk, vv, cx, dctx, p0, p1, p2, p3, ds, dk, dv = take(20)
    dqkv, outb, eb = take(3)
    if not first:
        e2s = take(1)[0]
    copies = Copies(take(1)[0])
    rows = xs.shape[1]
    t = t_ref[0]
    got_x = [copies.start(x, xs.at[r]) for r, x in enumerate(xpieces)]
    got_wt = copies.start(wt, wts)
    got_wo, got_wc = copies.start(wo, wos), copies.start(wc, wcs)
    got_act = copies.start(act, acts)
    got_g = [copies.start(g, gs.at[r ^ t]) for r, g in enumerate(gpieces)]
    if not first:
        got_e2 = copies.start(e2, e2s)
    block = lambda a: pl.ds(pl.multiple_of(a * rows, rows), rows)

    for r in range(4):
        a = r ^ t
        got_x[r].wait()
        n = normalize(xs[r].astype(F32))
        ns[a] = n.astype(BF)
        h1 = (n * gb[0:1] + gb[1:2]).astype(BF)
        h1s[block(a)] = h1
        if r == 0:
            got_wt.wait()
        qkv = dot_nt(h1, wts[...]) + bqkv[...]
        c = spread_table(cs[a], 1.0, 1.0)
        s = spread_table(sn[a], 0.0, -1.0)
        low = lax.broadcasted_iota(jnp.int32, c.shape, 1) < 64
        cos = jnp.concatenate([c, c, jnp.where(low, c, 1.0)], 1)
        sin = jnp.concatenate([s, s, jnp.where(low, s, 0.0)], 1)
        qkv = qkv * cos + swap_halves(qkv) * sin
        qrs[a] = (qkv[:, :QW] * 0.125).astype(BF)
        kk[block(a)], vv[block(a)] = doubled(qkv[:, QW:].astype(BF))

    for a, probs in enumerate((p0, p1, p2, p3)):
        span = (a + 1) * rows
        row = lax.broadcasted_iota(jnp.int32, (rows, 1), 0) + a * rows
        begin = jnp.zeros((rows, 1), jnp.int32)
        for d in range(ends.shape[0] - 1):
            begin = jnp.where(row >= ends[d], ends[d], begin)
        col = lax.broadcasted_iota(jnp.int32, (rows, span), 1)
        allowed = (col >= begin) & (col <= row)
        scores = dot_nt(stack_heads(qrs[a], heads), kk[:span])
        for h in range(heads):
            s = jnp.where(allowed, scores[h * rows : (h + 1) * rows], -1e30)
            e = jnp.exp(s - jnp.max(s, -1, keepdims=True))
            probs[h * rows : (h + 1) * rows] = (e * (1.0 / jnp.sum(e, -1, keepdims=True))).astype(BF)
        cx[a] = join_heads(dot(probs[...], vv[:span]), heads, rows).astype(BF)

    got_wo.wait()
    got_wc.wait()
    got_act.wait()
    sent = []
    for r in range(4):
        outb[r] = (dot(cx[r ^ t], wos[...]) + dot(acts[r], wcs[...])).astype(BF)
        sent.append(copies.start(outb.at[r], (outs if r % 2 else outm).at[r // 2]))

    for g in got_g:
        g.wait()
    grads = gs[...].reshape(4 * rows, gs.shape[2])
    dctx[...] = dot_nt(grads, wos[...]).astype(BF)
    ograd = dot_tn(cx[...].reshape(4 * rows, QW), grads)
    og[...] = ograd if first else og_in[...] + ograd

    dk[...] = jnp.zeros_like(dk)
    dv[...] = jnp.zeros_like(dv)
    for a, probs in enumerate((p0, p1, p2, p3)):
        span = (a + 1) * rows
        here = slice(a * rows, (a + 1) * rows)
        queries = stack_heads(qrs[a], heads)
        back = stack_heads(dctx[here], heads)
        dprobs = dot_nt(back, vv[:span])
        for h in range(heads):
            mine = slice(h * rows, (h + 1) * rows)
            p = probs[mine].astype(F32)
            weighted = p * dprobs[mine]
            delta = jnp.sum(weighted, -1, keepdims=True)
            ds[mine, :span] = (weighted - p * delta).astype(BF)
        dscores = ds[:, :span]
        dk[:span] += dot_tn(dscores, queries)
        dv[:span] += dot_tn(probs[...], back)
        dq = join_heads(dot(dscores, kk[:span]), heads, rows) * 0.125
        c = spread_table(cs[a], 1.0, 1.0)
        s = spread_table(sn[a], 0.0, -1.0)
        cos = jnp.concatenate([c, c], 1)
        sin = jnp.concatenate([s, s], 1)
        dqkv[here, :QW] = (dq * cos - swap_halves(dq) * sin).astype(BF)
    for a in range(4):
        here = slice(a * rows, (a + 1) * rows)
        c = spread_table(cs[a], 1.0, 1.0)
        s = spread_table(sn[a], 0.0, -1.0)
        dkf = dk[here] + pltpu.roll(dk[here], 64, 1)
        dvf = dv[here] + pltpu.roll(dv[here], 64, 1)
        dkf = dkf * c - swap_halves(dkf) * s
        low = lax.broadcasted_iota(jnp.int32, dkf.shape, 1) < 64
        dqkv[here, QW:] = jnp.where(low, dkf, dvf).astype(BF)

    qgrad = dot_tn(dqkv[...], h1s[...])
    qs[...] = qgrad if first else qs_in[...] + qgrad
    if not first:
        got_e2.wait()
    width = QW + LANES
    gain = jnp.zeros((1, gb.shape[1]), F32)
    bias = jnp.zeros((1, gb.shape[1]), F32)
    for r in range(4):
        a = r ^ t
        e1 = dot(dqkv[block(a)], wts[...])
        gain += jnp.sum(e1 * ns[a].astype(F32), 0, keepdims=True)
        bias += jnp.sum(e1, 0, keepdims=True)
        e = e1 * gb[0:1]
        if not first:
            e += e2s[r].astype(F32)
        eb[r] = e.astype(BF)
        sent.append(copies.start(eb.at[r], (es if r % 2 else em).at[r // 2]))
    column = jnp.sum(dqkv[...].astype(F32), 0, keepdims=True)
    column = jnp.concatenate([column, jnp.zeros((1, gb.shape[1] - width), F32)], 1)
    rowid = lax.broadcasted_iota(jnp.int32, vec.shape, 0)
    both = jnp.where(rowid == 0, gain, jnp.where(rowid == 1, bias, jnp.where(rowid == 2, column, 0.0)))
    vec[...] = both if first else vec_in[...] + both
    for c in sent:
        c.wait()


def attention(rank, ends, xs, gs, act, wt, bqkv, wo, wc, gb, cs, sn, heads, before=None):
    rows, feat = xs[0].shape
    ff = wc.shape[0]
    width = QW + LANES
    length = 4 * rows
    first = before is None
    ins = [(rank, SMEM), (ends, SMEM)] + [(a, ANY) for a in (*xs, *gs, act, wt)]
    ins += [(bqkv, VMEM), (wo, ANY), (wc, ANY), (gb, VMEM), (cs, VMEM), (sn, VMEM)]
    if not first:
        ins += [(before[0], ANY)] + [(a, VMEM) for a in before[1:]]
    halves = (shape((2, rows, feat)), ANY)
    outs = [halves] * 4 + [
        (shape((QW, feat), F32), VMEM),
        (shape((width, feat), F32), VMEM),
        (shape((8, feat), F32), VMEM),
    ]
    stack = pltpu.VMEM((4, rows, feat), BF)
    scratch = [
        stack, stack, pltpu.VMEM((4, rows, ff), BF), pltpu.VMEM((width, feat), BF),
        pltpu.VMEM((QW, feat), BF), pltpu.VMEM((ff, feat), BF),
        pltpu.VMEM((length, feat), BF), stack, pltpu.VMEM((4, rows, QW), BF),
        pltpu.VMEM((length, LANES), BF), pltpu.VMEM((length, LANES), BF),
        pltpu.VMEM((4, rows, QW), BF), pltpu.VMEM((length, QW), BF),
    ]
    scratch += [pltpu.VMEM((heads * rows, (a + 1) * rows), BF) for a in range(4)]
    scratch += [
        pltpu.VMEM((heads * rows, length), BF),
        pltpu.VMEM((length, LANES), F32), pltpu.VMEM((length, LANES), F32),
        pltpu.VMEM((length, width), BF), stack, stack,
    ]
    if not first:
        scratch.append(stack)
    return call(
        functools.partial(attention_kernel, heads, first), "attention", ins, outs, scratch, 21, 1e10
    )


def store_parts(acc, outs, me):
    part = acc.shape[0] // 8
    half = part // 2
    for j in range(2):
        for out, order in ((outs[2 * j], KEEP), (outs[2 * j + 1], SEND)):
            for i in range(4):
                start = pl.multiple_of((order[i] ^ me) * part + j * half, 16)
                out[i] = acc[pl.ds(start, half)].astype(BF)


def contract_kernel(first, *refs):
    refs = list(refs)
    take = lambda k: [refs.pop(0) for _ in range(k)]
    me_ref, go, gc, gy, gd, act = take(6)
    if not first:
        acc_in, gsum_in = take(2)
    outs = take(1 if first else 4)
    gsum, = take(1)
    gs, acts = take(2)
    if not first:
        accs, = take(1)
    copies = Copies(take(1)[0])
    rows = go.shape[0]
    got = [copies.start(act, acts)]
    got += [
        copies.start(g, gs.at[pl.ds(r * rows, rows)]) for r, g in enumerate((go, gc, gy, gd))
    ]
    if not first:
        got.append(copies.start(acc_in, accs))
    for c in got:
        c.wait()
    grad = dot_tn(acts[...].reshape(gs.shape[0], acts.shape[2]), gs[...])
    sums = jnp.broadcast_to(jnp.sum(gs[...].astype(F32), 0, keepdims=True), gsum.shape)
    if first:
        outs[0][...] = grad
        gsum[...] = sums
    else:
        accs[...] += grad
        gsum[...] = gsum_in[...] + sums
        store_parts(accs, outs, me_ref[0])


def contract(me, gs, act, before=None):
    rows, feat = gs[0].shape
    ff = act.shape[2]
    first = before is None
    ins = [(me, SMEM)] + [(g, ANY) for g in gs] + [(act, ANY)]
    if first:
        outs = [(shape((ff, feat), F32), VMEM)]
    else:
        ins += [(before[0], ANY), (before[1], VMEM)]
        outs = [(shape((4, ff // 16, feat)), VMEM)] * 4
    outs.append((shape((8, feat), F32), VMEM))
    scratch = [pltpu.VMEM((4 * rows, feat), BF), pltpu.VMEM(act.shape, BF)]
    if not first:
        scratch.append(pltpu.VMEM((ff, feat), F32))
    return call(
        functools.partial(contract_kernel, first),
        "contract_grad", ins, outs, scratch, 6, 8 * rows * feat * ff,
    )


def expand_kernel(first, *refs):
    refs = list(refs)
    take = lambda k: [refs.pop(0) for _ in range(k)]
    me_ref, = take(1)
    xpieces, gpieces = take(4), take(4)
    slope, we, wc, gb = take(4)
    e1m, e1s = take(2) if first else (None, None)
    if not first:
        acc_in, vec_in = take(2)
    outs = take(1 if first else 4)
    if first:
        em, es, vec = take(3)
    else:
        eo, vec = take(2)
    xs, gs, slopes, wes, wcs, h2s, dus, ebuf = take(8)
    accs = take(1)[0] if not first else None
    copies = Copies(take(1)[0])
    rows = xs.shape[1]
    got_w = copies.start(wc, wcs)
    got_g, got_s, got_x = [], [], []
    for r in range(4):
        got_g.append(copies.start(gpieces[r], gs.at[r]))
        got_s.append(copies.start(slope.at[r], slopes.at[r]))
        got_x.append(copies.start(xpieces[r], xs.at[r]))
    got_we = copies.start(we, wes)
    got_acc = None if first else copies.start(acc_in, accs)
    got_e1 = []
    if first:
        for r in range(4):
            got_e1.append(copies.start((e1s if r % 2 else e1m).at[r // 2], ebuf.at[r]))
    got_w.wait()
    column = jnp.zeros((1, slopes.shape[2]), F32)
    for r in range(4):
        here = slice(r * rows, (r + 1) * rows)
        got_g[r].wait()
        got_s[r].wait()
        du = (dot_nt(gs[r], wcs[...]) * slopes[r].astype(F32)).astype(BF)
        dus[here] = du
        column += jnp.sum(du.astype(F32), 0, keepdims=True)
        got_x[r].wait()
        n = normalize(xs[r].astype(F32))
        gs[r] = n.astype(BF)
        h2s[here] = (n * gb[2:3] + gb[3:4]).astype(BF)
    grad = dot_tn(h2s[...], dus[...])
    if first:
        outs[0][...] = grad
    else:
        got_acc.wait()
        accs[...] += grad
        store_parts(accs, outs, me_ref[0])
    got_we.wait()
    for c in got_e1:
        c.wait()
    sent = []
    gain = jnp.zeros((1, gb.shape[1]), F32)
    bias = jnp.zeros((1, gb.shape[1]), F32)
    for r in range(4):
        e2 = dot_nt(dus[r * rows : (r + 1) * rows], wes[...])
        gain += jnp.sum(e2 * gs[r].astype(F32), 0, keepdims=True)
        bias += jnp.sum(e2, 0, keepdims=True)
        e = e2 * gb[2:3]
        if first:
            e += ebuf[r].astype(F32)
        ebuf[r] = e.astype(BF)
        out = (es if r % 2 else em).at[r // 2] if first else eo.at[r]
        sent.append(copies.start(ebuf.at[r], out))
    rowid = lax.broadcasted_iota(jnp.int32, vec.shape, 0)
    both = jnp.where(rowid == 0, gain, jnp.where(rowid == 1, bias, jnp.where(rowid == 2, column, 0.0)))
    vec[...] = both if first else vec_in[...] + both
    for c in sent:
        c.wait()


def expand(me, xs, gs, slope, we, wc, gb, partial=None, before=None):
    rows, feat = gs[0].shape
    ff = wc.shape[0]
    first = before is None
    ins = [(me, SMEM)] + [(a, ANY) for a in (*xs, *gs, slope, we, wc)] + [(gb, VMEM)]
    halves = (shape((2, rows, feat)), ANY)
    if first:
        ins += [(a, ANY) for a in partial]
        outs = [(shape((feat, ff), F32), VMEM), halves, halves]
    else:
        ins += [(before[0], ANY), (before[1], VMEM)]
        outs = [(shape((4, feat // 16, ff)), VMEM)] * 4 + [(shape((4, rows, feat)), ANY)]
    outs.append((shape((8, feat), F32), VMEM))
    stack = pltpu.VMEM((4, rows, feat), BF)
    scratch = [
        stack, stack, pltpu.VMEM((4, rows, ff), BF), pltpu.VMEM(we.shape, BF),
        pltpu.VMEM(wc.shape, BF), pltpu.VMEM((4 * rows, feat), BF),
        pltpu.VMEM((4 * rows, ff), BF), stack,
    ]
    if not first:
        scratch.append(pltpu.VMEM((feat, ff), F32))
    return call(
        functools.partial(expand_kernel, first),
        "expand_grad", ins, outs, scratch, 24, 24 * rows * feat * ff,
    )


def after(value, *others):
    return lax.optimization_barrier((value, *others))[0]


def add(*terms):
    return sum(a.astype(F32) for a in terms).astype(BF)


def swap(value, axis, size, bit):
    return lax.ppermute(value, axis, [(i, i ^ bit) for i in range(size)])


class Order:
    def __init__(self):
        self.last = None

    def __call__(self, value):
        if self.last is not None:
            value = after(value, self.last)
        return value

    def step(self, result):
        self.last = result
        return result


class Sum:
    def __init__(self, order, size, keep, send):
        self.order, self.size = order, size
        self.have = keep
        self.flying = swap(send, "dp", size, 1)

    def kept(self):
        self.have = self.order.step(add(self.order(self.have), self.flying))
        self.flying = swap(self.have[2:], "dp", self.size, 2)

    def near(self):
        self.have = self.order.step(add(self.order(self.have[:2]), self.flying))
        self.flying = swap(self.have[1], "dp", self.size, 4)

    def own(self):
        own = self.order.step(add(self.order(self.have[0]), self.flying))
        if self.size > 8:
            groups = [[low + 8 * high for high in range(self.size // 8)] for low in range(8)]
            own = lax.psum(own.astype(F32), "dp", axis_index_groups=groups).astype(BF)
        self.have = own
        self.flying = swap(own, "dp", self.size, 4)

    def pair(self):
        self.have = self.order.step(jnp.stack([self.order(self.have), self.flying]))
        self.flying = swap(self.have, "dp", self.size, 2)

    def four(self):
        self.have = self.order.step(jnp.concatenate([self.order(self.have), self.flying], 0))
        self.flying = swap(self.have, "dp", self.size, 1)

    def parts(self):
        return self.have, self.flying


class Rows:
    def __init__(self, order, mine, send):
        self.order, self.mine = order, mine
        self.got = swap(send, "tp", 4, 1)

    def away(self):
        away = self.order.step(add(self.order(self.mine[1]), self.got[1]))
        self.far = swap(away, "tp", 4, 2)

    def terms(self):
        return self.mine[0], self.got[0], self.far


def place_kernel(me_ref, four_a, other_a, four_b, other_b, out):
    i = pl.program_id(0)
    half = out.shape[0] // 2

    @pl.when(i < 4)
    def _():
        out[:half] = four_a[0].astype(F32)
        out[half:] = four_b[0].astype(F32)

    @pl.when(i >= 4)
    def _():
        out[:half] = other_a[0].astype(F32)
        out[half:] = other_b[0].astype(F32)


def place(me, a, b):
    _, half, width = a[0].shape

    def where(i, me):
        j = i % 4
        order = (j // 2) * 2 + (j % 2) * 4
        return (order + i // 4) ^ me[0], 0

    kept = pl.BlockSpec((1, half, width), lambda i, me: (jnp.minimum(i, 3), 0, 0))
    other = pl.BlockSpec((1, half, width), lambda i, me: (jnp.maximum(i - 4, 0), 0, 0))
    return pl.pallas_call(
        place_kernel,
        grid_spec=pltpu.PrefetchScalarGridSpec(
            num_scalar_prefetch=1,
            grid=(8,),
            in_specs=[kept, other, kept, other],
            out_specs=pl.BlockSpec((2 * half, width), where),
        ),
        out_shape=shape((16 * half, width), F32),
        compiler_params=pltpu.CompilerParams(vmem_limit_bytes=32 * 2**20),
        cost_estimate=pl.CostEstimate(flops=0, bytes_accessed=16 * half * width, transcendentals=0),
        name="place_parts",
    )(me, *a, *b)


def pack_kernel(own_q, me_ref, og, qs, shared, vec, keep, send):
    me = me_ref[0]
    cut = own_q // 8
    tall = LANES // 8
    for out, order in ((keep, KEEP), (send, SEND)):
        for i in range(4):
            b = order[i] ^ me
            rows = lambda ref, size: ref[pl.ds(pl.multiple_of(b * size, 8), size)]
            line = jnp.broadcast_to(vec[pl.ds(b, 1)], (8, vec.shape[1]))
            part = [rows(og, cut), rows(qs, cut), rows(shared, tall), line]
            part.append(jnp.zeros((out.shape[1] - 2 * cut - tall - 8, vec.shape[1]), F32))
            out[i] = jnp.concatenate(part, 0).astype(BF)


def unpack_kernel(own_q, me_ref, four, other, og, qg, sg, vec, qs, shared):
    me = me_ref[0]
    cut = own_q // 8
    tall = LANES // 8
    for ref, order in ((four, KEEP), (other, SEND)):
        for i in range(4):
            b = order[i] ^ me
            part = ref[i].astype(F32)
            rows = lambda size: pl.ds(pl.multiple_of(b * size, 8), size)
            og[rows(cut)] = part[:cut]
            qs[rows(cut)] = part[cut : 2 * cut]
            shared[rows(tall)] = part[2 * cut : 2 * cut + tall]
            vec[pl.ds(b, 1)] = part[2 * cut + tall : 2 * cut + tall + 1]
    qg[...] = qs[...].T
    sg[...] = shared[...].T


def doc_layout(ends, scales, length):
    row_ids = jnp.arange(length, dtype=jnp.int32)
    doc_ids = jnp.sum((row_ids[:, None] >= ends[None, :]).astype(jnp.int32), 1)
    starts = jnp.concatenate([jnp.zeros((1,), jnp.int32), ends[:-1]])
    onehot = doc_ids[:, None] == jnp.arange(ends.shape[0], dtype=jnp.int32)[None, :]
    begins = jnp.sum(jnp.where(onehot, starts[None, :], 0), 1)
    steps_of = jnp.sum(jnp.where(onehot, scales[None, :], 0), 1)
    return (row_ids - begins) * steps_of


def angle_tables(placed, rows):
    freqs = 10000.0 ** (-jnp.arange(ROT // 2, dtype=F32) * 2.0 / ROT)
    blocks = placed.astype(F32).reshape(placed.shape[0], 4, 1, rows)
    angles = blocks * freqs[:, None]
    return jnp.cos(angles), jnp.sin(angles)


def on_device(
    size,
    tokens,
    cotangent,
    doc_ends,
    pos_scale,
    first_gain,
    first_bias,
    second_gain,
    second_bias,
    w_query,
    query_bias,
    w_shared,
    shared_bias,
    w_output,
    w_expand,
    expand_bias,
    w_contract,
    output_bias,
):
    micro, rows, feat = tokens.shape
    heads = w_query.shape[1] // 64
    own_q = w_query.shape[1]
    length = rows * 4
    rank = lax.axis_index("tp").astype(jnp.int32)[None]
    me = (lax.axis_index("dp").astype(jnp.int32) & 7)[None]

    def gather(values):
        far = swap(values, "tp", 4, 2)
        near = swap(values, "tp", 4, 1)
        return values, near, far, swap(far, "tp", 4, 1)

    x0, g0 = gather(tokens[0]), gather(cotangent[0])
    x1, g1 = gather(tokens[1]), gather(cotangent[1])

    wt = jnp.concatenate([w_query.T, jnp.zeros((QW - own_q, feat), BF), w_shared.T], 0)
    bqkv = jnp.concatenate([query_bias, jnp.zeros((QW - own_q,), F32), shared_bias])[None]
    wo = jnp.concatenate([w_output, jnp.zeros((QW - own_q, feat), BF)], 0)
    gb = jnp.stack([first_gain, first_bias, second_gain, second_bias])
    be = expand_bias[None]
    ends, scales = doc_ends[:, 0], pos_scale[:, 0]
    placed = jnp.stack([doc_layout(ends[m], scales[m], length) for m in range(micro)])
    cs, sn = angle_tables(placed, rows)

    order = Order()
    act0, slope0 = hidden(x0, gb, w_expand, be)
    out0m, out0s, e0m, e0s, og, qs, vec = attention(
        rank, ends[0], x0, g0, act0, wt, bqkv, wo, w_contract, gb, cs[0], sn[0], heads
    )
    order.step(vec)
    out0 = Rows(order, out0m, out0s)
    act1, slope1 = hidden(x1, order(gb), w_expand, be)
    order.step(act1)
    out0.away()
    cacc, gsum = contract(order(me), g0, act0)
    order.step(gsum)
    *c_parts, gsum = contract(order(me), g1, act1, (cacc, gsum))
    order.step(gsum)
    ca = Sum(order, size, c_parts[0], c_parts[1])
    cb = Sum(order, size, c_parts[2], c_parts[3])
    eacc, e0m, e0s, vec2 = expand(
        order(me), x0, g0, slope0, w_expand, w_contract, gb, partial=(e0m, e0s)
    )
    order.step(vec2)
    in0 = Rows(order, e0m, e0s)
    ca.kept()
    *e_parts, e2, vec2 = expand(
        order(me), x1, g1, slope1, w_expand, w_contract, gb, before=(eacc, vec2)
    )
    order.step(vec2)
    ea = Sum(order, size, e_parts[0], e_parts[1])
    eb = Sum(order, size, e_parts[2], e_parts[3])
    cb.kept()
    ca.near()
    in0.away()
    out1m, out1s, e1m, e1s, og, qs, vec = attention(
        order(rank), ends[1], x1, g1, act1, wt, bqkv, wo, w_contract, gb, cs[1], sn[1], heads,
        before=(e2, og, qs, vec),
    )
    order.step(vec)
    out1 = Rows(order, out1m, out1s)
    in1 = Rows(order, e1m, e1s)

    sbias = jnp.pad(vec[2:3, QW : QW + LANES], ((0, 0), (0, feat - LANES)))
    over_tp = jnp.concatenate(
        [qs[QW:], vec[:2], vec2[:2], sbias, jnp.zeros((11, feat), F32)], 0
    ).astype(BF)
    order.step(over_tp)
    over_core = swap(over_tp, "tp", 4, 1)
    cb.near()
    ca.own()
    ea.kept()
    over_tp = order.step(add(order(over_tp), over_core))
    over_chip = swap(over_tp, "tp", 4, 2)
    out1.away()
    in1.away()
    cb.own()
    ca.pair()
    eb.kept()
    ea.near()
    over_tp = order.step(add(order(over_tp), over_chip)).astype(F32)
    qbias = jnp.pad(vec[2:3, :own_q], ((0, 0), (0, feat - own_q)))
    lines = jnp.concatenate([over_tp[LANES : LANES + 5], gsum[:1], vec2[2:3], qbias], 0)
    part = (shape((4, 80, feat)), VMEM)
    keep, send = pl.pallas_call(
        functools.partial(pack_kernel, own_q),
        in_specs=[SMEM] + [VMEM] * 4,
        out_specs=[VMEM, VMEM],
        out_shape=[part[0], part[0]],
        compiler_params=pltpu.CompilerParams(vmem_limit_bytes=32 * 2**20),
        cost_estimate=pl.CostEstimate(flops=0, bytes_accessed=10**6, transcendentals=0),
        name="pack",
    )(me, og, qs, over_tp[:LANES], lines)
    order.step(send)
    rest = Sum(order, size, keep, send)
    cb.pair()
    ca.four()
    eb.near()
    ea.own()
    cb.four()
    eb.own()
    ea.pair()
    rest.kept()
    eb.pair()
    ea.four()
    rest.near()
    eb.four()
    rest.own()
    contract_grad = place(me, ca.parts(), cb.parts())
    rest.pair()
    rest.four()
    out0, in0, out1, in1 = [a.terms() for a in (out0, in0, out1, in1)]
    expand_grad = place(me, ea.parts(), eb.parts())
    four, other = rest.parts()
    output_grad, query_grad, shared_grad, lines = pl.pallas_call(
        functools.partial(unpack_kernel, own_q),
        in_specs=[SMEM, VMEM, VMEM],
        out_specs=[VMEM] * 4,
        out_shape=[
            shape((own_q, feat), F32), shape((feat, own_q), F32),
            shape((feat, LANES), F32), shape((8, feat), F32),
        ],
        scratch_shapes=[pltpu.VMEM((own_q, feat), F32), pltpu.VMEM((LANES, feat), F32)],
        compiler_params=pltpu.CompilerParams(vmem_limit_bytes=32 * 2**20),
        cost_estimate=pl.CostEstimate(flops=0, bytes_accessed=10**6, transcendentals=0),
        name="unpack",
    )(me, four, other)

    def joined(parts):
        return jnp.stack([sum(a.astype(F32) for a in p) for p in parts])

    x = tokens.astype(F32)
    layer_out = (x + joined([out0, out1]) + output_bias).astype(BF)
    norm_of = normalize_rows(x)
    norm, scale = norm_of
    e = joined([in0, in1])
    slope_mean = jnp.mean(e * norm, -1, keepdims=True)
    input_grad = cotangent.astype(F32) + scale * (
        e - jnp.mean(e, -1, keepdims=True) - norm * slope_mean
    )
    return (
        layer_out,
        input_grad,
        query_grad,
        lines[7, :own_q],
        shared_grad,
        lines[4, :LANES],
        output_grad,
        expand_grad,
        lines[6, : expand_bias.shape[0]],
        contract_grad,
        lines[5],
        lines[0],
        lines[1],
        lines[2],
        lines[3],
    )


def normalize_rows(x):
    centre = x - jnp.mean(x, -1, keepdims=True)
    scale = lax.rsqrt(jnp.mean(centre * centre, -1, keepdims=True) + 1e-05)
    return centre * scale, scale


def solution(mesh):
    rows = P(None, ("dp", "tp"), None)
    in_specs = (
        rows, rows, P(None, "dp", None), P(None, "dp", None),
        P(), P(), P(), P(),
        P(None, "tp"), P("tp"), P(), P(), P("tp", None),
        P(None, "tp"), P("tp"), P("tp", None), P(),
    )
    out_specs = (
        rows, rows,
        P(None, "tp"), P("tp"), P(), P(), P("tp", None),
        P(None, "tp"), P("tp"), P("tp", None),
        P(), P(), P(), P(), P(),
    )
    return jax.shard_map(
        functools.partial(on_device, mesh.shape["dp"]),
        mesh=mesh,
        in_specs=in_specs,
        out_specs=out_specs,
        check_vma=False,
    )
```

```python
import functools

import jax
import jax.numpy as jnp
from jax import lax
from jax.experimental import pallas as pl
from jax.experimental.pallas import tpu as pltpu
from jax.sharding import PartitionSpec as P

ROT = 16
LANES = 128
QW = 256
PART = 80
BF = jnp.bfloat16
F32 = jnp.float32
KEEP = (0, 4, 2, 6)
SEND = (1, 5, 3, 7)
NT = (((1,), (1,)), ((), ()))
TN = (((0,), (0,)), ((), ()))
ANY = pl.BlockSpec(memory_space=pl.ANY)
VMEM = pl.BlockSpec(memory_space=pltpu.VMEM)
SMEM = pl.BlockSpec(memory_space=pltpu.SMEM)


def dot(a, b):
    return jnp.dot(a, b, preferred_element_type=F32)


def dot_nt(a, b):
    return lax.dot_general(a, b, NT, preferred_element_type=F32)


def dot_tn(a, b):
    return lax.dot_general(a, b, TN, preferred_element_type=F32)


def shape(dims, dtype=BF):
    return jax.ShapeDtypeStruct(dims, dtype)


def call(kernel, name, ins, outs, scratch, copies, flops=10**10):
    specs = [s for _, s in ins]
    arrays = [a for a, _ in ins]
    return pl.pallas_call(
        kernel,
        in_specs=specs,
        out_specs=[s for _, s in outs],
        out_shape=[o for o, _ in outs],
        scratch_shapes=list(scratch) + [pltpu.SemaphoreType.DMA((copies,))],
        compiler_params=pltpu.CompilerParams(vmem_limit_bytes=64 * 2**20 - 65536),
        cost_estimate=pl.CostEstimate(flops=flops, bytes_accessed=0, transcendentals=0),
        name=name,
    )(*arrays)


class Copies:
    def __init__(self, sems):
        self.sems = sems
        self.count = 0

    def start(self, src, dst):
        copy = pltpu.make_async_copy(src, dst, self.sems.at[self.count])
        self.count += 1
        copy.start()
        return copy


def normalize(x):
    centre = x - jnp.mean(x, -1, keepdims=True)
    spread = jnp.mean(centre * centre, -1, keepdims=True)
    return centre * lax.rsqrt(spread + 1e-05)


def line(ref):
    return ref[...].reshape(1, -1)


def swap_halves(w):
    lane = lax.broadcasted_iota(jnp.int32, w.shape, 1)
    up = pltpu.roll(w, w.shape[1] - ROT // 2, 1)
    down = pltpu.roll(w, ROT // 2, 1)
    return jnp.where((lane % 64) < ROT // 2, up, down)


def spread_table(compact, filler, signs):
    fill = jnp.full((64 - ROT, compact.shape[1]), filler, F32)
    head = [signs * compact, compact, fill]
    return jnp.concatenate(head + head, 0).T


def hidden_kernel(
    pa, pb, gain1, bias1, gain2, bias2, we, be, acto, slopeo, h1o, h2o, no, xs, wev, acts, slopes, h1s, h2s, ns, sems
):
    copies = Copies(sems)
    got = [copies.start(pa, xs.at[0])]
    gotw = copies.start(we, wev)
    got.append(copies.start(pb, xs.at[1]))
    out = []
    for j in range(2):
        got[j].wait()
        for m in range(2):
            n = normalize(xs[j, m].astype(F32))
            ns[m, j] = n.astype(BF)
            h1s[m, j] = (n * line(gain1) + line(bias1)).astype(BF)
            h2 = (n * line(gain2) + line(bias2)).astype(BF)
            h2s[m, j] = h2
            for a, b in ((ns, no), (h1s, h1o), (h2s, h2o)):
                out.append(copies.start(a.at[m, j], b.at[m, j]))
            if j == 0 and m == 0:
                gotw.wait()
            u = dot(h2, wev[...]) + line(be)
            phi = 0.5 * (1.0 + lax.erf(u * 0.7071067811865476))
            acts[m, j] = (u * phi).astype(BF)
            slopes[m, j] = (phi + u * jnp.exp(-0.5 * u * u) * 0.3989422804014327).astype(BF)
            for a, b in ((acts, acto), (slopes, slopeo)):
                out.append(copies.start(a.at[m, j], b.at[m, j]))
    for c in out:
        c.wait()


def hidden(pieces, norms, we, be):
    _, rows, feat = pieces[0].shape
    ff = we.shape[1]
    wide, narrow = (2, 2, rows, ff), (2, 2, rows, feat)
    return call(
        hidden_kernel,
        "hidden",
        [(x, ANY) for x in pieces] + [(a, VMEM) for a in norms] + [(we, ANY), (be, VMEM)],
        [(shape(wide), ANY)] * 2 + [(shape(narrow), ANY)] * 3,
        [pltpu.VMEM(narrow, BF), pltpu.VMEM(we.shape, BF)]
        + [pltpu.VMEM(wide, BF)] * 2
        + [pltpu.VMEM(narrow, BF)] * 3,
        23,
        0,
    )


def doubled(kv):
    kv = kv.astype(F32)
    swapped = pltpu.roll(kv, 64, 1)
    low = lax.broadcasted_iota(jnp.int32, kv.shape, 1) < 64
    return jnp.where(low, kv, swapped).astype(BF), jnp.where(low, swapped, kv).astype(BF)


def stack_heads(block, heads):
    low = lax.broadcasted_iota(jnp.int32, (block.shape[0], LANES), 1) < 64
    zero = jnp.zeros((block.shape[0], LANES), block.dtype)
    parts = []
    for h in range(heads):
        part = block[:, LANES * (h // 2) : LANES * (h // 2 + 1)]
        parts.append(jnp.where(low, part, zero) if h % 2 == 0 else jnp.where(low, zero, part))
    return jnp.concatenate(parts, 0)


def join_heads(stacked, heads, rows):
    low = lax.broadcasted_iota(jnp.int32, (rows, LANES), 1) < 64
    part = lambda h: stacked[h * rows : (h + 1) * rows]
    zero = jnp.zeros((rows, LANES), stacked.dtype)
    cols = []
    for h in range(0, heads, 2):
        cols.append(jnp.where(low, part(h), part(h + 1) if h + 1 < heads else zero))
    return jnp.concatenate(cols, 1)


def send_rows(copies, rows, mine, send, which):
    places = (mine[0].at[which], send.at[0, which], mine[1].at[which], send.at[1, which])
    return [copies.start(rows.at[r], place) for r, place in enumerate(places)]


def halves_to(copies, halves, micro_id, into, t):
    return [
        copies.start(halves[r // 2].at[micro_id, r % 2], into.at[r ^ t]) for r in range(4)
    ]


def join_weights(wqs, wss, wts):
    own_q = wqs.shape[1]
    wts[:, :own_q] = wqs[...]
    wts[:, own_q:QW] = jnp.zeros((wts.shape[0], QW - own_q), BF)
    wts[:, QW:] = wss[...]


def project(micro_id, h1s, wts, qbias, sbias, bqkv, cs, sn, saved):
    qrs, kk, vv = saved[:3]
    rows = h1s.shape[1]
    own_q = qbias.shape[0]
    bqkv[:, :own_q] = line(qbias)
    bqkv[:, own_q:QW] = jnp.zeros((1, QW - own_q), F32)
    bqkv[:, QW:] = line(sbias)
    for a in range(4):
        here = slice(a * rows, (a + 1) * rows)
        qkv = dot(h1s[a], wts[...]) + bqkv[...]
        c = spread_table(cs[micro_id, a], 1.0, 1.0)
        s = spread_table(sn[micro_id, a], 0.0, -1.0)
        low = lax.broadcasted_iota(jnp.int32, c.shape, 1) < 64
        cos = jnp.concatenate([c, c, jnp.where(low, c, 1.0)], 1)
        sin = jnp.concatenate([s, s, jnp.where(low, s, 0.0)], 1)
        qkv = qkv * cos + swap_halves(qkv) * sin
        qrs[a] = (qkv[:, :QW] * 0.125).astype(BF)
        kk[here], vv[here] = doubled(qkv[:, QW:].astype(BF))


def attend_rows(micro_id, heads, ends, saved):
    qrs, kk, vv, cx, *probs_of = saved
    rows = qrs.shape[1]
    spans = [(a + 1) * rows for a in range(4)]
    scores = dot_nt(stack_heads(qrs[3], heads), kk[: spans[3]])
    for a in (3, 2, 1, 0):
        here = scores
        if a > 0:
            scores = dot_nt(stack_heads(qrs[a - 1], heads), kk[: spans[a - 1]])
        row = lax.broadcasted_iota(jnp.int32, (rows, 1), 0) + a * rows
        begin = jnp.zeros((rows, 1), jnp.int32)
        for d in range(ends.shape[2] - 1):
            begin = jnp.where(row >= ends[micro_id, 0, d], ends[micro_id, 0, d], begin)
        col = lax.broadcasted_iota(jnp.int32, (rows, spans[a]), 1)
        allowed = (col >= begin) & (col <= row)
        for h in range(heads):
            mine = slice(h * rows, (h + 1) * rows)
            s = jnp.where(allowed, here[mine], -1e30)
            e = jnp.exp(s - jnp.max(s, -1, keepdims=True))
            probs_of[a][mine] = (e * (1.0 / jnp.sum(e, -1, keepdims=True))).astype(BF)
        done = a + 1
        if done < 4:
            cx[done] = join_heads(dot(probs_of[done][...], vv[: spans[done]]), heads, rows).astype(BF)
    cx[0] = join_heads(dot(probs_of[0][...], vv[: spans[0]]), heads, rows).astype(BF)


def attend_kernel(micro_id, heads, *refs):
    refs = list(refs)
    take = lambda k: [refs.pop(0) for _ in range(k)]
    t_ref, ends = take(2)
    h1 = take(2)
    wq, ws, qbias, sbias, cs, sn = take(6)
    outs = take(8)
    h1s, wqs, wss, wts, bqkv = take(5)
    saved = take(8)
    copies = Copies(take(1)[0])
    got = [copies.start(wq, wqs), copies.start(ws, wss)]
    got += halves_to(copies, h1, micro_id, h1s, t_ref[0])
    for c in got:
        c.wait()
    join_weights(wqs, wss, wts)
    project(micro_id, h1s, wts, qbias, sbias, bqkv, cs, sn, saved)
    sent = [copies.start(saved[i], outs[i]) for i in range(3)]
    attend_rows(micro_id, heads, ends, saved)
    sent += [copies.start(saved[i], outs[i]) for i in range(3, 8)]
    for c in sent:
        c.wait()


def weights_scratch(wq, ws):
    width = QW + LANES
    scratch = [pltpu.VMEM(wq.shape, BF), pltpu.VMEM(ws.shape, BF)]
    return scratch + [pltpu.VMEM((wq.shape[0], width), BF), pltpu.VMEM((1, width), F32)]


def saved_shapes(rows, heads):
    length = 4 * rows
    saved = [(4, rows, QW), (length, LANES), (length, LANES), (4, rows, QW)]
    return saved + [(heads * rows, (a + 1) * rows) for a in range(4)]


def attend(micro_id, rank, ends, h1, wq, ws, qbias, sbias, cs, sn, heads, flops):
    _, _, rows, feat = h1[0].shape
    ins = [(rank, SMEM), (ends, SMEM)] + [(a, ANY) for a in (*h1, wq, ws)]
    ins += [(a, VMEM) for a in (qbias, sbias, cs, sn)]
    saved = saved_shapes(rows, heads)
    scratch = [pltpu.VMEM((4, rows, feat), BF)] + weights_scratch(wq, ws)
    return call(
        functools.partial(attend_kernel, micro_id, heads), "attend", ins,
        [(shape(a), ANY) for a in saved], scratch + [pltpu.VMEM(a, BF) for a in saved], 14, flops,
    )


def attend_back_kernel(micro_id, heads, first, whole, *refs):
    refs = list(refs)
    take = lambda k: [refs.pop(0) for _ in range(k)]
    t_ref, me_ref = take(2)
    if whole:
        ends, qbias, sbias = take(3)
    else:
        saved = take(8)
    gpieces = take(4)
    h1, act, du, n = take(2), take(2), take(2), take(2)
    wq, ws, wo, wc, we, gain1, gain2, cs, sn = take(9)
    if not first:
        og_in, qs_in, vec_in, hid_in = take(4)
    rows_kept = take(2)
    rows_sent, = take(1)
    results = take(3 if first else 2)
    gs, h1s, acts, dus, ns, wqs, wss, wts, bqkv, wos, wcs, wes = take(12)
    qrs, kk, vv, cx, *probs_of = kept = take(8)
    dctx, = take(1)
    dss = take(2)
    dk, dv, dqkv, outb, eb, ogs, qss = take(7)
    if not first:
        lines, keeps, sends = take(3)
    copies = Copies(take(1)[0])
    rows = gs.shape[1]
    t = t_ref[0]
    spans = [(a + 1) * rows for a in range(4)]
    got_h = [copies.start(wq, wqs), copies.start(ws, wss)]
    got_h += halves_to(copies, h1, micro_id, h1s, t)
    own_q = wo.shape[0]
    got_g = [copies.start(wo, wos.at[pl.ds(0, own_q)])]
    wos[own_q:] = jnp.zeros((QW - own_q, wo.shape[1]), BF)
    got_g += [copies.start(g.at[micro_id], gs.at[r ^ t]) for r, g in enumerate(gpieces)]
    order = (2, 7, 0, 1, 6, 5, 4, 3)
    got_saved = [] if whole else [copies.start(saved[i], kept[i]) for i in order]
    got_out = halves_to(copies, act, micro_id, acts, 0) + [copies.start(wc, wcs)]
    got_e = halves_to(copies, du, micro_id, dus, 0) + [copies.start(we, wes)]
    got_e += halves_to(copies, n, micro_id, ns, 0)
    if not first:
        got_e += [copies.start(og_in, ogs), copies.start(qs_in, qss)]
    if whole:
        for c in got_h:
            c.wait()
        join_weights(wqs, wss, wts)
        project(micro_id, h1s, wts, qbias, sbias, bqkv, cs, sn, kept)
        attend_rows(micro_id, heads, ends, kept)
    for c in got_g:
        c.wait()
    dctx[...] = dot_nt(gs[...].reshape(4 * rows, gs.shape[2]), wos[...]).astype(BF)
    for c in got_saved:
        c.wait()
    dk[...] = jnp.zeros_like(dk)
    dv[...] = jnp.zeros_like(dv)
    stacked = lambda a: stack_heads(dctx[a * rows : (a + 1) * rows], heads)

    def finish(a):
        dscores = dss[a % 2][:, : spans[a]]
        dk[: spans[a]] += dot_tn(dscores, stack_heads(qrs[a], heads))
        dv[: spans[a]] += dot_tn(probs_of[a][...], stacked(a))
        dq = join_heads(dot(dscores, kk[: spans[a]]), heads, rows) * 0.125
        c = spread_table(cs[micro_id, a], 1.0, 1.0)
        s = spread_table(sn[micro_id, a], 0.0, -1.0)
        cos = jnp.concatenate([c, c], 1)
        sin = jnp.concatenate([s, s], 1)
        dqkv[a, :, :QW] = (dq * cos - swap_halves(dq) * sin).astype(BF)

    dprobs = dot_nt(stacked(3), vv[: spans[3]])
    for a in (3, 2, 1, 0):
        here = dprobs
        if a > 0:
            dprobs = dot_nt(stacked(a - 1), vv[: spans[a - 1]])
        for h in range(heads):
            mine = slice(h * rows, (h + 1) * rows)
            p = probs_of[a][mine].astype(F32)
            weighted = p * here[mine]
            delta = jnp.sum(weighted, -1, keepdims=True)
            dss[a % 2][mine, : spans[a]] = (weighted - p * delta).astype(BF)
        if a < 3:
            finish(a + 1)
    finish(0)
    for a in range(4):
        here = slice(a * rows, (a + 1) * rows)
        c = spread_table(cs[micro_id, a], 1.0, 1.0)
        s = spread_table(sn[micro_id, a], 0.0, -1.0)
        dkf = dk[here] + pltpu.roll(dk[here], 64, 1)
        dvf = dv[here] + pltpu.roll(dv[here], 64, 1)
        dkf = dkf * c - swap_halves(dkf) * s
        low = lax.broadcasted_iota(jnp.int32, dkf.shape, 1) < 64
        dqkv[a, :, QW:] = jnp.where(low, dkf, dvf).astype(BF)
    for c in got_out:
        c.wait()
    for r in range(4):
        outb[r] = (dot(cx[r ^ t], wos[...]) + dot(acts[r], wcs[...])).astype(BF)
    sent = send_rows(copies, outb, rows_kept, rows_sent, 0)

    for c in got_e + ([] if whole else got_h):
        c.wait()
    if not whole:
        join_weights(wqs, wss, wts)
    width = QW + LANES
    vec_width = gs.shape[2]
    flat = dqkv[...].reshape(4 * rows, width)
    ograd = dot_tn(cx[...].reshape(4 * rows, QW), gs[...].reshape(4 * rows, gs.shape[2]))
    qgrad = dot_tn(flat, h1s[...].reshape(4 * rows, h1s.shape[2]))
    ogs[...] = ograd if first else ogs[...] + ograd
    qss[...] = qgrad if first else qss[...] + qgrad
    if first:
        sent += [copies.start(ogs, results[0]), copies.start(qss, results[1])]
    sums = [jnp.zeros((1, vec_width), F32) for _ in range(4)]
    for r in range(4):
        e1 = dot_nt(dqkv[r ^ t], wts[...])
        e2 = dot_nt(dus[r], wes[...])
        eb[r] = (e1 * line(gain1) + e2 * line(gain2)).astype(BF)
        norm = ns[r].astype(F32)
        for i, term in enumerate((e1 * norm, e1, e2 * norm, e2)):
            sums[i] += jnp.sum(term, 0, keepdims=True)
    sent += send_rows(copies, eb, rows_kept, rows_sent, 1)
    column = jnp.sum(flat.astype(F32), 0, keepdims=True)
    sums.append(jnp.concatenate([column, jnp.zeros((1, vec_width - width), F32)], 1))
    if first:
        results[2][...] = jnp.concatenate(sums + [jnp.zeros((3, vec_width), F32)], 0)
    else:
        sums = [a + vec_in[i : i + 1] for i, a in enumerate(sums)]
        zero = jnp.zeros((5, vec_width), F32)
        lines[...] = jnp.concatenate(
            [hid_in[0:1], hid_in[1:2], sums[4], zero] + sums + [zero[:3]], 0
        )
        pack_parts(ogs, qss, lines, keeps, sends, me_ref[0], heads * 8)
        sent += [copies.start(keeps, results[0]), copies.start(sends, results[1])]
    for c in sent:
        c.wait()


def pack_parts(og, qs, lines, keep, send, me, cut):
    tall = LANES // 8
    for out, order in ((keep, KEEP), (send, SEND)):
        for i in range(4):
            b = order[i] ^ me
            rows = lambda ref, size, base: ref[pl.ds(pl.multiple_of(b * size + base, 8), size)]
            line = lambda i: jnp.broadcast_to(lines[pl.ds(b + i, 1)], (8, lines.shape[1]))
            part = [rows(og, cut, 0), rows(qs, cut, 0), line(0), rows(qs, tall, QW), line(8)]
            out[i] = jnp.concatenate(part, 0).astype(BF)


def attend_back(
    micro_id, rank, me, saved, gs, h1, act, du, n, wq, ws, wo, wc, we, gain1, gain2, cs, sn, heads,
    whole=False, before=None,
):
    _, rows, feat = gs[0].shape
    ff = wc.shape[0]
    width = QW + LANES
    length = 4 * rows
    first = before is None
    ins = [(rank, SMEM), (me, SMEM)]
    ins += [(saved[0], SMEM)] + [(a, VMEM) for a in saved[1:]] if whole else [(a, ANY) for a in saved]
    ins += [(a, ANY) for a in (*gs, *h1, *act, *du, *n, wq, ws, wo, wc, we)]
    ins += [(a, VMEM) for a in (gain1, gain2, cs, sn)]
    if not first:
        ins += [(a, ANY) for a in before[:2]] + [(a, VMEM) for a in before[2:]]
    outs = [(shape((2, rows, feat)), ANY)] * 2 + [(shape((2, 2, rows, feat)), ANY)]
    grads = [shape((QW, feat), F32), shape((width, feat), F32)]
    part = shape((4, PART, feat))
    if first:
        outs += [(g, ANY) for g in grads] + [(shape((8, feat), F32), VMEM)]
    else:
        outs += [(part, ANY)] * 2
    stack, wide = pltpu.VMEM((4, rows, feat), BF), pltpu.VMEM((4, rows, ff), BF)
    scratch = [stack, stack, wide, wide, stack]
    scratch += weights_scratch(wq, ws)
    scratch += [pltpu.VMEM(a, BF) for a in ((QW, feat), wc.shape, we.shape)]
    scratch += [pltpu.VMEM(a, BF) for a in saved_shapes(rows, heads)]
    scratch += [
        pltpu.VMEM((length, QW), BF),
        pltpu.VMEM((heads * rows, length), BF), pltpu.VMEM((heads * rows, length), BF),
        pltpu.VMEM((length, LANES), F32), pltpu.VMEM((length, LANES), F32),
        pltpu.VMEM((4, rows, width), BF), stack, stack,
    ]
    scratch += [pltpu.VMEM(g.shape, F32) for g in grads]
    if not first:
        scratch += [pltpu.VMEM((16, feat), F32)] + [pltpu.VMEM(part.shape, BF)] * 2
    return call(
        functools.partial(attend_back_kernel, micro_id, heads, first, whole), "attend_grad", ins, outs,
        scratch, 46,
    )


def store_parts(acc, keep, send, me):
    part = acc.shape[0] // 8
    for out, order in ((keep, KEEP), (send, SEND)):
        for i in range(4):
            out[i] = acc[pl.ds(pl.multiple_of((order[i] ^ me) * part, 16), part)].astype(BF)


def pieces_to(copies, pieces, into):
    return [copies.start(p.at[m], into.at[m, j]) for j, p in enumerate(pieces) for m in range(2)]


def flat(ref):
    return ref[...].reshape(-1, ref.shape[-1])


def hidden_back_kernel(first, *refs):
    refs = list(refs)
    take = lambda k: [refs.pop(0) for _ in range(k)]
    me_ref, = take(1)
    pieces = take(2)
    act, slope, h2, wc = take(4)
    if not first:
        before = take(2)
        sums_in, = take(1)
    duo, = take(1)
    outs = take(2 if first else 4)
    sums, = take(1)
    gs, acts, slopes, wcs, h2s, dus, *accs = take(8)
    parts = None if first else take(4)
    copies = Copies(take(1)[0])
    got = pieces_to(copies, pieces, gs) + [copies.start(act, acts)]
    got_back = [copies.start(wc, wcs), copies.start(slope, slopes)]
    got_late = [copies.start(h2, h2s)]
    if not first:
        got_sums = [copies.start(a, b) for a, b in zip(before, accs)]

    def total(i, left, right):
        if first:
            accs[i][...] = dot_tn(flat(left), flat(right))
            return [copies.start(accs[i], outs[i])]
        got_sums[i].wait()
        accs[i][...] += dot_tn(flat(left), flat(right))
        store_parts(accs[i], parts[2 * i], parts[2 * i + 1], me_ref[0])
        return [copies.start(parts[2 * i + k], outs[2 * i + k]) for k in (0, 1)]

    for c in got:
        c.wait()
    sent = total(0, acts, gs)
    for c in got_back:
        c.wait()
    gsum = jnp.zeros((1, gs.shape[3]), F32)
    column = jnp.zeros((1, slopes.shape[3]), F32)
    for m in range(2):
        for j in range(2):
            g = gs[m, j]
            du = (dot_nt(g, wcs[...]) * slopes[m, j].astype(F32)).astype(BF)
            dus[m, j] = du
            gsum += jnp.sum(g.astype(F32), 0, keepdims=True)
            column += jnp.sum(du.astype(F32), 0, keepdims=True)
    sent.append(copies.start(dus, duo))
    for c in got_late:
        c.wait()
    sent += total(1, h2s, dus)
    rowid = lax.broadcasted_iota(jnp.int32, sums.shape, 0)
    both = jnp.where(rowid == 0, gsum, jnp.where(rowid == 1, column, 0.0))
    sums[...] = both if first else sums_in[...] + both
    for c in sent:
        c.wait()


def hidden_back(me, pieces, act, slope, h2, wc, before=None):
    _, _, rows, feat = h2.shape
    ff = wc.shape[0]
    first = before is None
    ins = [(me, SMEM)] + [(a, ANY) for a in (*pieces, act, slope, h2, wc)]
    outs = [(shape(slope.shape), ANY)]
    if first:
        outs += [(shape((ff, feat), F32), ANY), (shape((feat, ff), F32), ANY)]
    else:
        ins += [(before[0], ANY), (before[1], ANY), (before[2], VMEM)]
        outs += [(shape((4, ff // 8, feat)), ANY)] * 2 + [(shape((4, feat // 8, ff)), ANY)] * 2
    outs.append((shape((8, feat), F32), VMEM))
    scratch = [
        pltpu.VMEM(h2.shape, BF), pltpu.VMEM(act.shape, BF), pltpu.VMEM(slope.shape, BF),
        pltpu.VMEM(wc.shape, BF), pltpu.VMEM(h2.shape, BF), pltpu.VMEM(slope.shape, BF),
        pltpu.VMEM((ff, feat), F32), pltpu.VMEM((feat, ff), F32),
    ]
    if not first:
        scratch += [pltpu.VMEM((4, ff // 8, feat), BF)] * 2 + [pltpu.VMEM((4, feat // 8, ff), BF)] * 2
    return call(
        functools.partial(hidden_back_kernel, first), "hidden_grad", ins, outs, scratch, 15,
        0 if first else 10**10,
    )


def after(value, *others):
    return lax.optimization_barrier((value, others))[0]


def add(*terms):
    return sum(a.astype(F32) for a in terms).astype(BF)


def swap(value, axis, size, bit):
    return lax.ppermute(value, axis, [(i, i ^ bit) for i in range(size)])


class Order:
    def __init__(self):
        self.last = None

    def __call__(self, value):
        if self.last is not None:
            value = after(value, self.last)
        return value

    def step(self, result):
        self.last = result
        return result


class Sum:
    def __init__(self, order, size, keep, send):
        self.order, self.size = order, size
        self.have = keep
        self.flying = swap(order(send), "dp", size, 1)

    def kept(self):
        self.have, send = self.order.step(self.halves(self.have[:2], self.have[2:], 2))
        self.flying = swap(send, "dp", self.size, 2)

    def near(self):
        self.have, send = self.order.step(self.halves(self.have[0], self.have[1], 1))
        self.flying = swap(send, "dp", self.size, 4)

    def halves(self, stay, leave, count):
        stay, leave = self.order((stay, leave))
        if count == 1:
            got = self.flying[0], self.flying[1]
        else:
            got = self.flying[:count], self.flying[count:]
        return add(stay, got[0]), add(leave, got[1])

    def own(self, over_tp=0):
        own = self.order.step(add(self.order(self.have), self.flying))
        if over_tp:
            tail = own[over_tp:]
            whole = add(tail, *[swap(tail, "tp", 4, bit) for bit in (1, 2, 3)])
            own = self.order.step(jnp.concatenate([self.order(own[:over_tp]), whole], 0))
        if self.size > 8:
            groups = [[low + 8 * high for high in range(self.size // 8)] for low in range(8)]
            own = lax.psum(own.astype(F32), "dp", axis_index_groups=groups).astype(BF)
        self.have = own
        self.flying = swap(own, "dp", self.size, 4)

    def pair(self):
        self.have = self.order.step(jnp.stack([self.order(self.have), self.flying]))
        self.flying = swap(self.have, "dp", self.size, 2)

    def four(self):
        self.have = self.order.step(jnp.concatenate([self.order(self.have), self.flying], 0))
        self.flying = swap(self.have, "dp", self.size, 1)

    def parts(self):
        return self.have, self.flying


class Rows:
    def __init__(self, order, mine, send):
        self.order, self.mine = order, mine
        self.got = swap(order(send), "tp", 4, 1)

    def away(self):
        away = self.order.step(add(self.order(self.mine[1]), self.got[1]))
        self.far = swap(away, "tp", 4, 2)

    def land(self):
        terms = self.order(self.mine[0]), self.got[0], self.far
        self.total = self.order.step(sum(a.astype(F32) for a in terms))


def place_kernel(me_ref, four, other, out):
    i = pl.program_id(0)

    @pl.when(i < 4)
    def _():
        out[...] = four[0].astype(F32)

    @pl.when(i >= 4)
    def _():
        out[...] = other[0].astype(F32)


def place(me, four, other):
    _, part, width = four.shape

    def where(i, me):
        j = i % 4
        order = (j // 2) * 2 + (j % 2) * 4
        return (order + i // 4) ^ me[0], 0

    return pl.pallas_call(
        place_kernel,
        grid_spec=pltpu.PrefetchScalarGridSpec(
            num_scalar_prefetch=1,
            grid=(8,),
            in_specs=[
                pl.BlockSpec((1, part, width), lambda i, me: (jnp.minimum(i, 3), 0, 0)),
                pl.BlockSpec((1, part, width), lambda i, me: (jnp.maximum(i - 4, 0), 0, 0)),
            ],
            out_specs=pl.BlockSpec((part, width), where),
        ),
        out_shape=shape((8 * part, width), F32),
        compiler_params=pltpu.CompilerParams(vmem_limit_bytes=32 * 2**20),
        cost_estimate=pl.CostEstimate(flops=0, bytes_accessed=0, transcendentals=0),
        name="place_parts",
    )(me, four, other)


def unpack_kernel(own_q, me_ref, four, other, og, qg, sg, lines, qs, shared):
    me = me_ref[0]
    cut = own_q // 8
    tall = LANES // 8
    for ref, order in ((four, KEEP), (other, SEND)):
        for i in range(4):
            b = order[i] ^ me
            part = ref[i].astype(F32)
            rows = lambda size: pl.ds(pl.multiple_of(b * size, 8), size)
            og[rows(cut)] = part[:cut]
            qs[rows(cut)] = part[cut : 2 * cut]
            lines[pl.ds(b, 1)] = part[2 * cut : 2 * cut + 1]
            shared[rows(tall)] = part[2 * cut + 8 : 2 * cut + 8 + tall]
            lines[pl.ds(b + 8, 1)] = part[2 * cut + 8 + tall : 2 * cut + 9 + tall]
    qg[...] = qs[...].T
    sg[...] = shared[...].T


def unpack(me, four, other, own_q):
    feat = four.shape[2]
    return pl.pallas_call(
        functools.partial(unpack_kernel, own_q),
        in_specs=[SMEM, VMEM, VMEM],
        out_specs=[VMEM] * 4,
        out_shape=[
            shape((own_q, feat), F32), shape((feat, own_q), F32),
            shape((feat, LANES), F32), shape((16, feat), F32),
        ],
        scratch_shapes=[pltpu.VMEM((own_q, feat), F32), pltpu.VMEM((LANES, feat), F32)],
        compiler_params=pltpu.CompilerParams(vmem_limit_bytes=32 * 2**20),
        cost_estimate=pl.CostEstimate(flops=0, bytes_accessed=0, transcendentals=0),
        name="unpack",
    )(me, four, other)


def doc_layout(ends, scales, length):
    row = jnp.arange(length, dtype=jnp.int32)[None]
    begin = jnp.zeros_like(row)
    step = scales[:, :1]
    for d in range(ends.shape[1] - 1):
        past = row >= ends[:, d : d + 1]
        begin = jnp.where(past, ends[:, d : d + 1], begin)
        step = jnp.where(past, scales[:, d + 1 : d + 2], step)
    return (row - begin) * step


def angle_tables(placed, rows):
    freqs = 10000.0 ** (-jnp.arange(ROT // 2, dtype=F32) * 2.0 / ROT)
    blocks = placed.astype(F32).reshape(placed.shape[0], 4, 1, rows)
    angles = blocks * freqs[:, None]
    return jnp.cos(angles), jnp.sin(angles)


def on_device(
    size,
    tokens,
    cotangent,
    doc_ends,
    pos_scale,
    first_gain,
    first_bias,
    second_gain,
    second_bias,
    w_query,
    query_bias,
    w_shared,
    shared_bias,
    w_output,
    w_expand,
    expand_bias,
    w_contract,
    output_bias,
):
    micro, rows, feat = tokens.shape
    heads = w_query.shape[1] // 64
    own_q = w_query.shape[1]
    length = rows * 4
    rank = lax.axis_index("tp").astype(jnp.int32)[None]
    me = (lax.axis_index("dp").astype(jnp.int32) & 7)[None]

    order = Order()

    def begin(values):
        return values, swap(values, "tp", 4, 1), swap(values, "tp", 4, 2)

    def finish(own, near, far):
        return own, near, far, swap(far, "tp", 4, 1)

    xs, gs = begin(tokens), begin(cotangent)

    norms = (first_gain, first_bias, second_gain, second_bias)
    ends, scales = doc_ends[:, 0], pos_scale[:, 0]
    cs, sn = angle_tables(doc_layout(ends, scales, length), rows)

    act_a, slope_a, h1_a, h2_a, n_a = hidden(xs[:2], norms, w_expand, expand_bias)
    order.step(act_a)
    du_a, cacc, eacc, sums = hidden_back(order(me), gs[:2], act_a, slope_a, h2_a, w_contract)
    order.step(sums)
    xs = finish(xs[0], xs[1], order(xs[2]))
    act_b, slope_b, h1_b, h2_b, n_b = hidden(xs[2:], norms, w_expand, expand_bias)
    order.step(act_b)
    h1, n, act = (h1_a, h1_b), (n_a, n_b), (act_a, act_b)
    biases = (query_bias, shared_bias)
    saved0 = attend(
        0, order(rank), doc_ends, h1, w_query, w_shared, *biases, cs, sn, heads, 0
    )
    order.step(saved0[0])
    gs = finish(gs[0], gs[1], order(gs[2]))
    du_b, c_keep, c_send, e_keep, e_send, sums = hidden_back(
        order(me), gs[2:], act_b, slope_b, h2_b, w_contract, (cacc, eacc, sums)
    )
    order.step(sums)
    c = Sum(order, size, c_keep, c_send)
    weights = (w_query, w_shared, w_output, w_contract, w_expand, first_gain, second_gain)
    inputs = (gs, h1, act, (du_a, du_b), n, *weights, cs, sn, heads)
    *mine, send, og, qs, vec = attend_back(0, order(rank), me, saved0, *inputs)
    order.step(vec)
    c.kept()
    rows0 = Rows(order, mine, send)
    e = Sum(order, size, e_keep, e_send)
    *mine, send, r_keep, r_send = attend_back(
        1, order(rank), me, (doc_ends, *biases), *inputs, True, (og, qs, vec, sums)
    )
    order.step(r_send)
    rest = Sum(order, size, r_keep, r_send)
    c.near()
    e.kept()
    rows0.away()
    rows1 = Rows(order, mine, send)
    c.own()
    e.near()
    rest.kept()
    rows1.away()
    c.pair()
    e.own()
    rest.near()
    c.four()
    e.pair()
    rest.own(2 * (own_q // 8) + 8)
    rows0.land()
    e.four()
    rest.pair()
    contract_grad = order.step(place(order(me), *c.parts()))
    rest.four()
    rows1.land()
    late = order(tokens)
    expand_grad = place(me, *e.parts())
    output_grad, query_grad, shared_grad, lines = unpack(me, *rest.parts(), own_q)

    def joined(which):
        return jnp.stack([rows0.total[which], rows1.total[which]])

    x = late.astype(F32)
    layer_out = (x + joined(0) + output_bias).astype(BF)
    norm, scale = normalize_rows(x)
    e = joined(1)
    slope_mean = jnp.mean(e * norm, -1, keepdims=True)
    input_grad = cotangent.astype(F32) + scale * (
        e - jnp.mean(e, -1, keepdims=True) - norm * slope_mean
    )
    return (
        layer_out,
        input_grad,
        query_grad,
        lines[2, :own_q],
        shared_grad,
        lines[12, QW : QW + LANES],
        output_grad,
        expand_grad,
        lines[1, : expand_bias.shape[0]],
        contract_grad,
        lines[0],
        lines[8],
        lines[9],
        lines[10],
        lines[11],
    )


def normalize_rows(x):
    centre = x - jnp.mean(x, -1, keepdims=True)
    scale = lax.rsqrt(jnp.mean(centre * centre, -1, keepdims=True) + 1e-05)
    return centre * scale, scale


def solution(mesh):
    rows = P(None, ("dp", "tp"), None)
    in_specs = (
        rows, rows, P(None, "dp", None), P(None, "dp", None),
        P(), P(), P(), P(),
        P(None, "tp"), P("tp"), P(), P(), P("tp", None),
        P(None, "tp"), P("tp"), P("tp", None), P(),
    )
    out_specs = (
        rows, rows,
        P(None, "tp"), P("tp"), P(), P(), P("tp", None),
        P(None, "tp"), P("tp"), P("tp", None),
        P(), P(), P(), P(), P(),
    )
    return jax.shard_map(
        functools.partial(on_device, mesh.shape["dp"]),
        mesh=mesh,
        in_specs=in_specs,
        out_specs=out_specs,
        check_vma=False,
    )
```

```python
import functools

import jax
import jax.numpy as jnp
from jax import lax
from jax.experimental import pallas as pl
from jax.experimental.pallas import tpu as pltpu
from jax.sharding import PartitionSpec as P

ROT = 16
LANES = 128
QW = 256
PART = 72
LINES = ((0, 0), (1, 0), (2, 0), (8, 0), (9, 0), (10, 0), (11, 0), (12, QW))
BF = jnp.bfloat16
F32 = jnp.float32
ACROSS = (1, 2, 4)
ALONG = (2, 4, 1)
EXPAND = ALONG
BACK = ALONG
NT = (((1,), (1,)), ((), ()))
TN = (((0,), (0,)), ((), ()))
ANY = pl.BlockSpec(memory_space=pl.ANY)
VMEM = pl.BlockSpec(memory_space=pltpu.VMEM)
SMEM = pl.BlockSpec(memory_space=pltpu.SMEM)


def dot(a, b):
    return jnp.dot(a, b, preferred_element_type=F32)


def dot_nt(a, b):
    return lax.dot_general(a, b, NT, preferred_element_type=F32)


def dot_tn(a, b):
    return lax.dot_general(a, b, TN, preferred_element_type=F32)


def shape(dims, dtype=BF):
    return jax.ShapeDtypeStruct(dims, dtype)


def call(kernel, name, ins, outs, scratch, copies, flops=10**10):
    specs = [s for _, s in ins]
    arrays = [a for a, _ in ins]
    return pl.pallas_call(
        kernel,
        in_specs=specs,
        out_specs=[s for _, s in outs],
        out_shape=[o for o, _ in outs],
        scratch_shapes=list(scratch) + [pltpu.SemaphoreType.DMA((copies,))],
        compiler_params=pltpu.CompilerParams(vmem_limit_bytes=64 * 2**20 - 65536),
        cost_estimate=pl.CostEstimate(flops=flops, bytes_accessed=0, transcendentals=0),
        name=name,
    )(*arrays)


def offsets(bits):
    keep = (0, bits[2], bits[1], bits[1] | bits[2])
    return keep, tuple(k ^ bits[0] for k in keep)


class Copies:
    def __init__(self, sems):
        self.sems = sems
        self.count = 0

    def start(self, src, dst):
        copy = pltpu.make_async_copy(src, dst, self.sems.at[self.count])
        self.count += 1
        copy.start()
        return copy


def normalize(x):
    centre = x - jnp.mean(x, -1, keepdims=True)
    spread = jnp.mean(centre * centre, -1, keepdims=True)
    return centre * lax.rsqrt(spread + 1e-05)


def line(ref):
    return ref[...].reshape(1, -1)


def swap_halves(w):
    lane = lax.broadcasted_iota(jnp.int32, w.shape, 1)
    up = pltpu.roll(w, w.shape[1] - ROT // 2, 1)
    down = pltpu.roll(w, ROT // 2, 1)
    return jnp.where((lane % 64) < ROT // 2, up, down)


def spread_table(compact, filler, signs):
    fill = jnp.full((64 - ROT, compact.shape[1]), filler, F32)
    head = [signs * compact, compact, fill]
    return jnp.concatenate(head + head, 0).T


def hidden_kernel(
    pa, pb, gain1, bias1, gain2, bias2, we, be, acto, slopeo, h1o, h2o, no, xs, wev, acts, slopes, h1s, h2s, ns, sems
):
    copies = Copies(sems)
    got = [copies.start(pa, xs.at[0])]
    gotw = copies.start(we, wev)
    got.append(copies.start(pb, xs.at[1]))
    out = []
    for j in range(2):
        got[j].wait()
        for m in range(2):
            n = normalize(xs[j, m].astype(F32))
            ns[m, j] = n.astype(BF)
            h1s[m, j] = (n * line(gain1) + line(bias1)).astype(BF)
            h2 = (n * line(gain2) + line(bias2)).astype(BF)
            h2s[m, j] = h2
            for a, b in ((ns, no), (h1s, h1o), (h2s, h2o)):
                out.append(copies.start(a.at[m, j], b.at[m, j]))
            if j == 0 and m == 0:
                gotw.wait()
            u = dot(h2, wev[...]) + line(be)
            phi = 0.5 * (1.0 + lax.erf(u * 0.7071067811865476))
            acts[m, j] = (u * phi).astype(BF)
            slopes[m, j] = (phi + u * jnp.exp(-0.5 * u * u) * 0.3989422804014327).astype(BF)
            for a, b in ((acts, acto), (slopes, slopeo)):
                out.append(copies.start(a.at[m, j], b.at[m, j]))
    for c in out:
        c.wait()


def hidden(pieces, norms, we, be):
    _, rows, feat = pieces[0].shape
    ff = we.shape[1]
    wide, narrow = (2, 2, rows, ff), (2, 2, rows, feat)
    return call(
        hidden_kernel,
        "hidden",
        [(x, ANY) for x in pieces] + [(a, VMEM) for a in norms] + [(we, ANY), (be, VMEM)],
        [(shape(wide), ANY)] * 2 + [(shape(narrow), ANY)] * 3,
        [pltpu.VMEM(narrow, BF), pltpu.VMEM(we.shape, BF)]
        + [pltpu.VMEM(wide, BF)] * 2
        + [pltpu.VMEM(narrow, BF)] * 3,
        23,
        0,
    )


def doubled(kv):
    kv = kv.astype(F32)
    swapped = pltpu.roll(kv, 64, 1)
    low = lax.broadcasted_iota(jnp.int32, kv.shape, 1) < 64
    return jnp.where(low, kv, swapped).astype(BF), jnp.where(low, swapped, kv).astype(BF)


def stack_heads(block, heads):
    low = lax.broadcasted_iota(jnp.int32, (block.shape[0], LANES), 1) < 64
    zero = jnp.zeros((block.shape[0], LANES), block.dtype)
    parts = []
    for h in range(heads):
        part = block[:, LANES * (h // 2) : LANES * (h // 2 + 1)]
        parts.append(jnp.where(low, part, zero) if h % 2 == 0 else jnp.where(low, zero, part))
    return jnp.concatenate(parts, 0)


def join_heads(stacked, heads, rows):
    low = lax.broadcasted_iota(jnp.int32, (rows, LANES), 1) < 64
    part = lambda h: stacked[h * rows : (h + 1) * rows]
    zero = jnp.zeros((rows, LANES), stacked.dtype)
    cols = []
    for h in range(0, heads, 2):
        cols.append(jnp.where(low, part(h), part(h + 1) if h + 1 < heads else zero))
    return jnp.concatenate(cols, 1)


def send_rows(copies, rows, mine, send, which):
    places = (mine[0].at[which], send.at[0, which], mine[1].at[which], send.at[1, which])
    return [copies.start(rows.at[r], place) for r, place in enumerate(places)]


def halves_to(copies, halves, micro_id, into, t):
    return [
        copies.start(halves[r // 2].at[micro_id, r % 2], into.at[r ^ t]) for r in range(4)
    ]


def join_weights(wss, wts):
    wts[QW:] = wss[...].T


def project(micro_id, h1s, wts, qbias, sbias, bqkv, cs, sn, saved):
    qrs, kk, vv = saved[:3]
    rows = h1s.shape[1]
    own_q = qbias.shape[0]
    bqkv[:, :own_q] = line(qbias)
    bqkv[:, own_q:QW] = jnp.zeros((1, QW - own_q), F32)
    bqkv[:, QW:] = line(sbias)
    for a in range(4):
        here = slice(a * rows, (a + 1) * rows)
        qkv = dot_nt(h1s[a], wts[...]) + bqkv[...]
        c = spread_table(cs[micro_id, a], 1.0, 1.0)
        s = spread_table(sn[micro_id, a], 0.0, -1.0)
        low = lax.broadcasted_iota(jnp.int32, c.shape, 1) < 64
        cos = jnp.concatenate([c, c, jnp.where(low, c, 1.0)], 1)
        sin = jnp.concatenate([s, s, jnp.where(low, s, 0.0)], 1)
        qkv = qkv * cos + swap_halves(qkv) * sin
        qrs[a] = (qkv[:, :QW] * 0.125).astype(BF)
        kk[here], vv[here] = doubled(qkv[:, QW:].astype(BF))


def attend_rows(micro_id, heads, ends, saved):
    qrs, kk, vv, cx, *probs_of = saved
    rows = qrs.shape[1]
    spans = [(a + 1) * rows for a in range(4)]
    scores = dot_nt(stack_heads(qrs[3], heads), kk[: spans[3]])
    for a in (3, 2, 1, 0):
        here = scores
        if a > 0:
            scores = dot_nt(stack_heads(qrs[a - 1], heads), kk[: spans[a - 1]])
        row = lax.broadcasted_iota(jnp.int32, (rows, 1), 0) + a * rows
        begin = jnp.zeros((rows, 1), jnp.int32)
        for d in range(ends.shape[2] - 1):
            begin = jnp.where(row >= ends[micro_id, 0, d], ends[micro_id, 0, d], begin)
        col = lax.broadcasted_iota(jnp.int32, (rows, spans[a]), 1)
        allowed = (col >= begin) & (col <= row)
        for h in range(heads):
            mine = slice(h * rows, (h + 1) * rows)
            s = jnp.where(allowed, here[mine], -1e30)
            e = jnp.exp(s - jnp.max(s, -1, keepdims=True))
            probs_of[a][mine] = (e * (1.0 / jnp.sum(e, -1, keepdims=True))).astype(BF)
        done = a + 1
        if done < 4:
            cx[done] = join_heads(dot(probs_of[done][...], vv[: spans[done]]), heads, rows).astype(BF)
    cx[0] = join_heads(dot(probs_of[0][...], vv[: spans[0]]), heads, rows).astype(BF)


def attend_kernel(micro_id, heads, *refs):
    refs = list(refs)
    take = lambda k: [refs.pop(0) for _ in range(k)]
    t_ref, ends = take(2)
    h1 = take(2)
    wq, ws, qbias, sbias, cs, sn = take(6)
    outs = take(8)
    h1s, wss, wts, bqkv = take(4)
    saved = take(8)
    copies = Copies(take(1)[0])
    got = load_weights(copies, wq, ws, wss, wts)
    got += halves_to(copies, h1, micro_id, h1s, t_ref[0])
    for c in got:
        c.wait()
    join_weights(wss, wts)
    project(micro_id, h1s, wts, qbias, sbias, bqkv, cs, sn, saved)
    sent = [copies.start(saved[i], outs[i]) for i in range(3)]
    attend_rows(micro_id, heads, ends, saved)
    sent += [copies.start(saved[i], outs[i]) for i in range(3, 8)]
    for c in sent:
        c.wait()


def load_weights(copies, wq, ws, wss, wts):
    own_q = wq.shape[0]
    wts[own_q:QW] = jnp.zeros((QW - own_q, wts.shape[1]), BF)
    return [copies.start(wq, wts.at[pl.ds(0, own_q)]), copies.start(ws, wss)]


def weights_scratch(ws):
    width = QW + LANES
    return [
        pltpu.VMEM(ws.shape, BF), pltpu.VMEM((width, ws.shape[0]), BF), pltpu.VMEM((1, width), F32)
    ]


def saved_shapes(rows, heads):
    length = 4 * rows
    saved = [(4, rows, QW), (length, LANES), (length, LANES), (4, rows, QW)]
    return saved + [(heads * rows, (a + 1) * rows) for a in range(4)]


def attend(micro_id, rank, ends, h1, wq, ws, qbias, sbias, cs, sn, heads, flops):
    _, _, rows, feat = h1[0].shape
    ins = [(rank, SMEM), (ends, SMEM)] + [(a, ANY) for a in (*h1, wq, ws)]
    ins += [(a, VMEM) for a in (qbias, sbias, cs, sn)]
    saved = saved_shapes(rows, heads)
    scratch = [pltpu.VMEM((4, rows, feat), BF)] + weights_scratch(ws)
    return call(
        functools.partial(attend_kernel, micro_id, heads), "attend", ins,
        [(shape(a), ANY) for a in saved], scratch + [pltpu.VMEM(a, BF) for a in saved], 14, flops,
    )


def attend_back_kernel(micro_id, heads, first, whole, *refs):
    refs = list(refs)
    take = lambda k: [refs.pop(0) for _ in range(k)]
    t_ref, me_ref = take(2)
    if whole:
        ends, qbias, sbias = take(3)
    else:
        saved = take(8)
    gpieces = take(4)
    h1, act, du, n = take(2), take(2), take(2), take(2)
    wq, ws, wo, wc, we, gain1, gain2, cs, sn = take(9)
    if not first:
        og_in, qs_in, vec_in, hid_in = take(4)
    rows_kept = take(2)
    rows_sent, = take(1)
    results = take(3 if first else 2)
    gs, h1s, acts, dus, ns, wss, wts, bqkv, wos, wcs, wes = take(11)
    qrs, kk, vv, cx, *probs_of = kept = take(8)
    dctx, = take(1)
    dss = take(2)
    dk, dv, dqkv, outb, eb, ogs, qss = take(7)
    if not first:
        lines, keeps, sends = take(3)
    copies = Copies(take(1)[0])
    rows = gs.shape[1]
    t = t_ref[0]
    spans = [(a + 1) * rows for a in range(4)]
    def load_h():
        return load_weights(copies, wq, ws, wss, wts) + halves_to(copies, h1, micro_id, h1s, t)

    if whole:
        got_h = load_h()
    own_q = wo.shape[0]
    got_g = [copies.start(wo, wos.at[pl.ds(0, own_q)])]
    wos[own_q:] = jnp.zeros((QW - own_q, wo.shape[1]), BF)
    got_g += [copies.start(g.at[micro_id], gs.at[r ^ t]) for r, g in enumerate(gpieces)]
    order = (2, 7, 0, 1, 6, 5, 4, 3)
    got_saved = [] if whole else [copies.start(saved[i], kept[i]) for i in order]
    got_out = halves_to(copies, act, micro_id, acts, 0) + [copies.start(wc, wcs)]
    if not whole:
        got_h = load_h()
    got_e = halves_to(copies, du, micro_id, dus, 0) + [copies.start(we, wes)]
    got_e += halves_to(copies, n, micro_id, ns, 0)
    if not first:
        got_e += [copies.start(og_in, ogs), copies.start(qs_in, qss)]
    if whole:
        for c in got_h:
            c.wait()
        join_weights(wss, wts)
        project(micro_id, h1s, wts, qbias, sbias, bqkv, cs, sn, kept)
        attend_rows(micro_id, heads, ends, kept)
    for c in got_g:
        c.wait()
    dctx[...] = dot_nt(gs[...].reshape(4 * rows, gs.shape[2]), wos[...]).astype(BF)
    for c in got_saved:
        c.wait()
    dk[...] = jnp.zeros_like(dk)
    dv[...] = jnp.zeros_like(dv)
    stacked = lambda a: stack_heads(dctx[a * rows : (a + 1) * rows], heads)

    def finish(a):
        dscores = dss[a % 2][:, : spans[a]]
        dk[: spans[a]] += dot_tn(dscores, stack_heads(qrs[a], heads))
        dv[: spans[a]] += dot_tn(probs_of[a][...], stacked(a))
        dq = join_heads(dot(dscores, kk[: spans[a]]), heads, rows) * 0.125
        c = spread_table(cs[micro_id, a], 1.0, 1.0)
        s = spread_table(sn[micro_id, a], 0.0, -1.0)
        cos = jnp.concatenate([c, c], 1)
        sin = jnp.concatenate([s, s], 1)
        dqkv[a, :, :QW] = (dq * cos - swap_halves(dq) * sin).astype(BF)

    dprobs = dot_nt(stacked(3), vv[: spans[3]])
    for a in (3, 2, 1, 0):
        here = dprobs
        if a > 0:
            dprobs = dot_nt(stacked(a - 1), vv[: spans[a - 1]])
        for h in range(heads):
            mine = slice(h * rows, (h + 1) * rows)
            p = probs_of[a][mine].astype(F32)
            weighted = p * here[mine]
            delta = jnp.sum(weighted, -1, keepdims=True)
            dss[a % 2][mine, : spans[a]] = (weighted - p * delta).astype(BF)
        if a < 3:
            finish(a + 1)
    finish(0)
    for a in range(4):
        here = slice(a * rows, (a + 1) * rows)
        c = spread_table(cs[micro_id, a], 1.0, 1.0)
        s = spread_table(sn[micro_id, a], 0.0, -1.0)
        dkf = dk[here] + pltpu.roll(dk[here], 64, 1)
        dvf = dv[here] + pltpu.roll(dv[here], 64, 1)
        dkf = dkf * c - swap_halves(dkf) * s
        low = lax.broadcasted_iota(jnp.int32, dkf.shape, 1) < 64
        dqkv[a, :, QW:] = jnp.where(low, dkf, dvf).astype(BF)
    for c in got_out:
        c.wait()
    for r in range(4):
        outb[r] = (dot(cx[r ^ t], wos[...]) + dot(acts[r], wcs[...])).astype(BF)
    sent = send_rows(copies, outb, rows_kept, rows_sent, 0)

    for c in got_e + ([] if whole else got_h):
        c.wait()
    if not whole:
        join_weights(wss, wts)
    width = QW + LANES
    vec_width = gs.shape[2]
    flat = dqkv[...].reshape(4 * rows, width)
    ograd = dot_tn(cx[...].reshape(4 * rows, QW), gs[...].reshape(4 * rows, gs.shape[2]))
    qgrad = dot_tn(flat, h1s[...].reshape(4 * rows, h1s.shape[2]))
    ogs[...] = ograd if first else ogs[...] + ograd
    qss[...] = qgrad if first else qss[...] + qgrad
    if first:
        sent += [copies.start(ogs, results[0]), copies.start(qss, results[1])]
    sums = [jnp.zeros((1, vec_width), F32) for _ in range(4)]
    for r in range(4):
        e1 = dot(dqkv[r ^ t], wts[...])
        e2 = dot_nt(dus[r], wes[...])
        eb[r] = (e1 * line(gain1) + e2 * line(gain2)).astype(BF)
        norm = ns[r].astype(F32)
        for i, term in enumerate((e1 * norm, e1, e2 * norm, e2)):
            sums[i] += jnp.sum(term, 0, keepdims=True)
    sent += send_rows(copies, eb, rows_kept, rows_sent, 1)
    column = jnp.sum(flat.astype(F32), 0, keepdims=True)
    sums.append(jnp.concatenate([column, jnp.zeros((1, vec_width - width), F32)], 1))
    if first:
        results[2][...] = jnp.concatenate(sums + [jnp.zeros((3, vec_width), F32)], 0)
    else:
        sums = [a + vec_in[i : i + 1] for i, a in enumerate(sums)]
        zero = jnp.zeros((5, vec_width), F32)
        lines[...] = jnp.concatenate(
            [hid_in[0:1], hid_in[1:2], sums[4], zero] + sums + [zero[:3]], 0
        )
        pack_parts(ogs, qss, lines, keeps, sends, me_ref[0], heads * 8)
        sent += [copies.start(keeps, results[0]), copies.start(sends, results[1])]
    for c in sent:
        c.wait()


def pack_parts(og, qs, lines, keep, send, me, cut):
    tall = LANES // 8
    for out, order in zip((keep, send), offsets(ACROSS)):
        for i in range(4):
            b = order[i] ^ me
            rows = lambda ref, size, base: ref[pl.ds(pl.multiple_of(b * size + base, 8), size)]
            line = lambda i: jnp.broadcast_to(lines[pl.ds(b + i, 1)], (8, lines.shape[1]))
            own = lax.broadcasted_iota(jnp.int32, (8, lines.shape[1]), 0) < 4
            both = jnp.where(own, line(0), line(8))
            part = [rows(og, cut, 0), rows(qs, cut, 0), rows(qs, tall, QW), both]
            out[i] = jnp.concatenate(part, 0).astype(BF)


def attend_back(
    micro_id, rank, me, saved, gs, h1, act, du, n, wq, ws, wo, wc, we, gain1, gain2, cs, sn, heads,
    whole=False, before=None,
):
    _, rows, feat = gs[0].shape
    ff = wc.shape[0]
    width = QW + LANES
    length = 4 * rows
    first = before is None
    ins = [(rank, SMEM), (me, SMEM)]
    ins += [(saved[0], SMEM)] + [(a, VMEM) for a in saved[1:]] if whole else [(a, ANY) for a in saved]
    ins += [(a, ANY) for a in (*gs, *h1, *act, *du, *n, wq, ws, wo, wc, we)]
    ins += [(a, VMEM) for a in (gain1, gain2, cs, sn)]
    if not first:
        ins += [(a, ANY) for a in before[:2]] + [(a, VMEM) for a in before[2:]]
    outs = [(shape((2, rows, feat)), ANY)] * 2 + [(shape((2, 2, rows, feat)), ANY)]
    grads = [shape((QW, feat), F32), shape((width, feat), F32)]
    part = shape((4, PART, feat))
    if first:
        outs += [(g, ANY) for g in grads] + [(shape((8, feat), F32), VMEM)]
    else:
        outs += [(part, ANY)] * 2
    stack, wide = pltpu.VMEM((4, rows, feat), BF), pltpu.VMEM((4, rows, ff), BF)
    scratch = [stack, stack, wide, wide, stack]
    scratch += weights_scratch(ws)
    scratch += [pltpu.VMEM(a, BF) for a in ((QW, feat), wc.shape, we.shape)]
    scratch += [pltpu.VMEM(a, BF) for a in saved_shapes(rows, heads)]
    scratch += [
        pltpu.VMEM((length, QW), BF),
        pltpu.VMEM((heads * rows, length), BF), pltpu.VMEM((heads * rows, length), BF),
        pltpu.VMEM((length, LANES), F32), pltpu.VMEM((length, LANES), F32),
        pltpu.VMEM((4, rows, width), BF), stack, stack,
    ]
    scratch += [pltpu.VMEM(g.shape, F32) for g in grads]
    if not first:
        scratch += [pltpu.VMEM((16, feat), F32)] + [pltpu.VMEM(part.shape, BF)] * 2
    return call(
        functools.partial(attend_back_kernel, micro_id, heads, first, whole), "attend_grad", ins, outs,
        scratch, 46,
    )


def store_parts(total, parts, me, bits):
    part = total.shape[0] // 8
    for b in range(8):
        offset = b ^ me
        place = sum(((offset // bit) % 2) * weight for bit, weight in zip(bits, (4, 2, 1)))
        parts[place] = total[b * part : (b + 1) * part].astype(BF)


def pieces_to(copies, pieces, into):
    return [copies.start(p.at[m], into.at[m, j]) for j, p in enumerate(pieces) for m in range(2)]


def flat(ref):
    return ref[...].reshape(-1, ref.shape[-1])


def hidden_back_kernel(first, *refs):
    refs = list(refs)
    take = lambda k: [refs.pop(0) for _ in range(k)]
    me_ref, = take(1)
    pieces = take(2)
    act, slope, h2, wc = take(4)
    if not first:
        before = take(2)
        sums_in, = take(1)
    duo, = take(1)
    outs = take(2 if first else 4)
    sums, = take(1)
    gs, acts, slopes, wcs, h2s, dus, *accs = take(8)
    parts = None if first else take(2)
    copies = Copies(take(1)[0])
    got = pieces_to(copies, pieces, gs) + [copies.start(act, acts)]
    got_back = [copies.start(wc, wcs), copies.start(slope, slopes)]
    got_late = [copies.start(h2, h2s)]
    if not first:
        got_sums = [copies.start(a, b) for a, b in zip(before, accs)]

    def total(i, left, right):
        if first:
            accs[i][...] = dot_tn(flat(left), flat(right))
            return [copies.start(accs[i], outs[i])]
        got_sums[i].wait()
        both = accs[i][...] + dot_tn(flat(left), flat(right))
        store_parts(both, parts[i], me_ref[0], (ACROSS, EXPAND)[i])
        return [copies.start(parts[i].at[pl.ds(4 * k, 4)], outs[2 * i + k]) for k in (0, 1)]

    for c in got:
        c.wait()
    sent = total(0, acts, gs)
    for c in got_back:
        c.wait()
    gsum = jnp.zeros((1, gs.shape[3]), F32)
    column = jnp.zeros((1, slopes.shape[3]), F32)
    for m in range(2):
        for j in range(2):
            g = gs[m, j]
            du = (dot_nt(g, wcs[...]) * slopes[m, j].astype(F32)).astype(BF)
            dus[m, j] = du
            gsum += jnp.sum(g.astype(F32), 0, keepdims=True)
            column += jnp.sum(du.astype(F32), 0, keepdims=True)
    sent.append(copies.start(dus, duo))
    for c in got_late:
        c.wait()
    sent += total(1, h2s, dus)
    rowid = lax.broadcasted_iota(jnp.int32, sums.shape, 0)
    both = jnp.where(rowid == 0, gsum, jnp.where(rowid == 1, column, 0.0))
    sums[...] = both if first else sums_in[...] + both
    for c in sent:
        c.wait()


def hidden_back(me, pieces, act, slope, h2, wc, before=None):
    _, _, rows, feat = h2.shape
    ff = wc.shape[0]
    first = before is None
    ins = [(me, SMEM)] + [(a, ANY) for a in (*pieces, act, slope, h2, wc)]
    outs = [(shape(slope.shape), ANY)]
    if first:
        outs += [(shape((ff, feat), F32), ANY), (shape((feat, ff), F32), ANY)]
    else:
        ins += [(before[0], ANY), (before[1], ANY), (before[2], VMEM)]
        outs += [(shape((4, ff // 8, feat)), ANY)] * 2 + [(shape((4, feat // 8, ff)), ANY)] * 2
    outs.append((shape((8, feat), F32), VMEM))
    scratch = [
        pltpu.VMEM(h2.shape, BF), pltpu.VMEM(act.shape, BF), pltpu.VMEM(slope.shape, BF),
        pltpu.VMEM(wc.shape, BF), pltpu.VMEM(h2.shape, BF), pltpu.VMEM(slope.shape, BF),
        pltpu.VMEM((ff, feat), F32), pltpu.VMEM((feat, ff), F32),
    ]
    if not first:
        scratch += [pltpu.VMEM((8, ff // 8, feat), BF), pltpu.VMEM((8, feat // 8, ff), BF)]
    return call(
        functools.partial(hidden_back_kernel, first), "hidden_grad", ins, outs, scratch, 15,
        0 if first else 10**10,
    )


def after(value, *others):
    return lax.optimization_barrier((value, others))[0]


def add(*terms):
    return sum(a.astype(F32) for a in terms).astype(BF)


def swap(value, axis, size, bit):
    return lax.ppermute(value, axis, [(i, i ^ bit) for i in range(size)])


class Order:
    def __init__(self):
        self.last = None

    def __call__(self, value):
        if self.last is not None:
            value = after(value, self.last)
        return value

    def step(self, result):
        self.last = result
        return result


class Sum:
    def __init__(self, order, size, keep, send, bits, back):
        self.order, self.size, self.bits, self.back = order, size, bits, back
        self.have = keep
        self.flying = swap(order(send), "dp", size, bits[0])

    def kept(self):
        have = self.order(self.have)
        halves = add(have[:2], self.flying[:2]), add(have[2:], self.flying[2:])
        self.have, send = self.order.step(halves)
        self.flying = swap(send, "dp", self.size, self.bits[1])

    def near(self):
        have = self.order(self.have)
        halves = add(have[0], self.flying[0]), add(have[1], self.flying[1])
        self.have, send = self.order.step(halves)
        self.flying = swap(send, "dp", self.size, self.bits[2])

    def own(self, over_tp=0):
        own = self.order.step(add(self.order(self.have), self.flying))
        if over_tp:
            tail = own[over_tp:]
            whole = add(tail, *[swap(tail, "tp", 4, bit) for bit in (1, 2, 3)])
            row = lax.broadcasted_iota(jnp.int32, tail.shape, 0) - LANES // 8
            whole = jnp.where((row >= 0) & (row < 4), tail, whole)
            own = self.order.step(jnp.concatenate([self.order(own[:over_tp]), whole], 0))
        if self.size > 8:
            groups = [[low + 8 * high for high in range(self.size // 8)] for low in range(8)]
            own = lax.psum(own.astype(F32), "dp", axis_index_groups=groups).astype(BF)
        self.have = own
        self.flying = swap(own, "dp", self.size, self.back[2])

    def pair(self):
        self.have = self.order.step(jnp.stack([self.order(self.have), self.flying]))
        self.flying = swap(self.have, "dp", self.size, self.back[1])

    def four(self):
        self.have = self.order.step(jnp.concatenate([self.order(self.have), self.flying], 0))
        self.flying = swap(self.have, "dp", self.size, self.back[0])

    def parts(self):
        return self.have, self.flying


class Rows:
    def __init__(self, order, mine, send):
        self.order, self.mine = order, mine
        self.got = swap(order(send), "tp", 4, 1)

    def away(self):
        away = self.order.step(add(self.order(self.mine[1]), self.got[1]))
        self.far = swap(away, "tp", 4, 2)

    def land(self):
        terms = self.order(self.mine[0]), self.got[0], self.far
        self.total = self.order.step(sum(a.astype(F32) for a in terms))


def place_kernel(me_ref, four, other, out):
    i = pl.program_id(0)

    @pl.when(i < 4)
    def _():
        out[...] = four[0].astype(F32)

    @pl.when(i >= 4)
    def _():
        out[...] = other[0].astype(F32)


def place(me, four, other, bits):
    _, part, width = four.shape

    def where(i, me):
        j = i % 4
        order = (j // 2) * bits[1] + (j % 2) * bits[2] + (i // 4) * bits[0]
        return order ^ me[0], 0

    return pl.pallas_call(
        place_kernel,
        grid_spec=pltpu.PrefetchScalarGridSpec(
            num_scalar_prefetch=1,
            grid=(8,),
            in_specs=[
                pl.BlockSpec((1, part, width), lambda i, me: (jnp.minimum(i, 3), 0, 0)),
                pl.BlockSpec((1, part, width), lambda i, me: (jnp.maximum(i - 4, 0), 0, 0)),
            ],
            out_specs=pl.BlockSpec((part, width), where),
        ),
        out_shape=shape((8 * part, width), F32),
        compiler_params=pltpu.CompilerParams(vmem_limit_bytes=32 * 2**20),
        cost_estimate=pl.CostEstimate(flops=0, bytes_accessed=0, transcendentals=0),
        name="place_parts",
    )(me, four, other)


def unpack_kernel(own_q, me_ref, four, other, og, qs, sg, *refs):
    *vectors, shared, lines = refs
    me = me_ref[0]
    cut = own_q // 8
    tall = LANES // 8
    for ref, order in zip((four, other), offsets(ACROSS)):
        for i in range(4):
            b = order[i] ^ me
            part = ref[i].astype(F32)
            rows = lambda size: pl.ds(pl.multiple_of(b * size, 8), size)
            og[rows(cut)] = part[:cut]
            qs[rows(cut)] = part[cut : 2 * cut]
            shared[rows(tall)] = part[2 * cut : 2 * cut + tall]
            last = part[2 * cut + tall :]
            lines[pl.ds(b, 1)] = last[:1]
            lines[pl.ds(b + 8, 1)] = last[4:5]
    sg[...] = shared[...].T
    for ref, (i, base) in zip(vectors, LINES):
        ref[...] = lines[i, base : base + ref.shape[0]]


def unpack(me, four, other, own_q, ff):
    feat = four.shape[2]
    sizes = (feat, ff, own_q, feat, feat, feat, feat, LANES)
    outs = [(own_q, feat), (own_q, feat), (feat, LANES)] + [(n,) for n in sizes]
    return pl.pallas_call(
        functools.partial(unpack_kernel, own_q),
        in_specs=[SMEM, VMEM, VMEM],
        out_specs=[VMEM] * len(outs),
        out_shape=[shape(a, F32) for a in outs],
        scratch_shapes=[pltpu.VMEM((LANES, feat), F32), pltpu.VMEM((16, feat), F32)],
        compiler_params=pltpu.CompilerParams(vmem_limit_bytes=32 * 2**20),
        cost_estimate=pl.CostEstimate(flops=0, bytes_accessed=0, transcendentals=0),
        name="unpack",
    )(me, four, other)


def doc_layout(ends, scales, length):
    row = jnp.arange(length, dtype=jnp.int32)[None]
    begin = jnp.zeros_like(row)
    step = scales[:, :1]
    for d in range(ends.shape[1] - 1):
        past = row >= ends[:, d : d + 1]
        begin = jnp.where(past, ends[:, d : d + 1], begin)
        step = jnp.where(past, scales[:, d + 1 : d + 2], step)
    return (row - begin) * step


def angle_tables(placed, rows):
    freqs = 10000.0 ** (-jnp.arange(ROT // 2, dtype=F32) * 2.0 / ROT)
    blocks = placed.astype(F32).reshape(placed.shape[0], 4, 1, rows)
    angles = blocks * freqs[:, None]
    return jnp.cos(angles), jnp.sin(angles)


def on_device(
    size,
    tokens,
    cotangent,
    doc_ends,
    pos_scale,
    first_gain,
    first_bias,
    second_gain,
    second_bias,
    w_query,
    query_bias,
    w_shared,
    shared_bias,
    w_output,
    w_expand,
    expand_bias,
    w_contract,
    output_bias,
):
    micro, rows, feat = tokens.shape
    heads = w_query.shape[1] // 64
    own_q = w_query.shape[1]
    length = rows * 4
    rank = lax.axis_index("tp").astype(jnp.int32)[None]
    me = (lax.axis_index("dp").astype(jnp.int32) & 7)[None]

    order = Order()

    def begin(values):
        return values, swap(values, "tp", 4, 1), swap(values, "tp", 4, 2)

    def finish(own, near, far):
        return own, near, far, swap(far, "tp", 4, 1)

    xs, gs = begin(tokens), begin(cotangent)

    norms = (first_gain, first_bias, second_gain, second_bias)
    ends, scales = doc_ends[:, 0], pos_scale[:, 0]
    cs, sn = angle_tables(doc_layout(ends, scales, length), rows)

    act_a, slope_a, h1_a, h2_a, n_a = hidden(xs[:2], norms, w_expand, expand_bias)
    order.step(act_a)
    du_a, cacc, eacc, sums = hidden_back(order(me), gs[:2], act_a, slope_a, h2_a, w_contract)
    order.step(sums)
    xs = finish(xs[0], xs[1], order(xs[2]))
    act_b, slope_b, h1_b, h2_b, n_b = hidden(xs[2:], norms, w_expand, expand_bias)
    order.step(act_b)
    h1, n, act = (h1_a, h1_b), (n_a, n_b), (act_a, act_b)
    biases = (query_bias, shared_bias)
    saved0 = attend(
        0, order(rank), doc_ends, h1, w_query.T, w_shared, *biases, cs, sn, heads, 0
    )
    order.step(saved0[0])
    gs = finish(gs[0], gs[1], order(gs[2]))
    du_b, c_keep, c_send, e_keep, e_send, sums = hidden_back(
        order(me), gs[2:], act_b, slope_b, h2_b, w_contract, (cacc, eacc, sums)
    )
    order.step(sums)
    weights = (w_query.T, w_shared, w_output, w_contract, w_expand, first_gain, second_gain)
    inputs = (gs, h1, act, (du_a, du_b), n, *weights, cs, sn, heads)
    weights = (w_query.T, w_shared, w_output, w_contract, w_expand, first_gain, second_gain)
    inputs = (gs, h1, act, (du_a, du_b), n, *weights, cs, sn, heads)
    weights = (w_query.T, w_shared, w_output, w_contract, w_expand, first_gain, second_gain)
    inputs = (gs, h1, act, (du_a, du_b), n, *weights, cs, sn, heads)
    weights = (w_query.T, w_shared, w_output, w_contract, w_expand, first_gain, second_gain)
    inputs = (gs, h1, act, (du_a, du_b), n, *weights, cs, sn, heads)
    weights = (w_query.T, w_shared, w_output, w_contract, w_expand, first_gain, second_gain)
    inputs = (gs, h1, act, (du_a, du_b), n, *weights, cs, sn, heads)
    c = Sum(order, size, c_keep, c_send, ACROSS, ACROSS)
    e = Sum(order, size, e_keep, e_send, EXPAND, BACK)
    *mine0, send0, og, qs, vec = attend_back(0, order(rank), me, saved0, *inputs)
    order.step(vec)
    c.kept()
    e.kept()
    rows0 = Rows(order, mine0, send0)
    *mine1, send1, r_keep, r_send = attend_back(
        1, order(rank), me, (doc_ends, *biases), *inputs, True, (og, qs, vec, sums)
    )
    order.step(r_send)
    rest = Sum(order, size, r_keep, r_send, ACROSS, ACROSS)
    c.near()
    e.near()
    rows0.away()
    rows1 = Rows(order, mine1, send1)
    rest.kept()
    c.own()
    e.own()
    rest.near()
    e.pair()
    c.pair()
    rows0.land()
    rest.own(2 * (own_q // 8))
    rows1.away()
    c.four()
    e.four()
    rest.pair()
    contract_grad = order.step(place(order(me), *c.parts(), ACROSS))
    rest.four()
    rows1.land()
    expand_grad = order.step(place(order(me), *e.parts(), BACK))
    late = order(tokens)
    output_grad, query_grad, shared_grad, *vectors = unpack(
        me, *rest.parts(), own_q, expand_bias.shape[0]
    )
    out_bias, hidden_bias, query_bias, gain1, bias1, gain2, bias2, kv_bias = vectors

    def joined(which):
        return jnp.stack([rows0.total[which], rows1.total[which]])

    x = late.astype(F32)
    layer_out = (x + joined(0) + output_bias).astype(BF)
    norm, scale = normalize_rows(x)
    e = joined(1)
    slope_mean = jnp.mean(e * norm, -1, keepdims=True)
    input_grad = cotangent.astype(F32) + scale * (
        e - jnp.mean(e, -1, keepdims=True) - norm * slope_mean
    )
    return (
        layer_out,
        input_grad,
        query_grad.T,
        query_bias,
        shared_grad,
        kv_bias,
        output_grad,
        expand_grad,
        hidden_bias,
        contract_grad,
        out_bias,
        gain1,
        bias1,
        gain2,
        bias2,
    )


def normalize_rows(x):
    centre = x - jnp.mean(x, -1, keepdims=True)
    scale = lax.rsqrt(jnp.mean(centre * centre, -1, keepdims=True) + 1e-05)
    return centre * scale, scale


def solution(mesh):
    rows = P(None, ("dp", "tp"), None)
    in_specs = (
        rows, rows, P(None, "dp", None), P(None, "dp", None),
        P(), P(), P(), P(),
        P(None, "tp"), P("tp"), P(), P(), P("tp", None),
        P(None, "tp"), P("tp"), P("tp", None), P(),
    )
    out_specs = (
        rows, rows,
        P(None, "tp"), P("tp"), P(), P(), P("tp", None),
        P(None, "tp"), P("tp"), P("tp", None),
        P(), P(), P(), P(), P(),
    )
    return jax.shard_map(
        functools.partial(on_device, mesh.shape["dp"]),
        mesh=mesh,
        in_specs=in_specs,
        out_specs=out_specs,
        check_vma=False,
    )
```

```python
import functools

import jax
import jax.numpy as jnp
from jax import lax
from jax.experimental import pallas as pl
from jax.experimental.pallas import tpu as pltpu
from jax.sharding import PartitionSpec as P

ROT = 16
LANES = 128
QW = 256
PART = 72
LINES = ((0, 0), (1, 0), (2, 0), (8, 0), (9, 0), (10, 0), (11, 0), (12, QW))
BF = jnp.bfloat16
F32 = jnp.float32
ACROSS = (1, 2, 4)
ALONG = (2, 4, 1)
EXPAND = ALONG
BACK = ALONG
NT = (((1,), (1,)), ((), ()))
TN = (((0,), (0,)), ((), ()))
ANY = pl.BlockSpec(memory_space=pl.ANY)
VMEM = pl.BlockSpec(memory_space=pltpu.VMEM)
SMEM = pl.BlockSpec(memory_space=pltpu.SMEM)


def dot(a, b):
    return jnp.dot(a, b, preferred_element_type=F32)


def dot_nt(a, b):
    return lax.dot_general(a, b, NT, preferred_element_type=F32)


def dot_tn(a, b):
    return lax.dot_general(a, b, TN, preferred_element_type=F32)


def shape(dims, dtype=BF):
    return jax.ShapeDtypeStruct(dims, dtype)


def call(kernel, name, ins, outs, scratch, copies, flops=10**10):
    specs = [s for _, s in ins]
    arrays = [a for a, _ in ins]
    return pl.pallas_call(
        kernel,
        in_specs=specs,
        out_specs=[s for _, s in outs],
        out_shape=[o for o, _ in outs],
        scratch_shapes=list(scratch) + [pltpu.SemaphoreType.DMA((copies,))],
        compiler_params=pltpu.CompilerParams(vmem_limit_bytes=64 * 2**20 - 65536),
        cost_estimate=pl.CostEstimate(flops=flops, bytes_accessed=0, transcendentals=0),
        name=name,
    )(*arrays)


def offsets(bits):
    keep = (0, bits[2], bits[1], bits[1] | bits[2])
    return keep, tuple(k ^ bits[0] for k in keep)


class Copies:
    def __init__(self, sems):
        self.sems = sems
        self.count = 0

    def start(self, src, dst):
        copy = pltpu.make_async_copy(src, dst, self.sems.at[self.count])
        self.count += 1
        copy.start()
        return copy


def normalize(x):
    centre = x - jnp.mean(x, -1, keepdims=True)
    spread = jnp.mean(centre * centre, -1, keepdims=True)
    return centre * lax.rsqrt(spread + 1e-05)


def line(ref):
    return ref[...].reshape(1, -1)


def swap_halves(w):
    lane = lax.broadcasted_iota(jnp.int32, w.shape, 1)
    up = pltpu.roll(w, w.shape[1] - ROT // 2, 1)
    down = pltpu.roll(w, ROT // 2, 1)
    return jnp.where((lane % 64) < ROT // 2, up, down)


def spread_table(compact, filler, signs):
    fill = jnp.full((64 - ROT, compact.shape[1]), filler, F32)
    head = [signs * compact, compact, fill]
    return jnp.concatenate(head + head, 0).T


def hidden_kernel(
    pa, pb, gain1, bias1, gain2, bias2, we, be, acto, slopeo, h1o, h2o, no, xs, wev, acts, slopes, h1s, h2s, ns, sems
):
    copies = Copies(sems)
    got = [copies.start(pa, xs.at[0])]
    gotw = copies.start(we, wev)
    got.append(copies.start(pb, xs.at[1]))
    out = []
    for j in range(2):
        got[j].wait()
        for m in range(2):
            n = normalize(xs[j, m].astype(F32))
            ns[m, j] = n.astype(BF)
            h1s[m, j] = (n * line(gain1) + line(bias1)).astype(BF)
            h2 = (n * line(gain2) + line(bias2)).astype(BF)
            h2s[m, j] = h2
            for a, b in ((ns, no), (h1s, h1o), (h2s, h2o)):
                out.append(copies.start(a.at[m, j], b.at[m, j]))
            if j == 0 and m == 0:
                gotw.wait()
            u = dot(h2, wev[...]) + line(be)
            phi = 0.5 * (1.0 + lax.erf(u * 0.7071067811865476))
            acts[m, j] = (u * phi).astype(BF)
            slopes[m, j] = (phi + u * jnp.exp(-0.5 * u * u) * 0.3989422804014327).astype(BF)
            for a, b in ((acts, acto), (slopes, slopeo)):
                out.append(copies.start(a.at[m, j], b.at[m, j]))
    for c in out:
        c.wait()


def hidden(pieces, norms, we, be):
    _, rows, feat = pieces[0].shape
    ff = we.shape[1]
    wide, narrow = (2, 2, rows, ff), (2, 2, rows, feat)
    return call(
        hidden_kernel,
        "hidden",
        [(x, ANY) for x in pieces] + [(a, VMEM) for a in norms] + [(we, ANY), (be, VMEM)],
        [(shape(wide), ANY)] * 2 + [(shape(narrow), ANY)] * 3,
        [pltpu.VMEM(narrow, BF), pltpu.VMEM(we.shape, BF)]
        + [pltpu.VMEM(wide, BF)] * 2
        + [pltpu.VMEM(narrow, BF)] * 3,
        23,
        0,
    )


def doubled(kv):
    kv = kv.astype(F32)
    swapped = pltpu.roll(kv, 64, 1)
    low = lax.broadcasted_iota(jnp.int32, kv.shape, 1) < 64
    return jnp.where(low, kv, swapped).astype(BF), jnp.where(low, swapped, kv).astype(BF)


def stack_heads(block, heads):
    low = lax.broadcasted_iota(jnp.int32, (block.shape[0], LANES), 1) < 64
    zero = jnp.zeros((block.shape[0], LANES), block.dtype)
    parts = []
    for h in range(heads):
        part = block[:, LANES * (h // 2) : LANES * (h // 2 + 1)]
        parts.append(jnp.where(low, part, zero) if h % 2 == 0 else jnp.where(low, zero, part))
    return jnp.concatenate(parts, 0)


def join_heads(stacked, heads, rows):
    low = lax.broadcasted_iota(jnp.int32, (rows, LANES), 1) < 64
    part = lambda h: stacked[h * rows : (h + 1) * rows]
    zero = jnp.zeros((rows, LANES), stacked.dtype)
    cols = []
    for h in range(0, heads, 2):
        cols.append(jnp.where(low, part(h), part(h + 1) if h + 1 < heads else zero))
    return jnp.concatenate(cols, 1)


def send_rows(copies, rows, mine, send, which):
    places = (mine[0].at[which], send.at[0, which], mine[1].at[which], send.at[1, which])
    return [copies.start(rows.at[r], place) for r, place in enumerate(places)]


def halves_to(copies, halves, micro_id, into, t):
    return [
        copies.start(halves[r // 2].at[micro_id, r % 2], into.at[r ^ t]) for r in range(4)
    ]


def join_weights(wss, wts):
    wts[QW:] = wss[...].T


def project(micro_id, h1s, wts, qbias, sbias, bqkv, cs, sn, saved):
    qrs, kk, vv = saved[:3]
    rows = h1s.shape[1]
    own_q = qbias.shape[0]
    bqkv[:, :own_q] = line(qbias)
    bqkv[:, own_q:QW] = jnp.zeros((1, QW - own_q), F32)
    bqkv[:, QW:] = line(sbias)
    for a in range(4):
        here = slice(a * rows, (a + 1) * rows)
        qkv = dot_nt(h1s[a], wts[...]) + bqkv[...]
        c = spread_table(cs[micro_id, a], 1.0, 1.0)
        s = spread_table(sn[micro_id, a], 0.0, -1.0)
        low = lax.broadcasted_iota(jnp.int32, c.shape, 1) < 64
        cos = jnp.concatenate([c, c, jnp.where(low, c, 1.0)], 1)
        sin = jnp.concatenate([s, s, jnp.where(low, s, 0.0)], 1)
        qkv = qkv * cos + swap_halves(qkv) * sin
        qrs[a] = (qkv[:, :QW] * 0.125).astype(BF)
        kk[here], vv[here] = doubled(qkv[:, QW:].astype(BF))


def attend_rows(micro_id, heads, ends, saved, finished=lambda block: None):
    qrs, kk, vv, cx, *probs_of = saved
    rows = qrs.shape[1]
    spans = [(a + 1) * rows for a in range(4)]
    scores = dot_nt(stack_heads(qrs[3], heads), kk[: spans[3]])
    for a in (3, 2, 1, 0):
        here = scores
        if a > 0:
            scores = dot_nt(stack_heads(qrs[a - 1], heads), kk[: spans[a - 1]])
        row = lax.broadcasted_iota(jnp.int32, (rows, 1), 0) + a * rows
        begin = jnp.zeros((rows, 1), jnp.int32)
        for d in range(ends.shape[2] - 1):
            begin = jnp.where(row >= ends[micro_id, 0, d], ends[micro_id, 0, d], begin)
        col = lax.broadcasted_iota(jnp.int32, (rows, spans[a]), 1)
        allowed = (col >= begin) & (col <= row)
        for h in range(heads):
            mine = slice(h * rows, (h + 1) * rows)
            s = jnp.where(allowed, here[mine], -1e30)
            e = jnp.exp(s - jnp.max(s, -1, keepdims=True))
            probs_of[a][mine] = (e * (1.0 / jnp.sum(e, -1, keepdims=True))).astype(BF)
        done = a + 1
        if done < 4:
            cx[done] = join_heads(dot(probs_of[done][...], vv[: spans[done]]), heads, rows).astype(BF)
            finished(done)
    cx[0] = join_heads(dot(probs_of[0][...], vv[: spans[0]]), heads, rows).astype(BF)


def attend_kernel(micro_id, heads, *refs):
    refs = list(refs)
    take = lambda k: [refs.pop(0) for _ in range(k)]
    t_ref, ends = take(2)
    h1 = take(2)
    wq, ws, qbias, sbias, cs, sn = take(6)
    outs = take(8)
    h1s, wss, wts, bqkv = take(4)
    saved = take(8)
    copies = Copies(take(1)[0])
    got = load_weights(copies, wq, ws, wss, wts)
    got += halves_to(copies, h1, micro_id, h1s, t_ref[0])
    for c in got:
        c.wait()
    join_weights(wss, wts)
    project(micro_id, h1s, wts, qbias, sbias, bqkv, cs, sn, saved)
    sent = [copies.start(saved[i], outs[i]) for i in range(3)]

    def finished(block):
        sent.append(copies.start(saved[4 + block], outs[4 + block]))

    attend_rows(micro_id, heads, ends, saved, finished)
    finished(0)
    sent.append(copies.start(saved[3], outs[3]))
    for c in sent:
        c.wait()


def load_weights(copies, wq, ws, wss, wts):
    own_q = wq.shape[0]
    wts[own_q:QW] = jnp.zeros((QW - own_q, wts.shape[1]), BF)
    return [copies.start(wq, wts.at[pl.ds(0, own_q)]), copies.start(ws, wss)]


def weights_scratch(ws):
    width = QW + LANES
    return [
        pltpu.VMEM(ws.shape, BF), pltpu.VMEM((width, ws.shape[0]), BF), pltpu.VMEM((1, width), F32)
    ]


def saved_shapes(rows, heads):
    length = 4 * rows
    saved = [(4, rows, QW), (length, LANES), (length, LANES), (4, rows, QW)]
    return saved + [(heads * rows, (a + 1) * rows) for a in range(4)]


def attend(micro_id, rank, ends, h1, wq, ws, qbias, sbias, cs, sn, heads, flops):
    _, _, rows, feat = h1[0].shape
    ins = [(rank, SMEM), (ends, SMEM)] + [(a, ANY) for a in (*h1, wq, ws)]
    ins += [(a, VMEM) for a in (qbias, sbias, cs, sn)]
    saved = saved_shapes(rows, heads)
    scratch = [pltpu.VMEM((4, rows, feat), BF)] + weights_scratch(ws)
    return call(
        functools.partial(attend_kernel, micro_id, heads), "attend", ins,
        [(shape(a), ANY) for a in saved], scratch + [pltpu.VMEM(a, BF) for a in saved], 14, flops,
    )


def attend_back_kernel(micro_id, heads, first, whole, *refs):
    refs = list(refs)
    take = lambda k: [refs.pop(0) for _ in range(k)]
    t_ref, me_ref = take(2)
    if whole:
        ends, qbias, sbias = take(3)
    else:
        saved = take(8)
    gpieces = take(4)
    h1, act, du, n = take(2), take(2), take(2), take(2)
    wq, ws, wo, wc, we, gain1, gain2, cs, sn = take(9)
    if not first:
        og_in, qs_in, vec_in, hid_in = take(4)
    rows_kept = take(2)
    rows_sent, = take(1)
    results = take(3 if first else 2)
    gs, h1s, acts, dus, ns, wss, wts, bqkv, wos, wcs, wes = take(11)
    qrs, kk, vv, cx, *probs_of = kept = take(8)
    dctx, = take(1)
    dss = take(2)
    dk, dv, dqkv, outb, eb, ogs, qss = take(7)
    if not first:
        lines, keeps, sends = take(3)
    copies = Copies(take(1)[0])
    rows = gs.shape[1]
    t = t_ref[0]
    spans = [(a + 1) * rows for a in range(4)]
    def load_h():
        return load_weights(copies, wq, ws, wss, wts) + halves_to(copies, h1, micro_id, h1s, t)

    if whole:
        got_h = load_h()
    own_q = wo.shape[0]
    got_g = [copies.start(wo, wos.at[pl.ds(0, own_q)])]
    wos[own_q:] = jnp.zeros((QW - own_q, wo.shape[1]), BF)
    got_g += [copies.start(g.at[micro_id], gs.at[r ^ t]) for r, g in enumerate(gpieces)]
    order = (2, 7, 0, 1, 6, 5, 4, 3)
    got_saved = [] if whole else [copies.start(saved[i], kept[i]) for i in order]
    got_out = halves_to(copies, act, micro_id, acts, 0) + [copies.start(wc, wcs)]
    if not whole:
        got_h = load_h()
    got_e = halves_to(copies, du, micro_id, dus, 0) + [copies.start(we, wes)]
    got_e += halves_to(copies, n, micro_id, ns, 0)
    if not first:
        got_e += [copies.start(og_in, ogs), copies.start(qs_in, qss)]
    if whole:
        for c in got_h:
            c.wait()
        join_weights(wss, wts)
        project(micro_id, h1s, wts, qbias, sbias, bqkv, cs, sn, kept)
        attend_rows(micro_id, heads, ends, kept)
    for c in got_g + (got_out + got_e if whole else []):
        c.wait()
    dctx[...] = dot_nt(gs[...].reshape(4 * rows, gs.shape[2]), wos[...]).astype(BF)
    for c in got_saved:
        c.wait()
    dk[...] = jnp.zeros_like(dk)
    dv[...] = jnp.zeros_like(dv)
    stacked = lambda a: stack_heads(dctx[a * rows : (a + 1) * rows], heads)

    def finish(a):
        dscores = dss[a % 2][:, : spans[a]]
        dk[: spans[a]] += dot_tn(dscores, stack_heads(qrs[a], heads))
        dv[: spans[a]] += dot_tn(probs_of[a][...], stacked(a))
        dq = join_heads(dot(dscores, kk[: spans[a]]), heads, rows) * 0.125
        c = spread_table(cs[micro_id, a], 1.0, 1.0)
        s = spread_table(sn[micro_id, a], 0.0, -1.0)
        cos = jnp.concatenate([c, c], 1)
        sin = jnp.concatenate([s, s], 1)
        dqkv[a, :, :QW] = (dq * cos - swap_halves(dq) * sin).astype(BF)

    dprobs = dot_nt(stacked(3), vv[: spans[3]])
    for a in (3, 2, 1, 0):
        here = dprobs
        if a > 0:
            dprobs = dot_nt(stacked(a - 1), vv[: spans[a - 1]])
        for h in range(heads):
            mine = slice(h * rows, (h + 1) * rows)
            p = probs_of[a][mine].astype(F32)
            weighted = p * here[mine]
            delta = jnp.sum(weighted, -1, keepdims=True)
            dss[a % 2][mine, : spans[a]] = (weighted - p * delta).astype(BF)
        if a < 3:
            finish(a + 1)
    finish(0)
    for a in range(4):
        here = slice(a * rows, (a + 1) * rows)
        c = spread_table(cs[micro_id, a], 1.0, 1.0)
        s = spread_table(sn[micro_id, a], 0.0, -1.0)
        dkf = dk[here] + pltpu.roll(dk[here], 64, 1)
        dvf = dv[here] + pltpu.roll(dv[here], 64, 1)
        dkf = dkf * c - swap_halves(dkf) * s
        low = lax.broadcasted_iota(jnp.int32, dkf.shape, 1) < 64
        dqkv[a, :, QW:] = jnp.where(low, dkf, dvf).astype(BF)
    for c in [] if whole else got_out:
        c.wait()
    for r in range(4):
        outb[r] = (dot(cx[r ^ t], wos[...]) + dot(acts[r], wcs[...])).astype(BF)
    sent = send_rows(copies, outb, rows_kept, rows_sent, 0)

    for c in [] if whole else got_e + got_h:
        c.wait()
    if not whole:
        join_weights(wss, wts)
    width = QW + LANES
    vec_width = gs.shape[2]
    flat = dqkv[...].reshape(4 * rows, width)
    ograd = dot_tn(cx[...].reshape(4 * rows, QW), gs[...].reshape(4 * rows, gs.shape[2]))
    qgrad = dot_tn(flat, h1s[...].reshape(4 * rows, h1s.shape[2]))
    ogs[...] = ograd if first else ogs[...] + ograd
    qss[...] = qgrad if first else qss[...] + qgrad
    if first:
        sent += [copies.start(ogs, results[0]), copies.start(qss, results[1])]
    sums = [jnp.zeros((1, vec_width), F32) for _ in range(4)]
    for r in range(4):
        e1 = dot(dqkv[r ^ t], wts[...])
        e2 = dot_nt(dus[r], wes[...])
        eb[r] = (e1 * line(gain1) + e2 * line(gain2)).astype(BF)
        norm = ns[r].astype(F32)
        for i, term in enumerate((e1 * norm, e1, e2 * norm, e2)):
            sums[i] += jnp.sum(term, 0, keepdims=True)
    sent += send_rows(copies, eb, rows_kept, rows_sent, 1)
    column = jnp.sum(flat.astype(F32), 0, keepdims=True)
    sums.append(jnp.concatenate([column, jnp.zeros((1, vec_width - width), F32)], 1))
    if first:
        results[2][...] = jnp.concatenate(sums + [jnp.zeros((3, vec_width), F32)], 0)
    else:
        sums = [a + vec_in[i : i + 1] for i, a in enumerate(sums)]
        zero = jnp.zeros((5, vec_width), F32)
        lines[...] = jnp.concatenate(
            [hid_in[0:1], hid_in[1:2], sums[4], zero] + sums + [zero[:3]], 0
        )
        pack_parts(ogs, qss, lines, keeps, sends, me_ref[0], heads * 8)
        sent += [copies.start(keeps, results[0]), copies.start(sends, results[1])]
    for c in sent:
        c.wait()


def pack_parts(og, qs, lines, keep, send, me, cut):
    tall = LANES // 8
    for out, order in zip((keep, send), offsets(ACROSS)):
        for i in range(4):
            b = order[i] ^ me
            rows = lambda ref, size, base: ref[pl.ds(pl.multiple_of(b * size + base, 8), size)]
            line = lambda i: jnp.broadcast_to(lines[pl.ds(b + i, 1)], (8, lines.shape[1]))
            own = lax.broadcasted_iota(jnp.int32, (8, lines.shape[1]), 0) < 4
            both = jnp.where(own, line(0), line(8))
            part = [rows(og, cut, 0), rows(qs, cut, 0), rows(qs, tall, QW), both]
            out[i] = jnp.concatenate(part, 0).astype(BF)


def attend_back(
    micro_id, rank, me, saved, gs, h1, act, du, n, wq, ws, wo, wc, we, gain1, gain2, cs, sn, heads,
    whole=False, before=None,
):
    _, rows, feat = gs[0].shape
    ff = wc.shape[0]
    width = QW + LANES
    length = 4 * rows
    first = before is None
    ins = [(rank, SMEM), (me, SMEM)]
    ins += [(saved[0], SMEM)] + [(a, VMEM) for a in saved[1:]] if whole else [(a, ANY) for a in saved]
    ins += [(a, ANY) for a in (*gs, *h1, *act, *du, *n, wq, ws, wo, wc, we)]
    ins += [(a, VMEM) for a in (gain1, gain2, cs, sn)]
    if not first:
        ins += [(a, ANY) for a in before[:2]] + [(a, VMEM) for a in before[2:]]
    outs = [(shape((2, rows, feat)), ANY)] * 2 + [(shape((2, 2, rows, feat)), ANY)]
    grads = [shape((QW, feat), F32), shape((width, feat), F32)]
    part = shape((4, PART, feat))
    if first:
        outs += [(g, ANY) for g in grads] + [(shape((8, feat), F32), VMEM)]
    else:
        outs += [(part, ANY)] * 2
    stack, wide = pltpu.VMEM((4, rows, feat), BF), pltpu.VMEM((4, rows, ff), BF)
    scratch = [stack, stack, wide, wide, stack]
    scratch += weights_scratch(ws)
    scratch += [pltpu.VMEM(a, BF) for a in ((QW, feat), wc.shape, we.shape)]
    scratch += [pltpu.VMEM(a, BF) for a in saved_shapes(rows, heads)]
    scratch += [
        pltpu.VMEM((length, QW), BF),
        pltpu.VMEM((heads * rows, length), BF), pltpu.VMEM((heads * rows, length), BF),
        pltpu.VMEM((length, LANES), F32), pltpu.VMEM((length, LANES), F32),
        pltpu.VMEM((4, rows, width), BF), stack, stack,
    ]
    scratch += [pltpu.VMEM(g.shape, F32) for g in grads]
    if not first:
        scratch += [pltpu.VMEM((16, feat), F32)] + [pltpu.VMEM(part.shape, BF)] * 2
    return call(
        functools.partial(attend_back_kernel, micro_id, heads, first, whole), "attend_grad", ins, outs,
        scratch, 46,
    )


def store_parts(total, parts, me, bits):
    part = total.shape[0] // 8
    for b in range(8):
        offset = b ^ me
        place = sum(((offset // bit) % 2) * weight for bit, weight in zip(bits, (4, 2, 1)))
        parts[place] = total[b * part : (b + 1) * part].astype(BF)


def pieces_to(copies, pieces, into):
    return [copies.start(p.at[m], into.at[m, j]) for j, p in enumerate(pieces) for m in range(2)]


def flat(ref):
    return ref[...].reshape(-1, ref.shape[-1])


def hidden_back_kernel(first, *refs):
    refs = list(refs)
    take = lambda k: [refs.pop(0) for _ in range(k)]
    me_ref, = take(1)
    pieces = take(2)
    act, slope, h2, wc = take(4)
    if not first:
        before = take(2)
        sums_in, = take(1)
    duo, = take(1)
    outs = take(2 if first else 4)
    sums, = take(1)
    gs, acts, slopes, wcs, h2s, dus, *accs = take(8)
    parts = None if first else take(2)
    copies = Copies(take(1)[0])
    got = pieces_to(copies, pieces, gs) + [copies.start(act, acts)]
    if not first:
        got_sums = [copies.start(before[0], accs[0])]
    got_back = [copies.start(wc, wcs), copies.start(slope, slopes)]
    got_late = [copies.start(h2, h2s)]
    if not first:
        got_sums.append(copies.start(before[1], accs[1]))

    def total(i, left, right):
        if first:
            accs[i][...] = dot_tn(flat(left), flat(right))
            return [copies.start(accs[i], outs[i])]
        got_sums[i].wait()
        both = accs[i][...] + dot_tn(flat(left), flat(right))
        store_parts(both, parts[i], me_ref[0], (ACROSS, EXPAND)[i])
        return [copies.start(parts[i].at[pl.ds(4 * k, 4)], outs[2 * i + k]) for k in (0, 1)]

    for c in got:
        c.wait()
    sent = total(0, acts, gs)
    for c in got_back:
        c.wait()
    gsum = jnp.zeros((1, gs.shape[3]), F32)
    column = jnp.zeros((1, slopes.shape[3]), F32)
    for m in range(2):
        for j in range(2):
            g = gs[m, j]
            du = (dot_nt(g, wcs[...]) * slopes[m, j].astype(F32)).astype(BF)
            dus[m, j] = du
            gsum += jnp.sum(g.astype(F32), 0, keepdims=True)
            column += jnp.sum(du.astype(F32), 0, keepdims=True)
    sent.append(copies.start(dus, duo))
    for c in got_late:
        c.wait()
    sent += total(1, h2s, dus)
    rowid = lax.broadcasted_iota(jnp.int32, sums.shape, 0)
    both = jnp.where(rowid == 0, gsum, jnp.where(rowid == 1, column, 0.0))
    sums[...] = both if first else sums_in[...] + both
    for c in sent:
        c.wait()


def hidden_back(me, pieces, act, slope, h2, wc, before=None):
    _, _, rows, feat = h2.shape
    ff = wc.shape[0]
    first = before is None
    ins = [(me, SMEM)] + [(a, ANY) for a in (*pieces, act, slope, h2, wc)]
    outs = [(shape(slope.shape), ANY)]
    if first:
        outs += [(shape((ff, feat), F32), ANY), (shape((feat, ff), F32), ANY)]
    else:
        ins += [(before[0], ANY), (before[1], ANY), (before[2], VMEM)]
        outs += [(shape((4, ff // 8, feat)), ANY)] * 2 + [(shape((4, feat // 8, ff)), ANY)] * 2
    outs.append((shape((8, feat), F32), VMEM))
    scratch = [
        pltpu.VMEM(h2.shape, BF), pltpu.VMEM(act.shape, BF), pltpu.VMEM(slope.shape, BF),
        pltpu.VMEM(wc.shape, BF), pltpu.VMEM(h2.shape, BF), pltpu.VMEM(slope.shape, BF),
        pltpu.VMEM((ff, feat), F32), pltpu.VMEM((feat, ff), F32),
    ]
    if not first:
        scratch += [pltpu.VMEM((8, ff // 8, feat), BF), pltpu.VMEM((8, feat // 8, ff), BF)]
    return call(
        functools.partial(hidden_back_kernel, first), "hidden_grad", ins, outs, scratch, 15,
        0 if first else 10**10,
    )


def after(value, *others):
    return lax.optimization_barrier((value, others))[0]


def add(*terms):
    return sum(a.astype(F32) for a in terms).astype(BF)


def swap(value, axis, size, bit):
    return lax.ppermute(value, axis, [(i, i ^ bit) for i in range(size)])


class Order:
    def __init__(self):
        self.last = None

    def __call__(self, value):
        if self.last is not None:
            value = after(value, self.last)
        return value

    def step(self, result):
        self.last = result
        return result


class Sum:
    def __init__(self, order, size, keep, send, bits, back):
        self.order, self.size, self.bits, self.back = order, size, bits, back
        self.have = keep
        self.flying = swap(order(send), "dp", size, bits[0])

    def kept(self):
        have = self.order(self.have)
        halves = add(have[:2], self.flying[:2]), add(have[2:], self.flying[2:])
        self.have, send = self.order.step(halves)
        self.flying = swap(send, "dp", self.size, self.bits[1])

    def near(self):
        have = self.order(self.have)
        halves = add(have[0], self.flying[0]), add(have[1], self.flying[1])
        self.have, send = self.order.step(halves)
        self.flying = swap(send, "dp", self.size, self.bits[2])

    def own(self, over_tp=0):
        self.have = self.order.step(add(self.order(self.have), self.flying))
        if self.size > 8:
            groups = [[low + 8 * high for high in range(self.size // 8)] for low in range(8)]
            whole = lax.psum(self.have.astype(F32), "dp", axis_index_groups=groups)
            self.have = whole.astype(BF)
        if over_tp:
            self.tail = self.have[over_tp:]
            self.sums = [swap(self.tail, "tp", 4, bit) for bit in (1, 2, 3)]
        else:
            self.flying = swap(self.have, "dp", self.size, self.back[2])

    def over_tp(self, first):
        tail = self.order(self.tail)
        row = lax.broadcasted_iota(jnp.int32, tail.shape, 0) - LANES // 8
        whole = jnp.where((row >= 0) & (row < 4), tail, add(tail, *self.sums))
        self.have = self.order.step(jnp.concatenate([self.have[:first], whole], 0))
        self.flying = swap(self.have, "dp", self.size, self.back[2])

    def pair(self):
        self.have = self.order.step(jnp.stack([self.order(self.have), self.flying]))
        self.flying = swap(self.have, "dp", self.size, self.back[1])

    def four(self):
        self.have = self.order.step(jnp.concatenate([self.order(self.have), self.flying], 0))
        self.flying = swap(self.have, "dp", self.size, self.back[0])

    def parts(self):
        return self.have, self.flying


def halve_kernel(*refs):
    values, outs, held, sums, sems = refs[:4], refs[4:8], refs[8:12], refs[12:14], refs[14]
    copies = Copies(sems)
    got = [copies.start(a, b) for a, b in zip(values, held)]
    sent = []
    for i in range(2):
        got[2 * i].wait()
        got[2 * i + 1].wait()
        sums[i][...] = (held[2 * i][...].astype(F32) + held[2 * i + 1][...].astype(F32)).astype(BF)
        for k in range(2):
            sent.append(copies.start(sums[i].at[pl.ds(2 * k, 2)], outs[2 * i + k]))
    for c in sent:
        c.wait()


def kept_both(order, first, second):
    values = order((first.have, first.flying, second.have, second.flying))
    outs = [shape((2, *a.shape[1:])) for a in values]
    scratch = [pltpu.VMEM(a.shape, BF) for a in values]
    halves = call(
        halve_kernel, "halve", [(a, ANY) for a in values], [(o, ANY) for o in outs],
        scratch + [scratch[0], scratch[2]], 8, 0,
    )
    order.step(halves)
    for one, (stay, leave) in ((first, halves[:2]), (second, halves[2:])):
        one.have = stay
        one.flying = swap(leave, "dp", one.size, one.bits[1])


class Rows:
    def __init__(self, order, mine, send):
        self.order, self.mine = order, mine
        self.got = swap(order(send), "tp", 4, 1)

    def away(self):
        away = self.order.step(add(self.order(self.mine[1]), self.got[1]))
        self.far = swap(away, "tp", 4, 2)

    def land(self):
        terms = self.order(self.mine[0]), self.got[0], self.far
        self.total = self.order.step(sum(a.astype(F32) for a in terms))


def place_kernel(me_ref, four, other, out):
    i = pl.program_id(0)

    @pl.when(i < 4)
    def _():
        out[...] = four[0].astype(F32)

    @pl.when(i >= 4)
    def _():
        out[...] = other[0].astype(F32)


def place(me, four, other, bits):
    _, part, width = four.shape

    def where(i, me):
        j = i % 4
        order = (j // 2) * bits[1] + (j % 2) * bits[2] + (i // 4) * bits[0]
        return order ^ me[0], 0

    return pl.pallas_call(
        place_kernel,
        grid_spec=pltpu.PrefetchScalarGridSpec(
            num_scalar_prefetch=1,
            grid=(8,),
            in_specs=[
                pl.BlockSpec((1, part, width), lambda i, me: (jnp.minimum(i, 3), 0, 0)),
                pl.BlockSpec((1, part, width), lambda i, me: (jnp.maximum(i - 4, 0), 0, 0)),
            ],
            out_specs=pl.BlockSpec((part, width), where),
        ),
        out_shape=shape((8 * part, width), F32),
        compiler_params=pltpu.CompilerParams(vmem_limit_bytes=32 * 2**20),
        cost_estimate=pl.CostEstimate(flops=0, bytes_accessed=0, transcendentals=0),
        name="place_parts",
    )(me, four, other)


def unpack_kernel(own_q, me_ref, four, other, og, qs, sg, *refs):
    *vectors, shared, lines = refs
    me = me_ref[0]
    cut = own_q // 8
    tall = LANES // 8
    for ref, order in zip((four, other), offsets(ACROSS)):
        for i in range(4):
            b = order[i] ^ me
            part = ref[i].astype(F32)
            rows = lambda size: pl.ds(pl.multiple_of(b * size, 8), size)
            og[rows(cut)] = part[:cut]
            qs[rows(cut)] = part[cut : 2 * cut]
            shared[rows(tall)] = part[2 * cut : 2 * cut + tall]
            last = part[2 * cut + tall :]
            lines[pl.ds(b, 1)] = last[:1]
            lines[pl.ds(b + 8, 1)] = last[4:5]
    sg[...] = shared[...].T
    for ref, (i, base) in zip(vectors, LINES):
        ref[...] = lines[i, base : base + ref.shape[0]]


def unpack(me, four, other, own_q, ff):
    feat = four.shape[2]
    sizes = (feat, ff, own_q, feat, feat, feat, feat, LANES)
    outs = [(own_q, feat), (own_q, feat), (feat, LANES)] + [(n,) for n in sizes]
    return pl.pallas_call(
        functools.partial(unpack_kernel, own_q),
        in_specs=[SMEM, VMEM, VMEM],
        out_specs=[VMEM] * len(outs),
        out_shape=[shape(a, F32) for a in outs],
        scratch_shapes=[pltpu.VMEM((LANES, feat), F32), pltpu.VMEM((16, feat), F32)],
        compiler_params=pltpu.CompilerParams(vmem_limit_bytes=32 * 2**20),
        cost_estimate=pl.CostEstimate(flops=0, bytes_accessed=0, transcendentals=0),
        name="unpack",
    )(me, four, other)


def doc_layout(ends, scales, length):
    row = jnp.arange(length, dtype=jnp.int32)[None]
    begin = jnp.zeros_like(row)
    step = scales[:, :1]
    for d in range(ends.shape[1] - 1):
        past = row >= ends[:, d : d + 1]
        begin = jnp.where(past, ends[:, d : d + 1], begin)
        step = jnp.where(past, scales[:, d + 1 : d + 2], step)
    return (row - begin) * step


def angle_tables(placed, rows):
    freqs = 10000.0 ** (-jnp.arange(ROT // 2, dtype=F32) * 2.0 / ROT)
    blocks = placed.astype(F32).reshape(placed.shape[0], 4, 1, rows)
    angles = blocks * freqs[:, None]
    return jnp.cos(angles), jnp.sin(angles)


def on_device(
    size,
    tokens,
    cotangent,
    doc_ends,
    pos_scale,
    first_gain,
    first_bias,
    second_gain,
    second_bias,
    w_query,
    query_bias,
    w_shared,
    shared_bias,
    w_output,
    w_expand,
    expand_bias,
    w_contract,
    output_bias,
):
    micro, rows, feat = tokens.shape
    heads = w_query.shape[1] // 64
    own_q = w_query.shape[1]
    length = rows * 4
    rank = lax.axis_index("tp").astype(jnp.int32)[None]
    me = (lax.axis_index("dp").astype(jnp.int32) & 7)[None]

    order = Order()

    def begin(values):
        return values, swap(values, "tp", 4, 1), swap(values, "tp", 4, 2)

    def finish(own, near, far):
        return own, near, far, swap(far, "tp", 4, 1)

    xs, gs = begin(tokens), begin(cotangent)

    norms = (first_gain, first_bias, second_gain, second_bias)
    ends, scales = doc_ends[:, 0], pos_scale[:, 0]
    cs, sn = angle_tables(doc_layout(ends, scales, length), rows)

    act_a, slope_a, h1_a, h2_a, n_a = hidden(xs[:2], norms, w_expand, expand_bias)
    order.step(act_a)
    du_a, cacc, eacc, sums = hidden_back(order(me), gs[:2], act_a, slope_a, h2_a, w_contract)
    order.step(sums)
    xs = finish(xs[0], xs[1], order(xs[2]))
    act_b, slope_b, h1_b, h2_b, n_b = hidden(xs[2:], norms, w_expand, expand_bias)
    order.step(act_b)
    h1, n, act = (h1_a, h1_b), (n_a, n_b), (act_a, act_b)
    biases = (query_bias, shared_bias)
    saved0 = attend(
        0, order(rank), doc_ends, h1, w_query.T, w_shared, *biases, cs, sn, heads, 0
    )
    order.step(saved0[0])
    gs = finish(gs[0], gs[1], order(gs[2]))
    du_b, c_keep, c_send, e_keep, e_send, sums = hidden_back(
        order(me), gs[2:], act_b, slope_b, h2_b, w_contract, (cacc, eacc, sums)
    )
    order.step(sums)
    weights = (w_query.T, w_shared, w_output, w_contract, w_expand, first_gain, second_gain)
    inputs = (gs, h1, act, (du_a, du_b), n, *weights, cs, sn, heads)
    weights = (w_query.T, w_shared, w_output, w_contract, w_expand, first_gain, second_gain)
    inputs = (gs, h1, act, (du_a, du_b), n, *weights, cs, sn, heads)
    weights = (w_query.T, w_shared, w_output, w_contract, w_expand, first_gain, second_gain)
    inputs = (gs, h1, act, (du_a, du_b), n, *weights, cs, sn, heads)
    weights = (w_query.T, w_shared, w_output, w_contract, w_expand, first_gain, second_gain)
    inputs = (gs, h1, act, (du_a, du_b), n, *weights, cs, sn, heads)
    weights = (w_query.T, w_shared, w_output, w_contract, w_expand, first_gain, second_gain)
    inputs = (gs, h1, act, (du_a, du_b), n, *weights, cs, sn, heads)
    weights = (w_query.T, w_shared, w_output, w_contract, w_expand, first_gain, second_gain)
    inputs = (gs, h1, act, (du_a, du_b), n, *weights, cs, sn, heads)
    weights = (w_query.T, w_shared, w_output, w_contract, w_expand, first_gain, second_gain)
    inputs = (gs, h1, act, (du_a, du_b), n, *weights, cs, sn, heads)
    weights = (w_query.T, w_shared, w_output, w_contract, w_expand, first_gain, second_gain)
    inputs = (gs, h1, act, (du_a, du_b), n, *weights, cs, sn, heads)
    c = Sum(order, size, c_keep, c_send, ACROSS, ACROSS)
    e = Sum(order, size, e_keep, e_send, EXPAND, BACK)
    *mine0, send0, og, qs, vec = attend_back(0, order(rank), me, saved0, *inputs)
    order.step(vec)
    kept_both(order, c, e)
    rows0 = Rows(order, mine0, send0)
    *mine1, send1, r_keep, r_send = attend_back(
        1, order(rank), me, (doc_ends, *biases), *inputs, True, (og, qs, vec, sums)
    )
    order.step(r_send)
    rest = Sum(order, size, r_keep, r_send, ACROSS, ACROSS)
    c.near()
    e.near()
    rows0.away()
    rows1 = Rows(order, mine1, send1)
    rest.kept()
    c.own()
    e.own()
    rest.near()
    e.pair()
    c.pair()
    rest.own(2 * (own_q // 8))
    rest.over_tp(2 * (own_q // 8))
    rows0.land()
    rows1.away()
    c.four()
    rest.pair()
    e.four()
    contract_grad = order.step(place(order(me), *c.parts(), ACROSS))
    rest.four()
    rows1.land()
    late = order(tokens)
    expand_grad = order.step(place(order(me), *e.parts(), BACK))
    output_grad, query_grad, shared_grad, *vectors = unpack(
        me, *rest.parts(), own_q, expand_bias.shape[0]
    )
    out_bias, hidden_bias, query_bias, gain1, bias1, gain2, bias2, kv_bias = vectors

    def joined(which):
        return jnp.stack([rows0.total[which], rows1.total[which]])

    x = late.astype(F32)
    layer_out = (x + joined(0) + output_bias).astype(BF)
    norm, scale = normalize_rows(x)
    e = joined(1)
    slope_mean = jnp.mean(e * norm, -1, keepdims=True)
    input_grad = cotangent.astype(F32) + scale * (
        e - jnp.mean(e, -1, keepdims=True) - norm * slope_mean
    )
    return (
        layer_out,
        input_grad,
        query_grad.T,
        query_bias,
        shared_grad,
        kv_bias,
        output_grad,
        expand_grad,
        hidden_bias,
        contract_grad,
        out_bias,
        gain1,
        bias1,
        gain2,
        bias2,
    )


def normalize_rows(x):
    centre = x - jnp.mean(x, -1, keepdims=True)
    scale = lax.rsqrt(jnp.mean(centre * centre, -1, keepdims=True) + 1e-05)
    return centre * scale, scale


def solution(mesh):
    rows = P(None, ("dp", "tp"), None)
    in_specs = (
        rows, rows, P(None, "dp", None), P(None, "dp", None),
        P(), P(), P(), P(),
        P(None, "tp"), P("tp"), P(), P(), P("tp", None),
        P(None, "tp"), P("tp"), P("tp", None), P(),
    )
    out_specs = (
        rows, rows,
        P(None, "tp"), P("tp"), P(), P(), P("tp", None),
        P(None, "tp"), P("tp"), P("tp", None),
        P(), P(), P(), P(), P(),
    )
    return jax.shard_map(
        functools.partial(on_device, mesh.shape["dp"]),
        mesh=mesh,
        in_specs=in_specs,
        out_specs=out_specs,
        check_vma=False,
    )
```

```python
import functools

import jax
import jax.numpy as jnp
from jax import lax
from jax.experimental import pallas as pl
from jax.experimental.pallas import tpu as pltpu
from jax.sharding import PartitionSpec as P

ROT = 16
LANES = 128
QW = 256
PART = 72
LINES = ((0, 0), (1, 0), (2, 0), (8, 0), (9, 0), (10, 0), (11, 0), (12, QW))
BF = jnp.bfloat16
F32 = jnp.float32
ACROSS = (1, 2, 4)
ALONG = (2, 4, 1)
EXPAND = ALONG
BACK = ALONG
NT = (((1,), (1,)), ((), ()))
TN = (((0,), (0,)), ((), ()))
ANY = pl.BlockSpec(memory_space=pl.ANY)
VMEM = pl.BlockSpec(memory_space=pltpu.VMEM)
SMEM = pl.BlockSpec(memory_space=pltpu.SMEM)


def dot(a, b):
    return jnp.dot(a, b, preferred_element_type=F32)


def dot_nt(a, b):
    return lax.dot_general(a, b, NT, preferred_element_type=F32)


def dot_tn(a, b):
    return lax.dot_general(a, b, TN, preferred_element_type=F32)


def shape(dims, dtype=BF):
    return jax.ShapeDtypeStruct(dims, dtype)


def call(kernel, name, ins, outs, scratch, copies, flops=10**10):
    specs = [s for _, s in ins]
    arrays = [a for a, _ in ins]
    return pl.pallas_call(
        kernel,
        in_specs=specs,
        out_specs=[s for _, s in outs],
        out_shape=[o for o, _ in outs],
        scratch_shapes=list(scratch) + [pltpu.SemaphoreType.DMA((copies,))],
        compiler_params=pltpu.CompilerParams(vmem_limit_bytes=64 * 2**20 - 65536),
        cost_estimate=pl.CostEstimate(flops=flops, bytes_accessed=0, transcendentals=0),
        name=name,
    )(*arrays)


def offsets(bits):
    keep = (0, bits[2], bits[1], bits[1] | bits[2])
    return keep, tuple(k ^ bits[0] for k in keep)


class Copies:
    def __init__(self, sems):
        self.sems = sems
        self.count = 0

    def start(self, src, dst):
        copy = pltpu.make_async_copy(src, dst, self.sems.at[self.count])
        self.count += 1
        copy.start()
        return copy


def normalize(x):
    centre = x - jnp.mean(x, -1, keepdims=True)
    spread = jnp.mean(centre * centre, -1, keepdims=True)
    return centre * lax.rsqrt(spread + 1e-05)


def line(ref):
    return ref[...].reshape(1, -1)


def swap_halves(w):
    lane = lax.broadcasted_iota(jnp.int32, w.shape, 1)
    up = pltpu.roll(w, w.shape[1] - ROT // 2, 1)
    down = pltpu.roll(w, ROT // 2, 1)
    return jnp.where((lane % 64) < ROT // 2, up, down)


def spread_table(compact, filler, signs):
    fill = jnp.full((64 - ROT, compact.shape[1]), filler, F32)
    head = [signs * compact, compact, fill]
    return jnp.concatenate(head + head, 0).T


def hidden_kernel(
    pa, pb, gain1, bias1, gain2, bias2, we, be, acto, slopeo, h1o, h2o, no, xs, wev, acts, slopes, h1s, h2s, ns, sems
):
    copies = Copies(sems)
    got = [copies.start(pa, xs.at[0])]
    gotw = copies.start(we, wev)
    got.append(copies.start(pb, xs.at[1]))
    out = []
    for j in range(2):
        got[j].wait()
        for m in range(2):
            n = normalize(xs[j, m].astype(F32))
            ns[m, j] = n.astype(BF)
            h1s[m, j] = (n * line(gain1) + line(bias1)).astype(BF)
            h2 = (n * line(gain2) + line(bias2)).astype(BF)
            h2s[m, j] = h2
            for a, b in ((ns, no), (h1s, h1o), (h2s, h2o)):
                out.append(copies.start(a.at[m, j], b.at[m, j]))
            if j == 0 and m == 0:
                gotw.wait()
            u = dot(h2, wev[...]) + line(be)
            phi = 0.5 * (1.0 + lax.erf(u * 0.7071067811865476))
            acts[m, j] = (u * phi).astype(BF)
            slopes[m, j] = (phi + u * jnp.exp(-0.5 * u * u) * 0.3989422804014327).astype(BF)
            for a, b in ((acts, acto), (slopes, slopeo)):
                out.append(copies.start(a.at[m, j], b.at[m, j]))
    for c in out:
        c.wait()


def hidden(pieces, norms, we, be):
    _, rows, feat = pieces[0].shape
    ff = we.shape[1]
    wide, narrow = (2, 2, rows, ff), (2, 2, rows, feat)
    return call(
        hidden_kernel,
        "hidden",
        [(x, ANY) for x in pieces] + [(a, VMEM) for a in norms] + [(we, ANY), (be, VMEM)],
        [(shape(wide), ANY)] * 2 + [(shape(narrow), ANY)] * 3,
        [pltpu.VMEM(narrow, BF), pltpu.VMEM(we.shape, BF)]
        + [pltpu.VMEM(wide, BF)] * 2
        + [pltpu.VMEM(narrow, BF)] * 3,
        23,
        0,
    )


def doubled(kv):
    kv = kv.astype(F32)
    swapped = pltpu.roll(kv, 64, 1)
    low = lax.broadcasted_iota(jnp.int32, kv.shape, 1) < 64
    return jnp.where(low, kv, swapped).astype(BF), jnp.where(low, swapped, kv).astype(BF)


def stack_heads(block, heads):
    low = lax.broadcasted_iota(jnp.int32, (block.shape[0], LANES), 1) < 64
    zero = jnp.zeros((block.shape[0], LANES), block.dtype)
    parts = []
    for h in range(heads):
        part = block[:, LANES * (h // 2) : LANES * (h // 2 + 1)]
        parts.append(jnp.where(low, part, zero) if h % 2 == 0 else jnp.where(low, zero, part))
    return jnp.concatenate(parts, 0)


def join_heads(stacked, heads, rows):
    low = lax.broadcasted_iota(jnp.int32, (rows, LANES), 1) < 64
    part = lambda h: stacked[h * rows : (h + 1) * rows]
    zero = jnp.zeros((rows, LANES), stacked.dtype)
    cols = []
    for h in range(0, heads, 2):
        cols.append(jnp.where(low, part(h), part(h + 1) if h + 1 < heads else zero))
    return jnp.concatenate(cols, 1)


def send_rows(copies, rows, mine, send, which):
    places = (mine[0].at[which], send.at[0, which], mine[1].at[which], send.at[1, which])
    return [copies.start(rows.at[r], place) for r, place in enumerate(places)]


def halves_to(copies, halves, micro_id, into, t):
    return [
        copies.start(halves[r // 2].at[micro_id, r % 2], into.at[r ^ t]) for r in range(4)
    ]


def join_weights(wss, wts):
    wts[QW:] = wss[...].T


def project(micro_id, h1s, wts, qbias, sbias, bqkv, cs, sn, saved):
    qrs, kk, vv = saved[:3]
    rows = h1s.shape[1]
    own_q = qbias.shape[0]
    bqkv[:, :own_q] = line(qbias)
    bqkv[:, own_q:QW] = jnp.zeros((1, QW - own_q), F32)
    bqkv[:, QW:] = line(sbias)
    for a in range(4):
        here = slice(a * rows, (a + 1) * rows)
        qkv = dot_nt(h1s[a], wts[...]) + bqkv[...]
        c = spread_table(cs[micro_id, a], 1.0, 1.0)
        s = spread_table(sn[micro_id, a], 0.0, -1.0)
        low = lax.broadcasted_iota(jnp.int32, c.shape, 1) < 64
        cos = jnp.concatenate([c, c, jnp.where(low, c, 1.0)], 1)
        sin = jnp.concatenate([s, s, jnp.where(low, s, 0.0)], 1)
        qkv = qkv * cos + swap_halves(qkv) * sin
        qrs[a] = (qkv[:, :QW] * 0.125).astype(BF)
        kk[here], vv[here] = doubled(qkv[:, QW:].astype(BF))


def attend_rows(micro_id, heads, ends, saved, finished=lambda block: None):
    qrs, kk, vv, cx, *probs_of = saved
    rows = qrs.shape[1]
    spans = [(a + 1) * rows for a in range(4)]
    scores = dot_nt(stack_heads(qrs[3], heads), kk[: spans[3]])
    for a in (3, 2, 1, 0):
        here = scores
        if a > 0:
            scores = dot_nt(stack_heads(qrs[a - 1], heads), kk[: spans[a - 1]])
        row = lax.broadcasted_iota(jnp.int32, (rows, 1), 0) + a * rows
        begin = jnp.zeros((rows, 1), jnp.int32)
        for d in range(ends.shape[2] - 1):
            begin = jnp.where(row >= ends[micro_id, 0, d], ends[micro_id, 0, d], begin)
        col = lax.broadcasted_iota(jnp.int32, (rows, spans[a]), 1)
        allowed = (col >= begin) & (col <= row)
        for h in range(heads):
            mine = slice(h * rows, (h + 1) * rows)
            s = jnp.where(allowed, here[mine], -1e30)
            e = jnp.exp(s - jnp.max(s, -1, keepdims=True))
            probs_of[a][mine] = (e * (1.0 / jnp.sum(e, -1, keepdims=True))).astype(BF)
        done = a + 1
        if done < 4:
            cx[done] = join_heads(dot(probs_of[done][...], vv[: spans[done]]), heads, rows).astype(BF)
            finished(done)
    cx[0] = join_heads(dot(probs_of[0][...], vv[: spans[0]]), heads, rows).astype(BF)


def attend_kernel(micro_id, heads, *refs):
    refs = list(refs)
    take = lambda k: [refs.pop(0) for _ in range(k)]
    t_ref, ends = take(2)
    h1 = take(2)
    wq, ws, qbias, sbias, cs, sn = take(6)
    outs = take(8)
    h1s, wss, wts, bqkv = take(4)
    saved = take(8)
    copies = Copies(take(1)[0])
    got = load_weights(copies, wq, ws, wss, wts)
    got += halves_to(copies, h1, micro_id, h1s, t_ref[0])
    for c in got:
        c.wait()
    join_weights(wss, wts)
    project(micro_id, h1s, wts, qbias, sbias, bqkv, cs, sn, saved)
    sent = [copies.start(saved[i], outs[i]) for i in range(3)]

    def finished(block):
        sent.append(copies.start(saved[4 + block], outs[4 + block]))

    attend_rows(micro_id, heads, ends, saved, finished)
    finished(0)
    sent.append(copies.start(saved[3], outs[3]))
    for c in sent:
        c.wait()


def load_weights(copies, wq, ws, wss, wts):
    own_q = wq.shape[0]
    wts[own_q:QW] = jnp.zeros((QW - own_q, wts.shape[1]), BF)
    return [copies.start(wq, wts.at[pl.ds(0, own_q)]), copies.start(ws, wss)]


def weights_scratch(ws):
    width = QW + LANES
    return [
        pltpu.VMEM(ws.shape, BF), pltpu.VMEM((width, ws.shape[0]), BF), pltpu.VMEM((1, width), F32)
    ]


def saved_shapes(rows, heads):
    length = 4 * rows
    saved = [(4, rows, QW), (length, LANES), (length, LANES), (4, rows, QW)]
    return saved + [(heads * rows, (a + 1) * rows) for a in range(4)]


def attend(micro_id, rank, ends, h1, wq, ws, qbias, sbias, cs, sn, heads, flops):
    _, _, rows, feat = h1[0].shape
    ins = [(rank, SMEM), (ends, SMEM)] + [(a, ANY) for a in (*h1, wq, ws)]
    ins += [(a, VMEM) for a in (qbias, sbias, cs, sn)]
    saved = saved_shapes(rows, heads)
    scratch = [pltpu.VMEM((4, rows, feat), BF)] + weights_scratch(ws)
    return call(
        functools.partial(attend_kernel, micro_id, heads), "attend", ins,
        [(shape(a), ANY) for a in saved], scratch + [pltpu.VMEM(a, BF) for a in saved], 14, flops,
    )


def attend_back_kernel(micro_id, heads, first, whole, *refs):
    refs = list(refs)
    take = lambda k: [refs.pop(0) for _ in range(k)]
    t_ref, me_ref = take(2)
    if whole:
        ends, qbias, sbias = take(3)
    else:
        saved = take(8)
    gpieces = take(4)
    h1, act, du, n = take(2), take(2), take(2), take(2)
    wq, ws, wo, wc, we, gain1, gain2, cs, sn = take(9)
    if not first:
        og_in, qs_in, vec_in, hid_in = take(4)
    rows_kept = take(2)
    rows_sent, = take(1)
    results = take(3 if first else 2)
    gs, h1s, acts, dus, ns, wss, wts, bqkv, wos, wcs, wes = take(11)
    qrs, kk, vv, cx, *probs_of = kept = take(8)
    dctx, = take(1)
    dss = take(2)
    dk, dv, dqkv, outb, eb, ogs, qss = take(7)
    if not first:
        lines, keeps, sends = take(3)
    copies = Copies(take(1)[0])
    rows = gs.shape[1]
    t = t_ref[0]
    spans = [(a + 1) * rows for a in range(4)]
    def load_h():
        return load_weights(copies, wq, ws, wss, wts) + halves_to(copies, h1, micro_id, h1s, t)

    if whole:
        got_h = load_h()
    own_q = wo.shape[0]
    got_g = [copies.start(wo, wos.at[pl.ds(0, own_q)])]
    wos[own_q:] = jnp.zeros((QW - own_q, wo.shape[1]), BF)
    got_g += [copies.start(g.at[micro_id], gs.at[r ^ t]) for r, g in enumerate(gpieces)]
    order = (2, 7, 0, 1, 6, 5, 4, 3)
    got_saved = [] if whole else [copies.start(saved[i], kept[i]) for i in order]
    got_out = halves_to(copies, act, micro_id, acts, 0) + [copies.start(wc, wcs)]
    if not whole:
        got_h = load_h()
    got_e = halves_to(copies, du, micro_id, dus, 0) + [copies.start(we, wes)]
    got_e += halves_to(copies, n, micro_id, ns, 0)
    if not first:
        got_e += [copies.start(og_in, ogs), copies.start(qs_in, qss)]
    if whole:
        for c in got_h:
            c.wait()
        join_weights(wss, wts)
        project(micro_id, h1s, wts, qbias, sbias, bqkv, cs, sn, kept)
        attend_rows(micro_id, heads, ends, kept)
    for c in got_g + (got_out + got_e if whole else []):
        c.wait()
    dctx[...] = dot_nt(gs[...].reshape(4 * rows, gs.shape[2]), wos[...]).astype(BF)
    for c in got_saved:
        c.wait()
    dk[...] = jnp.zeros_like(dk)
    dv[...] = jnp.zeros_like(dv)
    stacked = lambda a: stack_heads(dctx[a * rows : (a + 1) * rows], heads)

    def finish(a):
        dscores = dss[a % 2][:, : spans[a]]
        dk[: spans[a]] += dot_tn(dscores, stack_heads(qrs[a], heads))
        dv[: spans[a]] += dot_tn(probs_of[a][...], stacked(a))
        dq = join_heads(dot(dscores, kk[: spans[a]]), heads, rows) * 0.125
        c = spread_table(cs[micro_id, a], 1.0, 1.0)
        s = spread_table(sn[micro_id, a], 0.0, -1.0)
        cos = jnp.concatenate([c, c], 1)
        sin = jnp.concatenate([s, s], 1)
        dqkv[a, :, :QW] = (dq * cos - swap_halves(dq) * sin).astype(BF)

    dprobs = dot_nt(stacked(3), vv[: spans[3]])
    for a in (3, 2, 1, 0):
        here = dprobs
        if a > 0:
            dprobs = dot_nt(stacked(a - 1), vv[: spans[a - 1]])
        for h in range(heads):
            mine = slice(h * rows, (h + 1) * rows)
            p = probs_of[a][mine].astype(F32)
            weighted = p * here[mine]
            delta = jnp.sum(weighted, -1, keepdims=True)
            dss[a % 2][mine, : spans[a]] = (weighted - p * delta).astype(BF)
        if a < 3:
            finish(a + 1)
    finish(0)
    for a in range(4):
        here = slice(a * rows, (a + 1) * rows)
        c = spread_table(cs[micro_id, a], 1.0, 1.0)
        s = spread_table(sn[micro_id, a], 0.0, -1.0)
        dkf = dk[here] + pltpu.roll(dk[here], 64, 1)
        dvf = dv[here] + pltpu.roll(dv[here], 64, 1)
        dkf = dkf * c - swap_halves(dkf) * s
        low = lax.broadcasted_iota(jnp.int32, dkf.shape, 1) < 64
        dqkv[a, :, QW:] = jnp.where(low, dkf, dvf).astype(BF)
    for c in [] if whole else got_out:
        c.wait()
    for r in range(4):
        outb[r] = (dot(cx[r ^ t], wos[...]) + dot(acts[r], wcs[...])).astype(BF)
    sent = send_rows(copies, outb, rows_kept, rows_sent, 0)

    for c in [] if whole else got_e + got_h:
        c.wait()
    if not whole:
        join_weights(wss, wts)
    width = QW + LANES
    vec_width = gs.shape[2]
    flat = dqkv[...].reshape(4 * rows, width)
    ograd = dot_tn(cx[...].reshape(4 * rows, QW), gs[...].reshape(4 * rows, gs.shape[2]))
    qgrad = dot_tn(flat, h1s[...].reshape(4 * rows, h1s.shape[2]))
    ogs[...] = ograd if first else ogs[...] + ograd
    qss[...] = qgrad if first else qss[...] + qgrad
    if first:
        sent += [copies.start(ogs, results[0]), copies.start(qss, results[1])]
    sums = [jnp.zeros((1, vec_width), F32) for _ in range(4)]
    for r in range(4):
        e1 = dot(dqkv[r ^ t], wts[...])
        e2 = dot_nt(dus[r], wes[...])
        eb[r] = (e1 * line(gain1) + e2 * line(gain2)).astype(BF)
        norm = ns[r].astype(F32)
        for i, term in enumerate((e1 * norm, e1, e2 * norm, e2)):
            sums[i] += jnp.sum(term, 0, keepdims=True)
    sent += send_rows(copies, eb, rows_kept, rows_sent, 1)
    column = jnp.sum(flat.astype(F32), 0, keepdims=True)
    sums.append(jnp.concatenate([column, jnp.zeros((1, vec_width - width), F32)], 1))
    if first:
        results[2][...] = jnp.concatenate(sums + [jnp.zeros((3, vec_width), F32)], 0)
    else:
        sums = [a + vec_in[i : i + 1] for i, a in enumerate(sums)]
        zero = jnp.zeros((5, vec_width), F32)
        lines[...] = jnp.concatenate(
            [hid_in[0:1], hid_in[1:2], sums[4], zero] + sums + [zero[:3]], 0
        )
        pack_parts(ogs, qss, lines, keeps, sends, me_ref[0], heads * 8)
        sent += [copies.start(keeps, results[0]), copies.start(sends, results[1])]
    for c in sent:
        c.wait()


def pack_parts(og, qs, lines, keep, send, me, cut):
    tall = LANES // 8
    for out, order in zip((keep, send), offsets(ACROSS)):
        for i in range(4):
            b = order[i] ^ me
            rows = lambda ref, size, base: ref[pl.ds(pl.multiple_of(b * size + base, 8), size)]
            line = lambda i: jnp.broadcast_to(lines[pl.ds(b + i, 1)], (8, lines.shape[1]))
            own = lax.broadcasted_iota(jnp.int32, (8, lines.shape[1]), 0) < 4
            both = jnp.where(own, line(0), line(8))
            part = [rows(og, cut, 0), rows(qs, cut, 0), rows(qs, tall, QW), both]
            out[i] = jnp.concatenate(part, 0).astype(BF)


def attend_back(
    micro_id, rank, me, saved, gs, h1, act, du, n, wq, ws, wo, wc, we, gain1, gain2, cs, sn, heads,
    whole=False, before=None,
):
    _, rows, feat = gs[0].shape
    ff = wc.shape[0]
    width = QW + LANES
    length = 4 * rows
    first = before is None
    ins = [(rank, SMEM), (me, SMEM)]
    ins += [(saved[0], SMEM)] + [(a, VMEM) for a in saved[1:]] if whole else [(a, ANY) for a in saved]
    ins += [(a, ANY) for a in (*gs, *h1, *act, *du, *n, wq, ws, wo, wc, we)]
    ins += [(a, VMEM) for a in (gain1, gain2, cs, sn)]
    if not first:
        ins += [(a, ANY) for a in before[:2]] + [(a, VMEM) for a in before[2:]]
    outs = [(shape((2, rows, feat)), ANY)] * 2 + [(shape((2, 2, rows, feat)), ANY)]
    grads = [shape((QW, feat), F32), shape((width, feat), F32)]
    part = shape((4, PART, feat))
    if first:
        outs += [(g, ANY) for g in grads] + [(shape((8, feat), F32), VMEM)]
    else:
        outs += [(part, ANY)] * 2
    stack, wide = pltpu.VMEM((4, rows, feat), BF), pltpu.VMEM((4, rows, ff), BF)
    scratch = [stack, stack, wide, wide, stack]
    scratch += weights_scratch(ws)
    scratch += [pltpu.VMEM(a, BF) for a in ((QW, feat), wc.shape, we.shape)]
    scratch += [pltpu.VMEM(a, BF) for a in saved_shapes(rows, heads)]
    scratch += [
        pltpu.VMEM((length, QW), BF),
        pltpu.VMEM((heads * rows, length), BF), pltpu.VMEM((heads * rows, length), BF),
        pltpu.VMEM((length, LANES), F32), pltpu.VMEM((length, LANES), F32),
        pltpu.VMEM((4, rows, width), BF), stack, stack,
    ]
    scratch += [pltpu.VMEM(g.shape, F32) for g in grads]
    if not first:
        scratch += [pltpu.VMEM((16, feat), F32)] + [pltpu.VMEM(part.shape, BF)] * 2
    return call(
        functools.partial(attend_back_kernel, micro_id, heads, first, whole), "attend_grad", ins, outs,
        scratch, 46,
    )


def store_parts(total, parts, me, bits):
    part = total.shape[0] // 8
    for b in range(8):
        offset = b ^ me
        place = sum(((offset // bit) % 2) * weight for bit, weight in zip(bits, (4, 2, 1)))
        parts[place] = total[b * part : (b + 1) * part].astype(BF)


def pieces_to(copies, pieces, into):
    return [copies.start(p.at[m], into.at[m, j]) for j, p in enumerate(pieces) for m in range(2)]


def flat(ref):
    return ref[...].reshape(-1, ref.shape[-1])


def hidden_back_kernel(first, *refs):
    refs = list(refs)
    take = lambda k: [refs.pop(0) for _ in range(k)]
    me_ref, = take(1)
    pieces = take(2)
    act, slope, h2, wc = take(4)
    if not first:
        before = take(2)
        sums_in, = take(1)
    duo, = take(1)
    outs = take(2 if first else 4)
    sums, = take(1)
    gs, acts, slopes, wcs, h2s, dus, *accs = take(8)
    parts = None if first else take(2)
    copies = Copies(take(1)[0])
    got = pieces_to(copies, pieces, gs) + [copies.start(act, acts)]
    if not first:
        got_sums = [copies.start(before[0], accs[0])]
    got_back = [copies.start(wc, wcs), copies.start(slope, slopes)]
    got_late = [copies.start(h2, h2s)]
    if not first:
        got_sums.append(copies.start(before[1], accs[1]))

    def total(i, left, right):
        if first:
            accs[i][...] = dot_tn(flat(left), flat(right))
            return [copies.start(accs[i], outs[i])]
        got_sums[i].wait()
        both = accs[i][...] + dot_tn(flat(left), flat(right))
        store_parts(both, parts[i], me_ref[0], (ACROSS, EXPAND)[i])
        return [copies.start(parts[i].at[pl.ds(4 * k, 4)], outs[2 * i + k]) for k in (0, 1)]

    for c in got:
        c.wait()
    sent = total(0, acts, gs)
    for c in got_back:
        c.wait()
    gsum = jnp.zeros((1, gs.shape[3]), F32)
    column = jnp.zeros((1, slopes.shape[3]), F32)
    for m in range(2):
        for j in range(2):
            g = gs[m, j]
            du = (dot_nt(g, wcs[...]) * slopes[m, j].astype(F32)).astype(BF)
            dus[m, j] = du
            gsum += jnp.sum(g.astype(F32), 0, keepdims=True)
            column += jnp.sum(du.astype(F32), 0, keepdims=True)
    sent.append(copies.start(dus, duo))
    for c in got_late:
        c.wait()
    sent += total(1, h2s, dus)
    rowid = lax.broadcasted_iota(jnp.int32, sums.shape, 0)
    both = jnp.where(rowid == 0, gsum, jnp.where(rowid == 1, column, 0.0))
    sums[...] = both if first else sums_in[...] + both
    for c in sent:
        c.wait()


def hidden_back(me, pieces, act, slope, h2, wc, before=None):
    _, _, rows, feat = h2.shape
    ff = wc.shape[0]
    first = before is None
    ins = [(me, SMEM)] + [(a, ANY) for a in (*pieces, act, slope, h2, wc)]
    outs = [(shape(slope.shape), ANY)]
    if first:
        outs += [(shape((ff, feat), F32), ANY), (shape((feat, ff), F32), ANY)]
    else:
        ins += [(before[0], ANY), (before[1], ANY), (before[2], VMEM)]
        outs += [(shape((4, ff // 8, feat)), ANY)] * 2 + [(shape((4, feat // 8, ff)), ANY)] * 2
    outs.append((shape((8, feat), F32), VMEM))
    scratch = [
        pltpu.VMEM(h2.shape, BF), pltpu.VMEM(act.shape, BF), pltpu.VMEM(slope.shape, BF),
        pltpu.VMEM(wc.shape, BF), pltpu.VMEM(h2.shape, BF), pltpu.VMEM(slope.shape, BF),
        pltpu.VMEM((ff, feat), F32), pltpu.VMEM((feat, ff), F32),
    ]
    if not first:
        scratch += [pltpu.VMEM((8, ff // 8, feat), BF), pltpu.VMEM((8, feat // 8, ff), BF)]
    return call(
        functools.partial(hidden_back_kernel, first), "hidden_grad", ins, outs, scratch, 15,
        0 if first else 10**10,
    )


def after(value, *others):
    return lax.optimization_barrier((value, others))[0]


def add(*terms):
    return sum(a.astype(F32) for a in terms).astype(BF)


def swap(value, axis, size, bit):
    return lax.ppermute(value, axis, [(i, i ^ bit) for i in range(size)])


class Order:
    def __init__(self):
        self.last = None

    def __call__(self, value):
        if self.last is not None:
            value = after(value, self.last)
        return value

    def step(self, result):
        self.last = result
        return result


class Sum:
    def __init__(self, order, size, keep, send, bits, back):
        self.order, self.size, self.bits, self.back = order, size, bits, back
        self.have = keep
        self.flying = swap(order(send), "dp", size, bits[0])

    def kept(self):
        have = self.order(self.have)
        halves = add(have[:2], self.flying[:2]), add(have[2:], self.flying[2:])
        self.have, send = self.order.step(halves)
        self.flying = swap(send, "dp", self.size, self.bits[1])

    def near(self):
        have = self.order(self.have)
        halves = add(have[0], self.flying[0]), add(have[1], self.flying[1])
        self.have, send = self.order.step(halves)
        self.flying = swap(send, "dp", self.size, self.bits[2])

    def own(self, over_tp=0):
        self.have = self.order.step(add(self.order(self.have), self.flying))
        if self.size > 8:
            groups = [[low + 8 * high for high in range(self.size // 8)] for low in range(8)]
            whole = lax.psum(self.have.astype(F32), "dp", axis_index_groups=groups)
            self.have = whole.astype(BF)
        if over_tp:
            self.tail = self.have[over_tp:]
            self.sums = [swap(self.tail, "tp", 4, bit) for bit in (1, 2, 3)]
        else:
            self.flying = swap(self.have, "dp", self.size, self.back[2])

    def over_tp(self, first):
        tail = self.order(self.tail)
        row = lax.broadcasted_iota(jnp.int32, tail.shape, 0) - LANES // 8
        whole = jnp.where((row >= 0) & (row < 4), tail, add(tail, *self.sums))
        self.have = self.order.step(jnp.concatenate([self.have[:first], whole], 0))
        self.flying = swap(self.have, "dp", self.size, self.back[2])

    def pair(self):
        self.have = self.order.step(jnp.stack([self.order(self.have), self.flying]))
        self.flying = swap(self.have, "dp", self.size, self.back[1])

    def four(self):
        self.have = self.order.step(jnp.concatenate([self.order(self.have), self.flying], 0))
        self.flying = swap(self.have, "dp", self.size, self.back[0])

    def parts(self):
        return self.have, self.flying


def halve_kernel(*refs):
    values, outs, held, sums, sems = refs[:4], refs[4:8], refs[8:12], refs[12:14], refs[14]
    copies = Copies(sems)
    got = [copies.start(a, b) for a, b in zip(values, held)]
    sent = []
    for i in range(2):
        got[2 * i].wait()
        got[2 * i + 1].wait()
        sums[i][...] = (held[2 * i][...].astype(F32) + held[2 * i + 1][...].astype(F32)).astype(BF)
        for k in range(2):
            sent.append(copies.start(sums[i].at[pl.ds(2 * k, 2)], outs[2 * i + k]))
    for c in sent:
        c.wait()


def kept_both(order, first, second):
    values = order((first.have, first.flying, second.have, second.flying))
    outs = [shape((2, *a.shape[1:])) for a in values]
    scratch = [pltpu.VMEM(a.shape, BF) for a in values]
    halves = call(
        halve_kernel, "halve", [(a, ANY) for a in values], [(o, ANY) for o in outs],
        scratch + [scratch[0], scratch[2]], 8, 0,
    )
    order.step(halves)
    for one, (stay, leave) in ((first, halves[:2]), (second, halves[2:])):
        one.have = stay
        one.flying = swap(leave, "dp", one.size, one.bits[1])


class Rows:
    def __init__(self, order, mine, send):
        self.order, self.mine = order, mine
        self.got = swap(order(send), "tp", 4, 1)

    def away(self):
        away = self.order.step(add(self.order(self.mine[1]), self.got[1]))
        self.far = swap(away, "tp", 4, 2)

    def land(self):
        terms = self.order(self.mine[0]), self.got[0], self.far
        self.total = self.order.step(sum(a.astype(F32) for a in terms))


def place_kernel(me_ref, four, other, out):
    i = pl.program_id(0)

    @pl.when(i < 4)
    def _():
        out[...] = four[0].astype(F32)

    @pl.when(i >= 4)
    def _():
        out[...] = other[0].astype(F32)


def place(me, four, other, bits):
    _, part, width = four.shape

    def where(i, me):
        j = i % 4
        order = (j // 2) * bits[1] + (j % 2) * bits[2] + (i // 4) * bits[0]
        return order ^ me[0], 0

    return pl.pallas_call(
        place_kernel,
        grid_spec=pltpu.PrefetchScalarGridSpec(
            num_scalar_prefetch=1,
            grid=(8,),
            in_specs=[
                pl.BlockSpec((1, part, width), lambda i, me: (jnp.minimum(i, 3), 0, 0)),
                pl.BlockSpec((1, part, width), lambda i, me: (jnp.maximum(i - 4, 0), 0, 0)),
            ],
            out_specs=pl.BlockSpec((part, width), where),
        ),
        out_shape=shape((8 * part, width), F32),
        compiler_params=pltpu.CompilerParams(vmem_limit_bytes=32 * 2**20),
        cost_estimate=pl.CostEstimate(flops=0, bytes_accessed=0, transcendentals=0),
        name="place_parts",
    )(me, four, other)


def unpack_kernel(own_q, me_ref, four, other, og, qs, sg, *refs):
    *vectors, shared, lines = refs
    me = me_ref[0]
    cut = own_q // 8
    tall = LANES // 8
    for ref, order in zip((four, other), offsets(ACROSS)):
        for i in range(4):
            b = order[i] ^ me
            part = ref[i].astype(F32)
            rows = lambda size: pl.ds(pl.multiple_of(b * size, 8), size)
            og[rows(cut)] = part[:cut]
            qs[rows(cut)] = part[cut : 2 * cut]
            shared[rows(tall)] = part[2 * cut : 2 * cut + tall]
            last = part[2 * cut + tall :]
            lines[pl.ds(b, 1)] = last[:1]
            lines[pl.ds(b + 8, 1)] = last[4:5]
    sg[...] = shared[...].T
    for ref, (i, base) in zip(vectors, LINES):
        ref[...] = lines[i, base : base + ref.shape[0]]


def unpack(me, four, other, own_q, ff):
    feat = four.shape[2]
    sizes = (feat, ff, own_q, feat, feat, feat, feat, LANES)
    outs = [(own_q, feat), (own_q, feat), (feat, LANES)] + [(n,) for n in sizes]
    return pl.pallas_call(
        functools.partial(unpack_kernel, own_q),
        in_specs=[SMEM, VMEM, VMEM],
        out_specs=[VMEM] * len(outs),
        out_shape=[shape(a, F32) for a in outs],
        scratch_shapes=[pltpu.VMEM((LANES, feat), F32), pltpu.VMEM((16, feat), F32)],
        compiler_params=pltpu.CompilerParams(vmem_limit_bytes=32 * 2**20),
        cost_estimate=pl.CostEstimate(flops=0, bytes_accessed=0, transcendentals=0),
        name="unpack",
    )(me, four, other)


def doc_layout(ends, scales, length):
    row = jnp.arange(length, dtype=jnp.int32)[None]
    begin = jnp.zeros_like(row)
    step = scales[:, :1]
    for d in range(ends.shape[1] - 1):
        past = row >= ends[:, d : d + 1]
        begin = jnp.where(past, ends[:, d : d + 1], begin)
        step = jnp.where(past, scales[:, d + 1 : d + 2], step)
    return (row - begin) * step


def angle_tables(placed, rows):
    freqs = 10000.0 ** (-jnp.arange(ROT // 2, dtype=F32) * 2.0 / ROT)
    blocks = placed.astype(F32).reshape(placed.shape[0], 4, 1, rows)
    angles = blocks * freqs[:, None]
    return jnp.cos(angles), jnp.sin(angles)


def on_device(
    size,
    tokens,
    cotangent,
    doc_ends,
    pos_scale,
    first_gain,
    first_bias,
    second_gain,
    second_bias,
    w_query,
    query_bias,
    w_shared,
    shared_bias,
    w_output,
    w_expand,
    expand_bias,
    w_contract,
    output_bias,
):
    micro, rows, feat = tokens.shape
    heads = w_query.shape[1] // 64
    own_q = w_query.shape[1]
    length = rows * 4
    rank = lax.axis_index("tp").astype(jnp.int32)[None]
    me = (lax.axis_index("dp").astype(jnp.int32) & 7)[None]

    order = Order()

    def begin(values):
        return values, swap(values, "tp", 4, 1), swap(values, "tp", 4, 2)

    def finish(own, near, far):
        return own, near, far, swap(far, "tp", 4, 1)

    xs, gs = begin(tokens), begin(cotangent)

    norms = (first_gain, first_bias, second_gain, second_bias)
    ends, scales = doc_ends[:, 0], pos_scale[:, 0]
    cs, sn = angle_tables(doc_layout(ends, scales, length), rows)

    act_a, slope_a, h1_a, h2_a, n_a = hidden(xs[:2], norms, w_expand, expand_bias)
    order.step(act_a)
    du_a, cacc, eacc, sums = hidden_back(order(me), gs[:2], act_a, slope_a, h2_a, w_contract)
    order.step(sums)
    xs = finish(xs[0], xs[1], order(xs[2]))
    act_b, slope_b, h1_b, h2_b, n_b = hidden(xs[2:], norms, w_expand, expand_bias)
    order.step(act_b)
    h1, n, act = (h1_a, h1_b), (n_a, n_b), (act_a, act_b)
    biases = (query_bias, shared_bias)
    saved0 = attend(
        0, order(rank), doc_ends, h1, w_query.T, w_shared, *biases, cs, sn, heads, 0
    )
    order.step(saved0[0])
    gs = finish(gs[0], gs[1], order(gs[2]))
    du_b, c_keep, c_send, e_keep, e_send, sums = hidden_back(
        order(me), gs[2:], act_b, slope_b, h2_b, w_contract, (cacc, eacc, sums)
    )
    order.step(sums)
    weights = (w_query.T, w_shared, w_output, w_contract, w_expand, first_gain, second_gain)
    inputs = (gs, h1, act, (du_a, du_b), n, *weights, cs, sn, heads)
    c = Sum(order, size, c_keep, c_send, ACROSS, ACROSS)
    e = Sum(order, size, e_keep, e_send, EXPAND, BACK)
    *mine0, send0, og, qs, vec = attend_back(0, order(rank), me, saved0, *inputs)
    order.step(vec)
    kept_both(order, c, e)
    rows0 = Rows(order, mine0, send0)
    *mine1, send1, r_keep, r_send = attend_back(
        1, order(rank), me, (doc_ends, *biases), *inputs, True, (og, qs, vec, sums)
    )
    order.step(r_send)
    rest = Sum(order, size, r_keep, r_send, ACROSS, ACROSS)
    c.near()
    rows0.away()
    rows1 = Rows(order, mine1, send1)
    e.near()
    rest.kept()
    c.own()
    rest.near()
    e.own()
    c.pair()
    rest.own(2 * (own_q // 8))
    rest.over_tp(2 * (own_q // 8))
    e.pair()
    rows0.land()
    rows1.away()
    c.four()
    rest.pair()
    e.four()
    contract_grad = order.step(place(order(me), *c.parts(), ACROSS))
    rest.four()
    rows1.land()
    layer_out, input_grad = order.step(
        final_rows(order(tokens), cotangent, output_bias, (rows0.total, rows1.total))
    )
    expand_grad = order.step(place(order(me), *e.parts(), BACK))
    output_grad, query_grad, shared_grad, *vectors = unpack(
        me, *rest.parts(), own_q, expand_bias.shape[0]
    )
    out_bias, hidden_bias, query_bias, gain1, bias1, gain2, bias2, kv_bias = vectors

    return (
        layer_out,
        input_grad,
        query_grad.T,
        query_bias,
        shared_grad,
        kv_bias,
        output_grad,
        expand_grad,
        hidden_bias,
        contract_grad,
        out_bias,
        gain1,
        bias1,
        gain2,
        bias2,
    )


def final_rows(tokens, cotangent, output_bias, terms):
    joined = lambda which: jnp.stack([t[which] for t in terms])
    x = tokens.astype(F32)
    layer_out = (x + joined(0) + output_bias).astype(BF)
    norm, scale = normalize_rows(x)
    e = joined(1)
    slope_mean = jnp.mean(e * norm, -1, keepdims=True)
    input_grad = cotangent.astype(F32) + scale * (
        e - jnp.mean(e, -1, keepdims=True) - norm * slope_mean
    )
    return layer_out, input_grad


def normalize_rows(x):
    centre = x - jnp.mean(x, -1, keepdims=True)
    scale = lax.rsqrt(jnp.mean(centre * centre, -1, keepdims=True) + 1e-05)
    return centre * scale, scale


def solution(mesh):
    rows = P(None, ("dp", "tp"), None)
    in_specs = (
        rows, rows, P(None, "dp", None), P(None, "dp", None),
        P(), P(), P(), P(),
        P(None, "tp"), P("tp"), P(), P(), P("tp", None),
        P(None, "tp"), P("tp"), P("tp", None), P(),
    )
    out_specs = (
        rows, rows,
        P(None, "tp"), P("tp"), P(), P(), P("tp", None),
        P(None, "tp"), P("tp"), P("tp", None),
        P(), P(), P(), P(), P(),
    )
    return jax.shard_map(
        functools.partial(on_device, mesh.shape["dp"]),
        mesh=mesh,
        in_specs=in_specs,
        out_specs=out_specs,
        check_vma=False,
    )
```

```python
import functools

import jax
import jax.numpy as jnp
from jax import lax
from jax.experimental import pallas as pl
from jax.experimental.pallas import tpu as pltpu
from jax.sharding import PartitionSpec as P

ROT = 16
LANES = 128
QW = 256
PART = 80
LINES = ((0, 0), (1, 0), (2, 0), (8, 0), (9, 0), (10, 0), (11, 0), (12, QW))
BF = jnp.bfloat16
F32 = jnp.float32
ACROSS = (1, 2, 4)
ALONG = (2, 4, 1)
EXPAND = ALONG
BACK = ALONG
NT = (((1,), (1,)), ((), ()))
TN = (((0,), (0,)), ((), ()))
ANY = pl.BlockSpec(memory_space=pl.ANY)
VMEM = pl.BlockSpec(memory_space=pltpu.VMEM)
SMEM = pl.BlockSpec(memory_space=pltpu.SMEM)


def dot(a, b):
    return jnp.dot(a, b, preferred_element_type=F32)


def dot_nt(a, b):
    return lax.dot_general(a, b, NT, preferred_element_type=F32)


def dot_tn(a, b):
    return lax.dot_general(a, b, TN, preferred_element_type=F32)


def shape(dims, dtype=BF):
    return jax.ShapeDtypeStruct(dims, dtype)


def call(kernel, name, ins, outs, scratch, copies, flops=10**10):
    specs = [s for _, s in ins]
    arrays = [a for a, _ in ins]
    return pl.pallas_call(
        kernel,
        in_specs=specs,
        out_specs=[s for _, s in outs],
        out_shape=[o for o, _ in outs],
        scratch_shapes=list(scratch) + [pltpu.SemaphoreType.DMA((copies,))],
        compiler_params=pltpu.CompilerParams(vmem_limit_bytes=64 * 2**20 - 65536),
        cost_estimate=pl.CostEstimate(flops=flops, bytes_accessed=0, transcendentals=0),
        name=name,
    )(*arrays)


def offsets(bits):
    keep = (0, bits[2], bits[1], bits[1] | bits[2])
    return keep, tuple(k ^ bits[0] for k in keep)


class Copies:
    def __init__(self, sems):
        self.sems = sems
        self.count = 0

    def start(self, src, dst):
        copy = pltpu.make_async_copy(src, dst, self.sems.at[self.count])
        self.count += 1
        copy.start()
        return copy


def normalize(x):
    centre = x - jnp.mean(x, -1, keepdims=True)
    spread = jnp.mean(centre * centre, -1, keepdims=True)
    return centre * lax.rsqrt(spread + 1e-05)


def line(ref):
    return ref[...].reshape(1, -1)


def swap_halves(w):
    lane = lax.broadcasted_iota(jnp.int32, w.shape, 1)
    up = pltpu.roll(w, w.shape[1] - ROT // 2, 1)
    down = pltpu.roll(w, ROT // 2, 1)
    return jnp.where((lane % 64) < ROT // 2, up, down)


def spread_table(compact, filler, signs):
    fill = jnp.full((64 - ROT, compact.shape[1]), filler, F32)
    head = [signs * compact, compact, fill]
    return jnp.concatenate(head + head, 0).T


def hidden_kernel(
    pa, pb, gain1, bias1, gain2, bias2, we, be, acto, slopeo, h1o, h2o, no, xs, wev, acts, slopes, h1s, h2s, ns, sems
):
    copies = Copies(sems)
    got = [copies.start(pa, xs.at[0])]
    gotw = copies.start(we, wev)
    got.append(copies.start(pb, xs.at[1]))
    out = []
    for j in range(2):
        got[j].wait()
        for m in range(2):
            n = normalize(xs[j, m].astype(F32))
            ns[m, j] = n.astype(BF)
            h1s[m, j] = (n * line(gain1) + line(bias1)).astype(BF)
            h2 = (n * line(gain2) + line(bias2)).astype(BF)
            h2s[m, j] = h2
            for a, b in ((ns, no), (h1s, h1o), (h2s, h2o)):
                out.append(copies.start(a.at[m, j], b.at[m, j]))
            if j == 0 and m == 0:
                gotw.wait()
            u = dot(h2, wev[...]) + line(be)
            phi = 0.5 * (1.0 + lax.erf(u * 0.7071067811865476))
            acts[m, j] = (u * phi).astype(BF)
            slopes[m, j] = (phi + u * jnp.exp(-0.5 * u * u) * 0.3989422804014327).astype(BF)
            for a, b in ((acts, acto), (slopes, slopeo)):
                out.append(copies.start(a.at[m, j], b.at[m, j]))
    for c in out:
        c.wait()


def hidden(pieces, norms, we, be):
    _, rows, feat = pieces[0].shape
    ff = we.shape[1]
    wide, narrow = (2, 2, rows, ff), (2, 2, rows, feat)
    return call(
        hidden_kernel,
        "hidden",
        [(x, ANY) for x in pieces] + [(a, VMEM) for a in norms] + [(we, ANY), (be, VMEM)],
        [(shape(wide), ANY)] * 2 + [(shape(narrow), ANY)] * 3,
        [pltpu.VMEM(narrow, BF), pltpu.VMEM(we.shape, BF)]
        + [pltpu.VMEM(wide, BF)] * 2
        + [pltpu.VMEM(narrow, BF)] * 3,
        23,
        0,
    )


def doubled(kv):
    kv = kv.astype(F32)
    swapped = pltpu.roll(kv, 64, 1)
    low = lax.broadcasted_iota(jnp.int32, kv.shape, 1) < 64
    return jnp.where(low, kv, swapped).astype(BF), jnp.where(low, swapped, kv).astype(BF)


def stack_heads(block, heads):
    low = lax.broadcasted_iota(jnp.int32, (block.shape[0], LANES), 1) < 64
    zero = jnp.zeros((block.shape[0], LANES), block.dtype)
    parts = []
    for h in range(heads):
        part = block[:, LANES * (h // 2) : LANES * (h // 2 + 1)]
        parts.append(jnp.where(low, part, zero) if h % 2 == 0 else jnp.where(low, zero, part))
    return jnp.concatenate(parts, 0)


def join_heads(stacked, heads, rows):
    low = lax.broadcasted_iota(jnp.int32, (rows, LANES), 1) < 64
    part = lambda h: stacked[h * rows : (h + 1) * rows]
    zero = jnp.zeros((rows, LANES), stacked.dtype)
    cols = []
    for h in range(0, heads, 2):
        cols.append(jnp.where(low, part(h), part(h + 1) if h + 1 < heads else zero))
    return jnp.concatenate(cols, 1)


def send_rows(copies, rows, mine, send, which):
    places = (mine[0].at[which], send.at[0, which], mine[1].at[which], send.at[1, which])
    return [copies.start(rows.at[r], place) for r, place in enumerate(places)]


def halves_to(copies, halves, micro_id, into, t):
    return [
        copies.start(halves[r // 2].at[micro_id, r % 2], into.at[r ^ t]) for r in range(4)
    ]


def join_weights(wss, wts):
    wts[QW:] = wss[...].T


def project(micro_id, h1s, wts, qbias, sbias, bqkv, cs, sn, saved):
    qrs, kk, vv = saved[:3]
    rows = h1s.shape[1]
    own_q = qbias.shape[0]
    bqkv[:, :own_q] = line(qbias)
    bqkv[:, own_q:QW] = jnp.zeros((1, QW - own_q), F32)
    bqkv[:, QW:] = line(sbias)
    for a in range(4):
        here = slice(a * rows, (a + 1) * rows)
        qkv = dot_nt(h1s[a], wts[...]) + bqkv[...]
        c = spread_table(cs[micro_id, a], 1.0, 1.0)
        s = spread_table(sn[micro_id, a], 0.0, -1.0)
        low = lax.broadcasted_iota(jnp.int32, c.shape, 1) < 64
        cos = jnp.concatenate([c, c, jnp.where(low, c, 1.0)], 1)
        sin = jnp.concatenate([s, s, jnp.where(low, s, 0.0)], 1)
        qkv = qkv * cos + swap_halves(qkv) * sin
        qrs[a] = (qkv[:, :QW] * 0.125).astype(BF)
        kk[here], vv[here] = doubled(qkv[:, QW:].astype(BF))


def attend_rows(micro_id, heads, ends, saved, finished=lambda block: None):
    qrs, kk, vv, cx, *probs_of = saved
    rows = qrs.shape[1]
    spans = [(a + 1) * rows for a in range(4)]
    scores = dot_nt(stack_heads(qrs[3], heads), kk[: spans[3]])
    for a in (3, 2, 1, 0):
        here = scores
        if a > 0:
            scores = dot_nt(stack_heads(qrs[a - 1], heads), kk[: spans[a - 1]])
        row = lax.broadcasted_iota(jnp.int32, (rows, 1), 0) + a * rows
        begin = jnp.zeros((rows, 1), jnp.int32)
        for d in range(ends.shape[2] - 1):
            begin = jnp.where(row >= ends[micro_id, 0, d], ends[micro_id, 0, d], begin)
        col = lax.broadcasted_iota(jnp.int32, (rows, spans[a]), 1)
        allowed = (col >= begin) & (col <= row)
        for h in range(heads):
            mine = slice(h * rows, (h + 1) * rows)
            s = jnp.where(allowed, here[mine], -1e30)
            e = jnp.exp(s - jnp.max(s, -1, keepdims=True))
            probs_of[a][mine] = (e * (1.0 / jnp.sum(e, -1, keepdims=True))).astype(BF)
        done = a + 1
        if done < 4:
            cx[done] = join_heads(dot(probs_of[done][...], vv[: spans[done]]), heads, rows).astype(BF)
            finished(done)
    cx[0] = join_heads(dot(probs_of[0][...], vv[: spans[0]]), heads, rows).astype(BF)


def attend_kernel(micro_id, heads, *refs):
    refs = list(refs)
    take = lambda k: [refs.pop(0) for _ in range(k)]
    t_ref, ends = take(2)
    h1 = take(2)
    wq, ws, qbias, sbias, cs, sn = take(6)
    outs = take(8)
    h1s, wss, wts, bqkv = take(4)
    saved = take(8)
    copies = Copies(take(1)[0])
    got = load_weights(copies, wq, ws, wss, wts)
    got += halves_to(copies, h1, micro_id, h1s, t_ref[0])
    for c in got:
        c.wait()
    join_weights(wss, wts)
    project(micro_id, h1s, wts, qbias, sbias, bqkv, cs, sn, saved)
    sent = [copies.start(saved[i], outs[i]) for i in range(3)]

    def finished(block):
        sent.append(copies.start(saved[4 + block], outs[4 + block]))

    attend_rows(micro_id, heads, ends, saved, finished)
    finished(0)
    sent.append(copies.start(saved[3], outs[3]))
    for c in sent:
        c.wait()


def load_weights(copies, wq, ws, wss, wts):
    own_q = wq.shape[0]
    wts[own_q:QW] = jnp.zeros((QW - own_q, wts.shape[1]), BF)
    return [copies.start(wq, wts.at[pl.ds(0, own_q)]), copies.start(ws, wss)]


def weights_scratch(ws):
    width = QW + LANES
    return [
        pltpu.VMEM(ws.shape, BF), pltpu.VMEM((width, ws.shape[0]), BF), pltpu.VMEM((1, width), F32)
    ]


def saved_shapes(rows, heads):
    length = 4 * rows
    saved = [(4, rows, QW), (length, LANES), (length, LANES), (4, rows, QW)]
    return saved + [(heads * rows, (a + 1) * rows) for a in range(4)]


def attend(micro_id, rank, ends, h1, wq, ws, qbias, sbias, cs, sn, heads, flops):
    _, _, rows, feat = h1[0].shape
    ins = [(rank, SMEM), (ends, SMEM)] + [(a, ANY) for a in (*h1, wq, ws)]
    ins += [(a, VMEM) for a in (qbias, sbias, cs, sn)]
    saved = saved_shapes(rows, heads)
    scratch = [pltpu.VMEM((4, rows, feat), BF)] + weights_scratch(ws)
    return call(
        functools.partial(attend_kernel, micro_id, heads), "attend", ins,
        [(shape(a), ANY) for a in saved], scratch + [pltpu.VMEM(a, BF) for a in saved], 14, flops,
    )


def attend_back_kernel(micro_id, heads, first, whole, *refs):
    refs = list(refs)
    take = lambda k: [refs.pop(0) for _ in range(k)]
    t_ref, me_ref = take(2)
    if whole:
        ends, qbias, sbias = take(3)
    else:
        saved = take(8)
    gpieces = take(4)
    h1, act, du, n = take(2), take(2), take(2), take(2)
    wq, ws, wo, wc, we, gain1, gain2, cs, sn = take(9)
    if not first:
        og_in, qs_in, vec_in, hid_in = take(4)
    rows_kept = take(2)
    rows_sent, = take(1)
    results = take(3 if first else 2)
    gs, h1s, acts, dus, ns, wss, wts, bqkv, wos, wcs, wes = take(11)
    qrs, kk, vv, cx, *probs_of = kept = take(8)
    dctx, = take(1)
    dss = take(2)
    dk, dv, dqkv, outb, eb, ogs, qss = take(7)
    if not first:
        lines, keeps, sends = take(3)
    copies = Copies(take(1)[0])
    rows = gs.shape[1]
    t = t_ref[0]
    spans = [(a + 1) * rows for a in range(4)]
    def load_h():
        return load_weights(copies, wq, ws, wss, wts) + halves_to(copies, h1, micro_id, h1s, t)

    if whole:
        got_h = load_h()
    own_q = wo.shape[0]
    got_g = [copies.start(wo, wos.at[pl.ds(0, own_q)])]
    wos[own_q:] = jnp.zeros((QW - own_q, wo.shape[1]), BF)
    got_g += [copies.start(g.at[micro_id], gs.at[r ^ t]) for r, g in enumerate(gpieces)]
    order = (2, 7, 0, 1, 6, 5, 4, 3)
    got_saved = [] if whole else [copies.start(saved[i], kept[i]) for i in order]
    got_out = halves_to(copies, act, micro_id, acts, 0) + [copies.start(wc, wcs)]
    if not whole:
        got_h = load_h()
    got_e = halves_to(copies, du, micro_id, dus, 0) + [copies.start(we, wes)]
    got_e += halves_to(copies, n, micro_id, ns, 0)
    if not first:
        got_e += [copies.start(og_in, ogs), copies.start(qs_in, qss)]
    if whole:
        for c in got_h:
            c.wait()
        join_weights(wss, wts)
        project(micro_id, h1s, wts, qbias, sbias, bqkv, cs, sn, kept)
        attend_rows(micro_id, heads, ends, kept)
    for c in got_g + (got_out + got_e if whole else []):
        c.wait()
    dctx[...] = dot_nt(gs[...].reshape(4 * rows, gs.shape[2]), wos[...]).astype(BF)
    for c in got_saved:
        c.wait()
    dk[...] = jnp.zeros_like(dk)
    dv[...] = jnp.zeros_like(dv)
    stacked = lambda a: stack_heads(dctx[a * rows : (a + 1) * rows], heads)

    def finish(a):
        dscores = dss[a % 2][:, : spans[a]]
        dk[: spans[a]] += dot_tn(dscores, stack_heads(qrs[a], heads))
        dv[: spans[a]] += dot_tn(probs_of[a][...], stacked(a))
        dq = join_heads(dot(dscores, kk[: spans[a]]), heads, rows) * 0.125
        c = spread_table(cs[micro_id, a], 1.0, 1.0)
        s = spread_table(sn[micro_id, a], 0.0, -1.0)
        cos = jnp.concatenate([c, c], 1)
        sin = jnp.concatenate([s, s], 1)
        dqkv[a, :, :QW] = (dq * cos - swap_halves(dq) * sin).astype(BF)

    dprobs = dot_nt(stacked(3), vv[: spans[3]])
    for a in (3, 2, 1, 0):
        here = dprobs
        if a > 0:
            dprobs = dot_nt(stacked(a - 1), vv[: spans[a - 1]])
        for h in range(heads):
            mine = slice(h * rows, (h + 1) * rows)
            p = probs_of[a][mine].astype(F32)
            weighted = p * here[mine]
            delta = jnp.sum(weighted, -1, keepdims=True)
            dss[a % 2][mine, : spans[a]] = (weighted - p * delta).astype(BF)
        if a < 3:
            finish(a + 1)
    finish(0)
    for a in range(4):
        here = slice(a * rows, (a + 1) * rows)
        c = spread_table(cs[micro_id, a], 1.0, 1.0)
        s = spread_table(sn[micro_id, a], 0.0, -1.0)
        dkf = dk[here] + pltpu.roll(dk[here], 64, 1)
        dvf = dv[here] + pltpu.roll(dv[here], 64, 1)
        dkf = dkf * c - swap_halves(dkf) * s
        low = lax.broadcasted_iota(jnp.int32, dkf.shape, 1) < 64
        dqkv[a, :, QW:] = jnp.where(low, dkf, dvf).astype(BF)
    for c in [] if whole else got_out:
        c.wait()
    for r in range(4):
        outb[r] = (dot(cx[r ^ t], wos[...]) + dot(acts[r], wcs[...])).astype(BF)
    sent = send_rows(copies, outb, rows_kept, rows_sent, 0)

    for c in [] if whole else got_e + got_h:
        c.wait()
    if not whole:
        join_weights(wss, wts)
    width = QW + LANES
    vec_width = gs.shape[2]
    flat = dqkv[...].reshape(4 * rows, width)
    ograd = dot_tn(cx[...].reshape(4 * rows, QW), gs[...].reshape(4 * rows, gs.shape[2]))
    qgrad = dot_tn(flat, h1s[...].reshape(4 * rows, h1s.shape[2]))
    ogs[...] = ograd if first else ogs[...] + ograd
    qss[...] = qgrad if first else qss[...] + qgrad
    if first:
        sent += [copies.start(ogs, results[0]), copies.start(qss, results[1])]
    sums = [jnp.zeros((1, vec_width), F32) for _ in range(4)]
    for r in range(4):
        e1 = dot(dqkv[r ^ t], wts[...])
        e2 = dot_nt(dus[r], wes[...])
        eb[r] = (e1 * line(gain1) + e2 * line(gain2)).astype(BF)
        norm = ns[r].astype(F32)
        for i, term in enumerate((e1 * norm, e1, e2 * norm, e2)):
            sums[i] += jnp.sum(term, 0, keepdims=True)
    sent += send_rows(copies, eb, rows_kept, rows_sent, 1)
    column = jnp.sum(flat.astype(F32), 0, keepdims=True)
    sums.append(jnp.concatenate([column, jnp.zeros((1, vec_width - width), F32)], 1))
    if first:
        results[2][...] = jnp.concatenate(sums + [jnp.zeros((3, vec_width), F32)], 0)
    else:
        sums = [a + vec_in[i : i + 1] for i, a in enumerate(sums)]
        zero = jnp.zeros((5, vec_width), F32)
        lines[...] = jnp.concatenate(
            [hid_in[0:1], hid_in[1:2], sums[4], zero] + sums + [zero[:3]], 0
        )
        pack_parts(ogs, qss, lines, keeps, sends, me_ref[0], heads * 8)
        sent += [copies.start(keeps, results[0]), copies.start(sends, results[1])]
    for c in sent:
        c.wait()


def pack_parts(og, qs, lines, keep, send, me, cut):
    tall = LANES // 8
    for out, order in zip((keep, send), offsets(ACROSS)):
        for i in range(4):
            b = order[i] ^ me
            rows = lambda ref, size, base: ref[pl.ds(pl.multiple_of(b * size + base, 8), size)]
            line = lambda i: jnp.broadcast_to(lines[pl.ds(b + i, 1)], (8, lines.shape[1]))
            own = lax.broadcasted_iota(jnp.int32, (8, lines.shape[1]), 0) < 4
            both = jnp.where(own, line(0), line(8))
            part = [rows(og, cut, 0), rows(qs, cut, 0), rows(qs, tall, QW), both]
            part.append(jnp.zeros((out.shape[1] - 2 * cut - tall - 8, lines.shape[1]), F32))
            out[i] = jnp.concatenate(part, 0).astype(BF)


def attend_back(
    micro_id, rank, me, saved, gs, h1, act, du, n, wq, ws, wo, wc, we, gain1, gain2, cs, sn, heads,
    whole=False, before=None,
):
    _, rows, feat = gs[0].shape
    ff = wc.shape[0]
    width = QW + LANES
    length = 4 * rows
    first = before is None
    ins = [(rank, SMEM), (me, SMEM)]
    ins += [(saved[0], SMEM)] + [(a, VMEM) for a in saved[1:]] if whole else [(a, ANY) for a in saved]
    ins += [(a, ANY) for a in (*gs, *h1, *act, *du, *n, wq, ws, wo, wc, we)]
    ins += [(a, VMEM) for a in (gain1, gain2, cs, sn)]
    if not first:
        ins += [(a, ANY) for a in before[:2]] + [(a, VMEM) for a in before[2:]]
    outs = [(shape((2, rows, feat)), ANY)] * 2 + [(shape((2, 2, rows, feat)), ANY)]
    grads = [shape((QW, feat), F32), shape((width, feat), F32)]
    part = shape((4, PART, feat))
    if first:
        outs += [(g, ANY) for g in grads] + [(shape((8, feat), F32), VMEM)]
    else:
        outs += [(part, ANY)] * 2
    stack, wide = pltpu.VMEM((4, rows, feat), BF), pltpu.VMEM((4, rows, ff), BF)
    scratch = [stack, stack, wide, wide, stack]
    scratch += weights_scratch(ws)
    scratch += [pltpu.VMEM(a, BF) for a in ((QW, feat), wc.shape, we.shape)]
    scratch += [pltpu.VMEM(a, BF) for a in saved_shapes(rows, heads)]
    scratch += [
        pltpu.VMEM((length, QW), BF),
        pltpu.VMEM((heads * rows, length), BF), pltpu.VMEM((heads * rows, length), BF),
        pltpu.VMEM((length, LANES), F32), pltpu.VMEM((length, LANES), F32),
        pltpu.VMEM((4, rows, width), BF), stack, stack,
    ]
    scratch += [pltpu.VMEM(g.shape, F32) for g in grads]
    if not first:
        scratch += [pltpu.VMEM((16, feat), F32)] + [pltpu.VMEM(part.shape, BF)] * 2
    return call(
        functools.partial(attend_back_kernel, micro_id, heads, first, whole), "attend_grad", ins, outs,
        scratch, 46,
    )


def store_parts(total, parts, me, bits):
    part = total.shape[0] // 8
    for b in range(8):
        offset = b ^ me
        place = sum(((offset // bit) % 2) * weight for bit, weight in zip(bits, (4, 2, 1)))
        parts[place] = total[b * part : (b + 1) * part].astype(BF)


def pieces_to(copies, pieces, into):
    return [copies.start(p.at[m], into.at[m, j]) for j, p in enumerate(pieces) for m in range(2)]


def flat(ref):
    return ref[...].reshape(-1, ref.shape[-1])


def hidden_back_kernel(first, *refs):
    refs = list(refs)
    take = lambda k: [refs.pop(0) for _ in range(k)]
    me_ref, = take(1)
    pieces = take(2)
    act, slope, h2, wc = take(4)
    if not first:
        before = take(2)
        sums_in, = take(1)
    duo, = take(1)
    outs = take(2 if first else 4)
    sums, = take(1)
    gs, acts, slopes, wcs, h2s, dus, *accs = take(8)
    parts = None if first else take(2)
    copies = Copies(take(1)[0])
    got = pieces_to(copies, pieces, gs) + [copies.start(act, acts)]
    if not first:
        got_sums = [copies.start(before[0], accs[0])]
    got_back = [copies.start(wc, wcs), copies.start(slope, slopes)]
    got_late = [copies.start(h2, h2s)]
    if not first:
        got_sums.append(copies.start(before[1], accs[1]))

    def total(i, left, right):
        if first:
            accs[i][...] = dot_tn(flat(left), flat(right))
            return [copies.start(accs[i], outs[i])]
        got_sums[i].wait()
        both = accs[i][...] + dot_tn(flat(left), flat(right))
        store_parts(both, parts[i], me_ref[0], (ACROSS, EXPAND)[i])
        return [copies.start(parts[i].at[pl.ds(4 * k, 4)], outs[2 * i + k]) for k in (0, 1)]

    for c in got:
        c.wait()
    sent = total(0, acts, gs)
    for c in got_back:
        c.wait()
    gsum = jnp.zeros((1, gs.shape[3]), F32)
    column = jnp.zeros((1, slopes.shape[3]), F32)
    for m in range(2):
        for j in range(2):
            g = gs[m, j]
            du = (dot_nt(g, wcs[...]) * slopes[m, j].astype(F32)).astype(BF)
            dus[m, j] = du
            gsum += jnp.sum(g.astype(F32), 0, keepdims=True)
            column += jnp.sum(du.astype(F32), 0, keepdims=True)
    sent.append(copies.start(dus, duo))
    for c in got_late:
        c.wait()
    sent += total(1, h2s, dus)
    rowid = lax.broadcasted_iota(jnp.int32, sums.shape, 0)
    both = jnp.where(rowid == 0, gsum, jnp.where(rowid == 1, column, 0.0))
    sums[...] = both if first else sums_in[...] + both
    for c in sent:
        c.wait()


def hidden_back(me, pieces, act, slope, h2, wc, before=None):
    _, _, rows, feat = h2.shape
    ff = wc.shape[0]
    first = before is None
    ins = [(me, SMEM)] + [(a, ANY) for a in (*pieces, act, slope, h2, wc)]
    outs = [(shape(slope.shape), ANY)]
    if first:
        outs += [(shape((ff, feat), F32), ANY), (shape((feat, ff), F32), ANY)]
    else:
        ins += [(before[0], ANY), (before[1], ANY), (before[2], VMEM)]
        outs += [(shape((4, ff // 8, feat)), ANY)] * 2 + [(shape((4, feat // 8, ff)), ANY)] * 2
    outs.append((shape((8, feat), F32), VMEM))
    scratch = [
        pltpu.VMEM(h2.shape, BF), pltpu.VMEM(act.shape, BF), pltpu.VMEM(slope.shape, BF),
        pltpu.VMEM(wc.shape, BF), pltpu.VMEM(h2.shape, BF), pltpu.VMEM(slope.shape, BF),
        pltpu.VMEM((ff, feat), F32), pltpu.VMEM((feat, ff), F32),
    ]
    if not first:
        scratch += [pltpu.VMEM((8, ff // 8, feat), BF), pltpu.VMEM((8, feat // 8, ff), BF)]
    return call(
        functools.partial(hidden_back_kernel, first), "hidden_grad", ins, outs, scratch, 15,
        0 if first else 10**10,
    )


def after(value, *others):
    return lax.optimization_barrier((value, others))[0]


def add(*terms):
    return sum(a.astype(F32) for a in terms).astype(BF)


def swap(value, axis, size, bit):
    return lax.ppermute(value, axis, [(i, i ^ bit) for i in range(size)])


class Order:
    def __init__(self):
        self.last = None

    def __call__(self, value):
        if self.last is not None:
            value = after(value, self.last)
        return value

    def step(self, result):
        self.last = result
        return result


class Sum:
    def __init__(self, order, size, keep, send, bits, back):
        self.order, self.size, self.bits, self.back = order, size, bits, back
        self.have = keep
        self.flying = swap(order(send), "dp", size, bits[0])

    def kept(self):
        have = self.order(self.have)
        halves = add(have[:2], self.flying[:2]), add(have[2:], self.flying[2:])
        self.have, send = self.order.step(halves)
        self.flying = swap(send, "dp", self.size, self.bits[1])

    def near(self):
        have = self.order(self.have)
        halves = add(have[0], self.flying[0]), add(have[1], self.flying[1])
        self.have, send = self.order.step(halves)
        self.flying = swap(send, "dp", self.size, self.bits[2])

    def own(self, over_tp=0):
        self.have = self.order.step(add(self.order(self.have), self.flying))
        if self.size > 8:
            groups = [[low + 8 * high for high in range(self.size // 8)] for low in range(8)]
            whole = lax.psum(self.have.astype(F32), "dp", axis_index_groups=groups)
            self.have = whole.astype(BF)
        if over_tp:
            self.tail = self.have[over_tp:]
            self.sums = [swap(self.tail, "tp", 4, bit) for bit in (1, 2, 3)]
        else:
            self.flying = swap(self.have, "dp", self.size, self.back[2])

    def over_tp(self, first):
        tail = self.order(self.tail)
        row = lax.broadcasted_iota(jnp.int32, tail.shape, 0) - LANES // 8
        whole = jnp.where((row >= 0) & (row < 4), tail, add(tail, *self.sums))
        self.have = self.order.step(jnp.concatenate([self.have[:first], whole], 0))
        self.flying = swap(self.have, "dp", self.size, self.back[2])

    def pair(self):
        self.have = self.order.step(jnp.stack([self.order(self.have), self.flying]))
        self.flying = swap(self.have, "dp", self.size, self.back[1])

    def four(self):
        self.have = self.order.step(jnp.concatenate([self.order(self.have), self.flying], 0))
        self.flying = swap(self.have, "dp", self.size, self.back[0])

    def parts(self):
        return self.have, self.flying


def halve_kernel(*refs):
    values, outs, held, sums, sems = refs[:4], refs[4:8], refs[8:12], refs[12:14], refs[14]
    copies = Copies(sems)
    got = [copies.start(a, b) for a, b in zip(values, held)]
    sent = []
    for i in range(2):
        got[2 * i].wait()
        got[2 * i + 1].wait()
        sums[i][...] = (held[2 * i][...].astype(F32) + held[2 * i + 1][...].astype(F32)).astype(BF)
        for k in range(2):
            sent.append(copies.start(sums[i].at[pl.ds(2 * k, 2)], outs[2 * i + k]))
    for c in sent:
        c.wait()


def kept_both(order, first, second):
    values = order((first.have, first.flying, second.have, second.flying))
    outs = [shape((2, *a.shape[1:])) for a in values]
    scratch = [pltpu.VMEM(a.shape, BF) for a in values]
    halves = call(
        halve_kernel, "halve", [(a, ANY) for a in values], [(o, ANY) for o in outs],
        scratch + [scratch[0], scratch[2]], 8, 0,
    )
    order.step(halves)
    for one, (stay, leave) in ((first, halves[:2]), (second, halves[2:])):
        one.have = stay
        one.flying = swap(leave, "dp", one.size, one.bits[1])


class Rows:
    def __init__(self, order, mine, send):
        self.order, self.mine = order, mine
        self.got = swap(order(send), "tp", 4, 1)

    def away(self):
        away = self.order.step(add(self.order(self.mine[1]), self.got[1]))
        self.far = swap(away, "tp", 4, 2)

    def land(self):
        terms = self.order(self.mine[0]), self.got[0], self.far
        self.total = self.order.step(sum(a.astype(F32) for a in terms))


def place_kernel(me_ref, four, other, out):
    i = pl.program_id(0)

    @pl.when(i < 4)
    def _():
        out[...] = four[0].astype(F32)

    @pl.when(i >= 4)
    def _():
        out[...] = other[0].astype(F32)


def place(me, four, other, bits):
    _, part, width = four.shape

    def where(i, me):
        j = i % 4
        order = (j // 2) * bits[1] + (j % 2) * bits[2] + (i // 4) * bits[0]
        return order ^ me[0], 0

    return pl.pallas_call(
        place_kernel,
        grid_spec=pltpu.PrefetchScalarGridSpec(
            num_scalar_prefetch=1,
            grid=(8,),
            in_specs=[
                pl.BlockSpec((1, part, width), lambda i, me: (jnp.minimum(i, 3), 0, 0)),
                pl.BlockSpec((1, part, width), lambda i, me: (jnp.maximum(i - 4, 0), 0, 0)),
            ],
            out_specs=pl.BlockSpec((part, width), where),
        ),
        out_shape=shape((8 * part, width), F32),
        compiler_params=pltpu.CompilerParams(vmem_limit_bytes=32 * 2**20),
        cost_estimate=pl.CostEstimate(flops=0, bytes_accessed=0, transcendentals=0),
        name="place_parts",
    )(me, four, other)


def unpack_kernel(own_q, me_ref, four, other, og, qs, sg, *refs):
    *vectors, shared, lines = refs
    me = me_ref[0]
    cut = own_q // 8
    tall = LANES // 8
    for ref, order in zip((four, other), offsets(ACROSS)):
        for i in range(4):
            b = order[i] ^ me
            part = ref[i].astype(F32)
            rows = lambda size: pl.ds(pl.multiple_of(b * size, 8), size)
            og[rows(cut)] = part[:cut]
            qs[rows(cut)] = part[cut : 2 * cut]
            shared[rows(tall)] = part[2 * cut : 2 * cut + tall]
            last = part[2 * cut + tall : 2 * cut + tall + 8]
            lines[pl.ds(b, 1)] = last[:1]
            lines[pl.ds(b + 8, 1)] = last[4:5]
    sg[...] = shared[...].T
    for ref, (i, base) in zip(vectors, LINES):
        ref[...] = lines[i, base : base + ref.shape[0]]


def unpack(me, four, other, own_q, ff):
    feat = four.shape[2]
    sizes = (feat, ff, own_q, feat, feat, feat, feat, LANES)
    outs = [(own_q, feat), (own_q, feat), (feat, LANES)] + [(n,) for n in sizes]
    return pl.pallas_call(
        functools.partial(unpack_kernel, own_q),
        in_specs=[SMEM, VMEM, VMEM],
        out_specs=[VMEM] * len(outs),
        out_shape=[shape(a, F32) for a in outs],
        scratch_shapes=[pltpu.VMEM((LANES, feat), F32), pltpu.VMEM((16, feat), F32)],
        compiler_params=pltpu.CompilerParams(vmem_limit_bytes=32 * 2**20),
        cost_estimate=pl.CostEstimate(flops=0, bytes_accessed=0, transcendentals=0),
        name="unpack",
    )(me, four, other)


def doc_layout(ends, scales, length):
    row = jnp.arange(length, dtype=jnp.int32)[None]
    begin = jnp.zeros_like(row)
    step = scales[:, :1]
    for d in range(ends.shape[1] - 1):
        past = row >= ends[:, d : d + 1]
        begin = jnp.where(past, ends[:, d : d + 1], begin)
        step = jnp.where(past, scales[:, d + 1 : d + 2], step)
    return (row - begin) * step


def angle_tables(placed, rows):
    freqs = 10000.0 ** (-jnp.arange(ROT // 2, dtype=F32) * 2.0 / ROT)
    blocks = placed.astype(F32).reshape(placed.shape[0], 4, 1, rows)
    angles = blocks * freqs[:, None]
    return jnp.cos(angles), jnp.sin(angles)


def on_device(
    size,
    tokens,
    cotangent,
    doc_ends,
    pos_scale,
    first_gain,
    first_bias,
    second_gain,
    second_bias,
    w_query,
    query_bias,
    w_shared,
    shared_bias,
    w_output,
    w_expand,
    expand_bias,
    w_contract,
    output_bias,
):
    micro, rows, feat = tokens.shape
    heads = w_query.shape[1] // 64
    own_q = w_query.shape[1]
    length = rows * 4
    rank = lax.axis_index("tp").astype(jnp.int32)[None]
    me = (lax.axis_index("dp").astype(jnp.int32) & 7)[None]

    order = Order()

    def begin(values):
        return values, swap(values, "tp", 4, 1), swap(values, "tp", 4, 2)

    def finish(own, near, far):
        return own, near, far, swap(far, "tp", 4, 1)

    xs, gs = begin(tokens), begin(cotangent)

    norms = (first_gain, first_bias, second_gain, second_bias)
    ends, scales = doc_ends[:, 0], pos_scale[:, 0]
    cs, sn = angle_tables(doc_layout(ends, scales, length), rows)

    act_a, slope_a, h1_a, h2_a, n_a = hidden(xs[:2], norms, w_expand, expand_bias)
    order.step(act_a)
    du_a, cacc, eacc, sums = hidden_back(order(me), gs[:2], act_a, slope_a, h2_a, w_contract)
    order.step(sums)
    xs = finish(xs[0], xs[1], order(xs[2]))
    act_b, slope_b, h1_b, h2_b, n_b = hidden(xs[2:], norms, w_expand, expand_bias)
    order.step(act_b)
    h1, n, act = (h1_a, h1_b), (n_a, n_b), (act_a, act_b)
    biases = (query_bias, shared_bias)
    saved0 = attend(
        0, order(rank), doc_ends, h1, w_query.T, w_shared, *biases, cs, sn, heads, 0
    )
    order.step(saved0[0])
    gs = finish(gs[0], gs[1], order(gs[2]))
    du_b, c_keep, c_send, e_keep, e_send, sums = hidden_back(
        order(me), gs[2:], act_b, slope_b, h2_b, w_contract, (cacc, eacc, sums)
    )
    order.step(sums)
    weights = (w_query.T, w_shared, w_output, w_contract, w_expand, first_gain, second_gain)
    inputs = (gs, h1, act, (du_a, du_b), n, *weights, cs, sn, heads)
    c = Sum(order, size, c_keep, c_send, ACROSS, ACROSS)
    e = Sum(order, size, e_keep, e_send, EXPAND, BACK)
    *mine0, send0, og, qs, vec = attend_back(0, order(rank), me, saved0, *inputs)
    order.step(vec)
    kept_both(order, c, e)
    rows0 = Rows(order, mine0, send0)
    *mine1, send1, r_keep, r_send = attend_back(
        1, order(rank), me, (doc_ends, *biases), *inputs, True, (og, qs, vec, sums)
    )
    order.step(r_send)
    rest = Sum(order, size, r_keep, r_send, ACROSS, ACROSS)
    c.near()
    rows0.away()
    rows1 = Rows(order, mine1, send1)
    e.near()
    rest.kept()
    c.own()
    rest.near()
    e.own()
    c.pair()
    rest.own(2 * (own_q // 8))
    rest.over_tp(2 * (own_q // 8))
    e.pair()
    rows0.land()
    rows1.away()
    c.four()
    rest.pair()
    e.four()
    contract_grad = order.step(place(order(me), *c.parts(), ACROSS))
    rest.four()
    rows1.land()
    layer_out, input_grad = order.step(
        final_rows(order(tokens), cotangent, output_bias, (rows0.total, rows1.total))
    )
    expand_grad = order.step(place(order(me), *e.parts(), BACK))
    output_grad, query_grad, shared_grad, *vectors = unpack(
        me, *rest.parts(), own_q, expand_bias.shape[0]
    )
    out_bias, hidden_bias, query_bias, gain1, bias1, gain2, bias2, kv_bias = vectors

    return (
        layer_out,
        input_grad,
        query_grad.T,
        query_bias,
        shared_grad,
        kv_bias,
        output_grad,
        expand_grad,
        hidden_bias,
        contract_grad,
        out_bias,
        gain1,
        bias1,
        gain2,
        bias2,
    )


def final_rows(tokens, cotangent, output_bias, terms):
    joined = lambda which: jnp.stack([t[which] for t in terms])
    x = tokens.astype(F32)
    layer_out = (x + joined(0) + output_bias).astype(BF)
    norm, scale = normalize_rows(x)
    e = joined(1)
    slope_mean = jnp.mean(e * norm, -1, keepdims=True)
    input_grad = cotangent.astype(F32) + scale * (
        e - jnp.mean(e, -1, keepdims=True) - norm * slope_mean
    )
    return layer_out, input_grad


def normalize_rows(x):
    centre = x - jnp.mean(x, -1, keepdims=True)
    scale = lax.rsqrt(jnp.mean(centre * centre, -1, keepdims=True) + 1e-05)
    return centre * scale, scale


def solution(mesh):
    rows = P(None, ("dp", "tp"), None)
    in_specs = (
        rows, rows, P(None, "dp", None), P(None, "dp", None),
        P(), P(), P(), P(),
        P(None, "tp"), P("tp"), P(), P(), P("tp", None),
        P(None, "tp"), P("tp"), P("tp", None), P(),
    )
    out_specs = (
        rows, rows,
        P(None, "tp"), P("tp"), P(), P(), P("tp", None),
        P(None, "tp"), P("tp"), P("tp", None),
        P(), P(), P(), P(), P(),
    )
    return jax.shard_map(
        functools.partial(on_device, mesh.shape["dp"]),
        mesh=mesh,
        in_specs=in_specs,
        out_specs=out_specs,
        check_vma=False,
    )
```

```python
import functools

import jax
import jax.numpy as jnp
from jax import lax
from jax.experimental import pallas as pl
from jax.experimental.pallas import tpu as pltpu
from jax.sharding import PartitionSpec as P

ROT = 16
LANES = 128
QW = 256
PART = 80
LINES = ((0, 0), (1, 0), (2, 0), (8, 0), (9, 0), (10, 0), (11, 0), (12, QW))
BF = jnp.bfloat16
F32 = jnp.float32
ACROSS = (1, 2, 4)
ALONG = (2, 4, 1)
EXPAND = ALONG
BACK = ALONG
NT = (((1,), (1,)), ((), ()))
TN = (((0,), (0,)), ((), ()))
ANY = pl.BlockSpec(memory_space=pl.ANY)
VMEM = pl.BlockSpec(memory_space=pltpu.VMEM)
SMEM = pl.BlockSpec(memory_space=pltpu.SMEM)


def dot(a, b):
    return jnp.dot(a, b, preferred_element_type=F32)


def dot_nt(a, b):
    return lax.dot_general(a, b, NT, preferred_element_type=F32)


def dot_tn(a, b):
    return lax.dot_general(a, b, TN, preferred_element_type=F32)


def shape(dims, dtype=BF):
    return jax.ShapeDtypeStruct(dims, dtype)


def call(kernel, name, ins, outs, scratch, copies, flops=10**10):
    specs = [s for _, s in ins]
    arrays = [a for a, _ in ins]
    return pl.pallas_call(
        kernel,
        in_specs=specs,
        out_specs=[s for _, s in outs],
        out_shape=[o for o, _ in outs],
        scratch_shapes=list(scratch) + [pltpu.SemaphoreType.DMA((copies,))],
        compiler_params=pltpu.CompilerParams(vmem_limit_bytes=64 * 2**20 - 65536),
        cost_estimate=pl.CostEstimate(flops=flops, bytes_accessed=0, transcendentals=0),
        name=name,
    )(*arrays)


def offsets(bits):
    keep = (0, bits[2], bits[1], bits[1] | bits[2])
    return keep, tuple(k ^ bits[0] for k in keep)


class Copies:
    def __init__(self, sems):
        self.sems = sems
        self.count = 0

    def start(self, src, dst):
        copy = pltpu.make_async_copy(src, dst, self.sems.at[self.count])
        self.count += 1
        copy.start()
        return copy


def normalize(x):
    centre = x - jnp.mean(x, -1, keepdims=True)
    spread = jnp.mean(centre * centre, -1, keepdims=True)
    return centre * lax.rsqrt(spread + 1e-05)


def line(ref):
    return ref[...].reshape(1, -1)


def swap_halves(w):
    lane = lax.broadcasted_iota(jnp.int32, w.shape, 1)
    up = pltpu.roll(w, w.shape[1] - ROT // 2, 1)
    down = pltpu.roll(w, ROT // 2, 1)
    return jnp.where((lane % 64) < ROT // 2, up, down)


def spread_table(compact, filler, signs):
    fill = jnp.full((64 - ROT, compact.shape[1]), filler, F32)
    head = [signs * compact, compact, fill]
    return jnp.concatenate(head + head, 0).T


def hidden_kernel(
    pa, pb, gain1, bias1, gain2, bias2, we, be, acto, slopeo, h1o, h2o, no, xs, wev, acts, slopes, h1s, h2s, ns, sems
):
    copies = Copies(sems)
    got = [copies.start(pa, xs.at[0])]
    gotw = copies.start(we, wev)
    got.append(copies.start(pb, xs.at[1]))
    out = []
    for j in range(2):
        got[j].wait()
        for m in range(2):
            n = normalize(xs[j, m].astype(F32))
            ns[m, j] = n.astype(BF)
            h1s[m, j] = (n * line(gain1) + line(bias1)).astype(BF)
            h2 = (n * line(gain2) + line(bias2)).astype(BF)
            h2s[m, j] = h2
            for a, b in ((ns, no), (h1s, h1o), (h2s, h2o)):
                out.append(copies.start(a.at[m, j], b.at[m, j]))
            if j == 0 and m == 0:
                gotw.wait()
            u = dot(h2, wev[...]) + line(be)
            phi = 0.5 * (1.0 + lax.erf(u * 0.7071067811865476))
            acts[m, j] = (u * phi).astype(BF)
            slopes[m, j] = (phi + u * jnp.exp(-0.5 * u * u) * 0.3989422804014327).astype(BF)
            for a, b in ((acts, acto), (slopes, slopeo)):
                out.append(copies.start(a.at[m, j], b.at[m, j]))
    for c in out:
        c.wait()


def hidden(pieces, norms, we, be):
    _, rows, feat = pieces[0].shape
    ff = we.shape[1]
    wide, narrow = (2, 2, rows, ff), (2, 2, rows, feat)
    return call(
        hidden_kernel,
        "hidden",
        [(x, ANY) for x in pieces] + [(a, VMEM) for a in norms] + [(we, ANY), (be, VMEM)],
        [(shape(wide), ANY)] * 2 + [(shape(narrow), ANY)] * 3,
        [pltpu.VMEM(narrow, BF), pltpu.VMEM(we.shape, BF)]
        + [pltpu.VMEM(wide, BF)] * 2
        + [pltpu.VMEM(narrow, BF)] * 3,
        23,
        0,
    )


def doubled(kv):
    kv = kv.astype(F32)
    swapped = pltpu.roll(kv, 64, 1)
    low = lax.broadcasted_iota(jnp.int32, kv.shape, 1) < 64
    return jnp.where(low, kv, swapped).astype(BF), jnp.where(low, swapped, kv).astype(BF)


def stack_heads(block, heads):
    low = lax.broadcasted_iota(jnp.int32, (block.shape[0], LANES), 1) < 64
    zero = jnp.zeros((block.shape[0], LANES), block.dtype)
    parts = []
    for h in range(heads):
        part = block[:, LANES * (h // 2) : LANES * (h // 2 + 1)]
        parts.append(jnp.where(low, part, zero) if h % 2 == 0 else jnp.where(low, zero, part))
    return jnp.concatenate(parts, 0)


def join_heads(stacked, heads, rows):
    low = lax.broadcasted_iota(jnp.int32, (rows, LANES), 1) < 64
    part = lambda h: stacked[h * rows : (h + 1) * rows]
    zero = jnp.zeros((rows, LANES), stacked.dtype)
    cols = []
    for h in range(0, heads, 2):
        cols.append(jnp.where(low, part(h), part(h + 1) if h + 1 < heads else zero))
    return jnp.concatenate(cols, 1)


def send_rows(copies, rows, mine, send, which):
    places = (mine[0].at[which], send.at[0, which], mine[1].at[which], send.at[1, which])
    return [copies.start(rows.at[r], place) for r, place in enumerate(places)]


def halves_to(copies, halves, micro_id, into, t):
    return [
        copies.start(halves[r // 2].at[micro_id, r % 2], into.at[r ^ t]) for r in range(4)
    ]


def join_weights(wss, wts):
    wts[QW:] = wss[...].T


def project(micro_id, h1s, wts, qbias, sbias, bqkv, cs, sn, saved):
    qrs, kk, vv = saved[:3]
    rows = h1s.shape[1]
    own_q = qbias.shape[0]
    bqkv[:, :own_q] = line(qbias)
    bqkv[:, own_q:QW] = jnp.zeros((1, QW - own_q), F32)
    bqkv[:, QW:] = line(sbias)
    for a in range(4):
        here = slice(a * rows, (a + 1) * rows)
        qkv = dot_nt(h1s[a], wts[...]) + bqkv[...]
        c = spread_table(cs[micro_id, a], 1.0, 1.0)
        s = spread_table(sn[micro_id, a], 0.0, -1.0)
        low = lax.broadcasted_iota(jnp.int32, c.shape, 1) < 64
        cos = jnp.concatenate([c, c, jnp.where(low, c, 1.0)], 1)
        sin = jnp.concatenate([s, s, jnp.where(low, s, 0.0)], 1)
        qkv = qkv * cos + swap_halves(qkv) * sin
        qrs[a] = (qkv[:, :QW] * 0.125).astype(BF)
        kk[here], vv[here] = doubled(qkv[:, QW:].astype(BF))


def attend_rows(micro_id, heads, ends, saved, finished=lambda block: None):
    qrs, kk, vv, cx, *probs_of = saved
    rows = qrs.shape[1]
    spans = [(a + 1) * rows for a in range(4)]
    scores = dot_nt(stack_heads(qrs[3], heads), kk[: spans[3]])
    for a in (3, 2, 1, 0):
        here = scores
        if a > 0:
            scores = dot_nt(stack_heads(qrs[a - 1], heads), kk[: spans[a - 1]])
        row = lax.broadcasted_iota(jnp.int32, (rows, 1), 0) + a * rows
        begin = jnp.zeros((rows, 1), jnp.int32)
        for d in range(ends.shape[2] - 1):
            begin = jnp.where(row >= ends[micro_id, 0, d], ends[micro_id, 0, d], begin)
        col = lax.broadcasted_iota(jnp.int32, (rows, spans[a]), 1)
        allowed = (col >= begin) & (col <= row)
        for h in range(heads):
            mine = slice(h * rows, (h + 1) * rows)
            s = jnp.where(allowed, here[mine], -1e30)
            e = jnp.exp(s - jnp.max(s, -1, keepdims=True))
            probs_of[a][mine] = (e * (1.0 / jnp.sum(e, -1, keepdims=True))).astype(BF)
        done = a + 1
        if done < 4:
            cx[done] = join_heads(dot(probs_of[done][...], vv[: spans[done]]), heads, rows).astype(BF)
            finished(done)
    cx[0] = join_heads(dot(probs_of[0][...], vv[: spans[0]]), heads, rows).astype(BF)


def attend_kernel(micro_id, heads, *refs):
    refs = list(refs)
    take = lambda k: [refs.pop(0) for _ in range(k)]
    t_ref, ends = take(2)
    h1 = take(2)
    wq, ws, qbias, sbias, cs, sn = take(6)
    outs = take(8)
    h1s, wss, wts, bqkv = take(4)
    saved = take(8)
    copies = Copies(take(1)[0])
    got = load_weights(copies, wq, ws, wss, wts)
    got += halves_to(copies, h1, micro_id, h1s, t_ref[0])
    for c in got:
        c.wait()
    join_weights(wss, wts)
    project(micro_id, h1s, wts, qbias, sbias, bqkv, cs, sn, saved)
    sent = [copies.start(saved[i], outs[i]) for i in range(3)]

    def finished(block):
        sent.append(copies.start(saved[4 + block], outs[4 + block]))

    attend_rows(micro_id, heads, ends, saved, finished)
    finished(0)
    sent.append(copies.start(saved[3], outs[3]))
    for c in sent:
        c.wait()


def load_weights(copies, wq, ws, wss, wts):
    own_q = wq.shape[0]
    wts[own_q:QW] = jnp.zeros((QW - own_q, wts.shape[1]), BF)
    return [copies.start(wq, wts.at[pl.ds(0, own_q)]), copies.start(ws, wss)]


def weights_scratch(ws):
    width = QW + LANES
    return [
        pltpu.VMEM(ws.shape, BF), pltpu.VMEM((width, ws.shape[0]), BF), pltpu.VMEM((1, width), F32)
    ]


def saved_shapes(rows, heads):
    length = 4 * rows
    saved = [(4, rows, QW), (length, LANES), (length, LANES), (4, rows, QW)]
    return saved + [(heads * rows, (a + 1) * rows) for a in range(4)]


def attend(micro_id, rank, ends, h1, wq, ws, qbias, sbias, cs, sn, heads, flops):
    _, _, rows, feat = h1[0].shape
    ins = [(rank, SMEM), (ends, SMEM)] + [(a, ANY) for a in (*h1, wq, ws)]
    ins += [(a, VMEM) for a in (qbias, sbias, cs, sn)]
    saved = saved_shapes(rows, heads)
    scratch = [pltpu.VMEM((4, rows, feat), BF)] + weights_scratch(ws)
    return call(
        functools.partial(attend_kernel, micro_id, heads), "attend", ins,
        [(shape(a), ANY) for a in saved], scratch + [pltpu.VMEM(a, BF) for a in saved], 14, flops,
    )


def attend_back_kernel(micro_id, heads, first, whole, *refs):
    refs = list(refs)
    take = lambda k: [refs.pop(0) for _ in range(k)]
    t_ref, me_ref = take(2)
    if whole:
        ends, qbias, sbias = take(3)
    else:
        saved = take(8)
    gpieces = take(4)
    h1, act, du, n = take(2), take(2), take(2), take(2)
    wq, ws, wo, wc, we, gain1, gain2, cs, sn = take(9)
    if not first:
        og_in, qs_in, vec_in, hid_in = take(4)
    rows_kept = take(2)
    rows_sent, = take(1)
    results = take(3 if first else 2)
    gs, h1s, acts, dus, ns, wss, wts, bqkv, wos, wcs, wes = take(11)
    qrs, kk, vv, cx, *probs_of = kept = take(8)
    dctx, = take(1)
    dss = take(2)
    dk, dv, dqkv, outb, eb, ogs, qss = take(7)
    if not first:
        lines, keeps, sends = take(3)
    copies = Copies(take(1)[0])
    rows = gs.shape[1]
    t = t_ref[0]
    spans = [(a + 1) * rows for a in range(4)]
    def load_h():
        return load_weights(copies, wq, ws, wss, wts) + halves_to(copies, h1, micro_id, h1s, t)

    if whole:
        got_h = load_h()
    own_q = wo.shape[0]
    got_g = [copies.start(wo, wos.at[pl.ds(0, own_q)])]
    wos[own_q:] = jnp.zeros((QW - own_q, wo.shape[1]), BF)
    got_g += [copies.start(g.at[micro_id], gs.at[r ^ t]) for r, g in enumerate(gpieces)]
    order = (2, 7, 0, 1, 6, 5, 4, 3)
    got_saved = [] if whole else [copies.start(saved[i], kept[i]) for i in order]
    got_out = halves_to(copies, act, micro_id, acts, 0) + [copies.start(wc, wcs)]
    if not whole:
        got_h = load_h()
    got_e = halves_to(copies, du, micro_id, dus, 0) + [copies.start(we, wes)]
    got_e += halves_to(copies, n, micro_id, ns, 0)
    if not first:
        got_e += [copies.start(og_in, ogs), copies.start(qs_in, qss)]
    if whole:
        for c in got_h:
            c.wait()
        join_weights(wss, wts)
        project(micro_id, h1s, wts, qbias, sbias, bqkv, cs, sn, kept)
        attend_rows(micro_id, heads, ends, kept)
    for c in got_g + (got_out + got_e if whole else []):
        c.wait()
    dctx[...] = dot_nt(gs[...].reshape(4 * rows, gs.shape[2]), wos[...]).astype(BF)
    for c in got_saved:
        c.wait()
    dk[...] = jnp.zeros_like(dk)
    dv[...] = jnp.zeros_like(dv)
    stacked = lambda a: stack_heads(dctx[a * rows : (a + 1) * rows], heads)

    def finish(a):
        dscores = dss[a % 2][:, : spans[a]]
        dk[: spans[a]] += dot_tn(dscores, stack_heads(qrs[a], heads))
        dv[: spans[a]] += dot_tn(probs_of[a][...], stacked(a))
        dq = join_heads(dot(dscores, kk[: spans[a]]), heads, rows) * 0.125
        c = spread_table(cs[micro_id, a], 1.0, 1.0)
        s = spread_table(sn[micro_id, a], 0.0, -1.0)
        cos = jnp.concatenate([c, c], 1)
        sin = jnp.concatenate([s, s], 1)
        dqkv[a, :, :QW] = (dq * cos - swap_halves(dq) * sin).astype(BF)

    dprobs = dot_nt(stacked(3), vv[: spans[3]])
    for a in (3, 2, 1, 0):
        here = dprobs
        if a > 0:
            dprobs = dot_nt(stacked(a - 1), vv[: spans[a - 1]])
        for h in range(heads):
            mine = slice(h * rows, (h + 1) * rows)
            p = probs_of[a][mine].astype(F32)
            weighted = p * here[mine]
            delta = jnp.sum(weighted, -1, keepdims=True)
            dss[a % 2][mine, : spans[a]] = (weighted - p * delta).astype(BF)
        if a < 3:
            finish(a + 1)
    finish(0)
    for a in range(4):
        here = slice(a * rows, (a + 1) * rows)
        c = spread_table(cs[micro_id, a], 1.0, 1.0)
        s = spread_table(sn[micro_id, a], 0.0, -1.0)
        dkf = dk[here] + pltpu.roll(dk[here], 64, 1)
        dvf = dv[here] + pltpu.roll(dv[here], 64, 1)
        dkf = dkf * c - swap_halves(dkf) * s
        low = lax.broadcasted_iota(jnp.int32, dkf.shape, 1) < 64
        dqkv[a, :, QW:] = jnp.where(low, dkf, dvf).astype(BF)
    for c in [] if whole else got_out:
        c.wait()
    for r in range(4):
        outb[r] = (dot(cx[r ^ t], wos[...]) + dot(acts[r], wcs[...])).astype(BF)
    sent = send_rows(copies, outb, rows_kept, rows_sent, 0)

    for c in [] if whole else got_e + got_h:
        c.wait()
    if not whole:
        join_weights(wss, wts)
    width = QW + LANES
    vec_width = gs.shape[2]
    flat = dqkv[...].reshape(4 * rows, width)
    ograd = dot_tn(cx[...].reshape(4 * rows, QW), gs[...].reshape(4 * rows, gs.shape[2]))
    qgrad = dot_tn(flat, h1s[...].reshape(4 * rows, h1s.shape[2]))
    ogs[...] = ograd if first else ogs[...] + ograd
    qss[...] = qgrad if first else qss[...] + qgrad
    if first:
        sent += [copies.start(ogs, results[0]), copies.start(qss, results[1])]
    sums = [jnp.zeros((1, vec_width), F32) for _ in range(4)]
    for r in range(4):
        e1 = dot(dqkv[r ^ t], wts[...])
        e2 = dot_nt(dus[r], wes[...])
        eb[r] = (e1 * line(gain1) + e2 * line(gain2)).astype(BF)
        norm = ns[r].astype(F32)
        for i, term in enumerate((e1 * norm, e1, e2 * norm, e2)):
            sums[i] += jnp.sum(term, 0, keepdims=True)
    sent += send_rows(copies, eb, rows_kept, rows_sent, 1)
    column = jnp.sum(flat.astype(F32), 0, keepdims=True)
    sums.append(jnp.concatenate([column, jnp.zeros((1, vec_width - width), F32)], 1))
    if first:
        results[2][...] = jnp.concatenate(sums + [jnp.zeros((3, vec_width), F32)], 0)
    else:
        sums = [a + vec_in[i : i + 1] for i, a in enumerate(sums)]
        zero = jnp.zeros((5, vec_width), F32)
        lines[...] = jnp.concatenate(
            [hid_in[0:1], hid_in[1:2], sums[4], zero] + sums + [zero[:3]], 0
        )
        pack_parts(ogs, qss, lines, keeps, sends, me_ref[0], heads * 8)
        sent += [copies.start(keeps, results[0]), copies.start(sends, results[1])]
    for c in sent:
        c.wait()


def pack_parts(og, qs, lines, keep, send, me, cut):
    tall = LANES // 8
    for out, order in zip((keep, send), offsets(ACROSS)):
        for i in range(4):
            b = order[i] ^ me
            rows = lambda ref, size, base: ref[pl.ds(pl.multiple_of(b * size + base, 8), size)]
            line = lambda i: jnp.broadcast_to(lines[pl.ds(b + i, 1)], (8, lines.shape[1]))
            own = lax.broadcasted_iota(jnp.int32, (8, lines.shape[1]), 0) < 4
            both = jnp.where(own, line(0), line(8))
            part = [rows(og, cut, 0), rows(qs, cut, 0), rows(qs, tall, QW), both]
            part.append(jnp.zeros((out.shape[1] - 2 * cut - tall - 8, lines.shape[1]), F32))
            out[i] = jnp.concatenate(part, 0).astype(BF)


def attend_back(
    micro_id, rank, me, saved, gs, h1, act, du, n, wq, ws, wo, wc, we, gain1, gain2, cs, sn, heads,
    whole=False, before=None,
):
    _, rows, feat = gs[0].shape
    ff = wc.shape[0]
    width = QW + LANES
    length = 4 * rows
    first = before is None
    ins = [(rank, SMEM), (me, SMEM)]
    ins += [(saved[0], SMEM)] + [(a, VMEM) for a in saved[1:]] if whole else [(a, ANY) for a in saved]
    ins += [(a, ANY) for a in (*gs, *h1, *act, *du, *n, wq, ws, wo, wc, we)]
    ins += [(a, VMEM) for a in (gain1, gain2, cs, sn)]
    if not first:
        ins += [(a, ANY) for a in before[:2]] + [(a, VMEM) for a in before[2:]]
    outs = [(shape((2, rows, feat)), ANY)] * 2 + [(shape((2, 2, rows, feat)), ANY)]
    grads = [shape((QW, feat), F32), shape((width, feat), F32)]
    part = shape((4, PART, feat))
    if first:
        outs += [(g, ANY) for g in grads] + [(shape((8, feat), F32), VMEM)]
    else:
        outs += [(part, ANY)] * 2
    stack, wide = pltpu.VMEM((4, rows, feat), BF), pltpu.VMEM((4, rows, ff), BF)
    scratch = [stack, stack, wide, wide, stack]
    scratch += weights_scratch(ws)
    scratch += [pltpu.VMEM(a, BF) for a in ((QW, feat), wc.shape, we.shape)]
    scratch += [pltpu.VMEM(a, BF) for a in saved_shapes(rows, heads)]
    scratch += [
        pltpu.VMEM((length, QW), BF),
        pltpu.VMEM((heads * rows, length), BF), pltpu.VMEM((heads * rows, length), BF),
        pltpu.VMEM((length, LANES), F32), pltpu.VMEM((length, LANES), F32),
        pltpu.VMEM((4, rows, width), BF), stack, stack,
    ]
    scratch += [pltpu.VMEM(g.shape, F32) for g in grads]
    if not first:
        scratch += [pltpu.VMEM((16, feat), F32)] + [pltpu.VMEM(part.shape, BF)] * 2
    return call(
        functools.partial(attend_back_kernel, micro_id, heads, first, whole), "attend_grad", ins, outs,
        scratch, 46,
    )


def store_parts(total, parts, me, bits):
    part = total.shape[0] // 8
    for b in range(8):
        offset = b ^ me
        place = sum(((offset // bit) % 2) * weight for bit, weight in zip(bits, (4, 2, 1)))
        parts[place] = total[b * part : (b + 1) * part].astype(BF)


def pieces_to(copies, pieces, into):
    return [copies.start(p.at[m], into.at[m, j]) for j, p in enumerate(pieces) for m in range(2)]


def flat(ref):
    return ref[...].reshape(-1, ref.shape[-1])


def hidden_back_kernel(first, *refs):
    refs = list(refs)
    take = lambda k: [refs.pop(0) for _ in range(k)]
    me_ref, = take(1)
    pieces = take(2)
    act, slope, h2, wc = take(4)
    if not first:
        before = take(2)
        sums_in, = take(1)
    duo, = take(1)
    outs = take(2 if first else 4)
    sums, = take(1)
    gs, acts, slopes, wcs, h2s, dus, *accs = take(8)
    parts = None if first else take(2)
    copies = Copies(take(1)[0])
    got = pieces_to(copies, pieces, gs) + [copies.start(act, acts)]
    if not first:
        got_sums = [copies.start(before[0], accs[0])]
    got_back = [copies.start(wc, wcs), copies.start(slope, slopes)]
    got_late = [copies.start(h2, h2s)]
    if not first:
        got_sums.append(copies.start(before[1], accs[1]))

    def total(i, left, right):
        if first:
            accs[i][...] = dot_tn(flat(left), flat(right))
            return [copies.start(accs[i], outs[i])]
        got_sums[i].wait()
        both = accs[i][...] + dot_tn(flat(left), flat(right))
        store_parts(both, parts[i], me_ref[0], (ACROSS, EXPAND)[i])
        return [copies.start(parts[i].at[pl.ds(4 * k, 4)], outs[2 * i + k]) for k in (0, 1)]

    for c in got:
        c.wait()
    sent = total(0, acts, gs)
    for c in got_back:
        c.wait()
    gsum = jnp.zeros((1, gs.shape[3]), F32)
    column = jnp.zeros((1, slopes.shape[3]), F32)
    for m in range(2):
        for j in range(2):
            g = gs[m, j]
            du = (dot_nt(g, wcs[...]) * slopes[m, j].astype(F32)).astype(BF)
            dus[m, j] = du
            gsum += jnp.sum(g.astype(F32), 0, keepdims=True)
            column += jnp.sum(du.astype(F32), 0, keepdims=True)
    sent.append(copies.start(dus, duo))
    for c in got_late:
        c.wait()
    sent += total(1, h2s, dus)
    rowid = lax.broadcasted_iota(jnp.int32, sums.shape, 0)
    both = jnp.where(rowid == 0, gsum, jnp.where(rowid == 1, column, 0.0))
    sums[...] = both if first else sums_in[...] + both
    for c in sent:
        c.wait()


def hidden_back(me, pieces, act, slope, h2, wc, before=None):
    _, _, rows, feat = h2.shape
    ff = wc.shape[0]
    first = before is None
    ins = [(me, SMEM)] + [(a, ANY) for a in (*pieces, act, slope, h2, wc)]
    outs = [(shape(slope.shape), ANY)]
    if first:
        outs += [(shape((ff, feat), F32), ANY), (shape((feat, ff), F32), ANY)]
    else:
        ins += [(before[0], ANY), (before[1], ANY), (before[2], VMEM)]
        outs += [(shape((4, ff // 8, feat)), ANY)] * 2 + [(shape((4, feat // 8, ff)), ANY)] * 2
    outs.append((shape((8, feat), F32), VMEM))
    scratch = [
        pltpu.VMEM(h2.shape, BF), pltpu.VMEM(act.shape, BF), pltpu.VMEM(slope.shape, BF),
        pltpu.VMEM(wc.shape, BF), pltpu.VMEM(h2.shape, BF), pltpu.VMEM(slope.shape, BF),
        pltpu.VMEM((ff, feat), F32), pltpu.VMEM((feat, ff), F32),
    ]
    if not first:
        scratch += [pltpu.VMEM((8, ff // 8, feat), BF), pltpu.VMEM((8, feat // 8, ff), BF)]
    return call(
        functools.partial(hidden_back_kernel, first), "hidden_grad", ins, outs, scratch, 15,
        0 if first else 10**10,
    )


def after(value, *others):
    return lax.optimization_barrier((value, others))[0]


def add(*terms):
    return sum(a.astype(F32) for a in terms).astype(BF)


def swap(value, axis, size, bit):
    return lax.ppermute(value, axis, [(i, i ^ bit) for i in range(size)])


class Order:
    def __init__(self):
        self.last = None

    def __call__(self, value):
        if self.last is not None:
            value = after(value, self.last)
        return value

    def step(self, result):
        self.last = result
        return result


class Sum:
    def __init__(self, order, size, keep, send, bits, back, rows=None):
        self.full_rows = keep.shape[1]
        self.rows = rows or self.full_rows
        self.order, self.size, self.bits, self.back = order, size, bits, back
        self.have = keep
        self.flying = swap(order(send), "dp", size, bits[0])

    def kept(self):
        have, got = self.order(self.have)[:, : self.rows], self.flying[:, : self.rows]
        halves = add(have[:2], got[:2]), add(have[2:], got[2:])
        self.have, send = self.order.step(halves)
        self.flying = swap(send, "dp", self.size, self.bits[1])

    def near(self):
        have = self.order(self.have)
        halves = add(have[0], self.flying[0]), add(have[1], self.flying[1])
        self.have, send = self.order.step(halves)
        self.flying = swap(send, "dp", self.size, self.bits[2])

    def own(self, over_tp=0):
        self.have = self.order.step(add(self.order(self.have), self.flying))
        if self.size > 8:
            groups = [[low + 8 * high for high in range(self.size // 8)] for low in range(8)]
            whole = lax.psum(self.have.astype(F32), "dp", axis_index_groups=groups)
            self.have = whole.astype(BF)
        if over_tp:
            self.tail = self.have[over_tp:]
            self.sums = [swap(self.tail, "tp", 4, bit) for bit in (1, 2, 3)]
        else:
            self.flying = swap(self.have, "dp", self.size, self.back[2])

    def over_tp(self, first):
        tail = self.order(self.tail)
        row = lax.broadcasted_iota(jnp.int32, tail.shape, 0) - LANES // 8
        whole = jnp.where((row >= 0) & (row < 4), tail, add(tail, *self.sums))
        self.have = self.order.step(jnp.concatenate([self.have[:first], whole], 0))
        self.flying = swap(self.have, "dp", self.size, self.back[2])

    def pair(self):
        self.have = self.order.step(jnp.stack([self.order(self.have), self.flying]))
        self.flying = swap(self.have, "dp", self.size, self.back[1])

    def four(self):
        whole = jnp.concatenate([self.order(self.have), self.flying], 0)
        padding = self.full_rows - whole.shape[1]
        self.have = self.order.step(jnp.pad(whole, ((0, 0), (0, padding), (0, 0))))
        self.flying = swap(self.have, "dp", self.size, self.back[0])

    def parts(self):
        return self.have, self.flying


def halve_kernel(*refs):
    values, outs, held, sums, sems = refs[:4], refs[4:8], refs[8:12], refs[12:14], refs[14]
    copies = Copies(sems)
    got = [copies.start(a, b) for a, b in zip(values, held)]
    sent = []
    for i in range(2):
        got[2 * i].wait()
        got[2 * i + 1].wait()
        sums[i][...] = (held[2 * i][...].astype(F32) + held[2 * i + 1][...].astype(F32)).astype(BF)
        for k in range(2):
            sent.append(copies.start(sums[i].at[pl.ds(2 * k, 2)], outs[2 * i + k]))
    for c in sent:
        c.wait()


def kept_both(order, first, second):
    values = order((first.have, first.flying, second.have, second.flying))
    outs = [shape((2, *a.shape[1:])) for a in values]
    scratch = [pltpu.VMEM(a.shape, BF) for a in values]
    halves = call(
        halve_kernel, "halve", [(a, ANY) for a in values], [(o, ANY) for o in outs],
        scratch + [scratch[0], scratch[2]], 8, 0,
    )
    order.step(halves)
    for one, (stay, leave) in ((first, halves[:2]), (second, halves[2:])):
        one.have = stay
        one.flying = swap(leave, "dp", one.size, one.bits[1])


class Rows:
    def __init__(self, order, mine, send):
        self.order, self.mine = order, mine
        self.got = swap(order(send), "tp", 4, 1)

    def away(self):
        away = self.order.step(add(self.order(self.mine[1]), self.got[1]))
        self.far = swap(away, "tp", 4, 2)

    def land(self):
        terms = self.order(self.mine[0]), self.got[0], self.far
        self.total = self.order.step(sum(a.astype(F32) for a in terms))


def place_kernel(me_ref, four, other, out):
    i = pl.program_id(0)

    @pl.when(i < 4)
    def _():
        out[...] = four[0].astype(F32)

    @pl.when(i >= 4)
    def _():
        out[...] = other[0].astype(F32)


def place(me, four, other, bits):
    _, part, width = four.shape

    def where(i, me):
        j = i % 4
        order = (j // 2) * bits[1] + (j % 2) * bits[2] + (i // 4) * bits[0]
        return order ^ me[0], 0

    return pl.pallas_call(
        place_kernel,
        grid_spec=pltpu.PrefetchScalarGridSpec(
            num_scalar_prefetch=1,
            grid=(8,),
            in_specs=[
                pl.BlockSpec((1, part, width), lambda i, me: (jnp.minimum(i, 3), 0, 0)),
                pl.BlockSpec((1, part, width), lambda i, me: (jnp.maximum(i - 4, 0), 0, 0)),
            ],
            out_specs=pl.BlockSpec((part, width), where),
        ),
        out_shape=shape((8 * part, width), F32),
        compiler_params=pltpu.CompilerParams(vmem_limit_bytes=32 * 2**20),
        cost_estimate=pl.CostEstimate(flops=0, bytes_accessed=0, transcendentals=0),
        name="place_parts",
    )(me, four, other)


def unpack_kernel(own_q, me_ref, four, other, og, qs, sg, *refs):
    *vectors, shared, lines = refs
    me = me_ref[0]
    cut = own_q // 8
    tall = LANES // 8
    for ref, order in zip((four, other), offsets(ACROSS)):
        for i in range(4):
            b = order[i] ^ me
            part = ref[i].astype(F32)
            rows = lambda size: pl.ds(pl.multiple_of(b * size, 8), size)
            og[rows(cut)] = part[:cut]
            qs[rows(cut)] = part[cut : 2 * cut]
            shared[rows(tall)] = part[2 * cut : 2 * cut + tall]
            last = part[2 * cut + tall : 2 * cut + tall + 8]
            lines[pl.ds(b, 1)] = last[:1]
            lines[pl.ds(b + 8, 1)] = last[4:5]
    sg[...] = shared[...].T
    for ref, (i, base) in zip(vectors, LINES):
        ref[...] = lines[i, base : base + ref.shape[0]]


def unpack(me, four, other, own_q, ff):
    feat = four.shape[2]
    sizes = (feat, ff, own_q, feat, feat, feat, feat, LANES)
    outs = [(own_q, feat), (own_q, feat), (feat, LANES)] + [(n,) for n in sizes]
    return pl.pallas_call(
        functools.partial(unpack_kernel, own_q),
        in_specs=[SMEM, VMEM, VMEM],
        out_specs=[VMEM] * len(outs),
        out_shape=[shape(a, F32) for a in outs],
        scratch_shapes=[pltpu.VMEM((LANES, feat), F32), pltpu.VMEM((16, feat), F32)],
        compiler_params=pltpu.CompilerParams(vmem_limit_bytes=32 * 2**20),
        cost_estimate=pl.CostEstimate(flops=0, bytes_accessed=0, transcendentals=0),
        name="unpack",
    )(me, four, other)


def doc_layout(ends, scales, length):
    row = jnp.arange(length, dtype=jnp.int32)[None]
    begin = jnp.zeros_like(row)
    step = scales[:, :1]
    for d in range(ends.shape[1] - 1):
        past = row >= ends[:, d : d + 1]
        begin = jnp.where(past, ends[:, d : d + 1], begin)
        step = jnp.where(past, scales[:, d + 1 : d + 2], step)
    return (row - begin) * step


def angle_tables(placed, rows):
    freqs = 10000.0 ** (-jnp.arange(ROT // 2, dtype=F32) * 2.0 / ROT)
    blocks = placed.astype(F32).reshape(placed.shape[0], 4, 1, rows)
    angles = blocks * freqs[:, None]
    return jnp.cos(angles), jnp.sin(angles)


def on_device(
    size,
    tokens,
    cotangent,
    doc_ends,
    pos_scale,
    first_gain,
    first_bias,
    second_gain,
    second_bias,
    w_query,
    query_bias,
    w_shared,
    shared_bias,
    w_output,
    w_expand,
    expand_bias,
    w_contract,
    output_bias,
):
    micro, rows, feat = tokens.shape
    heads = w_query.shape[1] // 64
    own_q = w_query.shape[1]
    length = rows * 4
    rank = lax.axis_index("tp").astype(jnp.int32)[None]
    me = (lax.axis_index("dp").astype(jnp.int32) & 7)[None]

    order = Order()

    def begin(values):
        return values, swap(values, "tp", 4, 1), swap(values, "tp", 4, 2)

    def finish(own, near, far):
        return own, near, far, swap(far, "tp", 4, 1)

    xs, gs = begin(tokens), begin(cotangent)

    norms = (first_gain, first_bias, second_gain, second_bias)
    ends, scales = doc_ends[:, 0], pos_scale[:, 0]
    cs, sn = angle_tables(doc_layout(ends, scales, length), rows)

    act_a, slope_a, h1_a, h2_a, n_a = hidden(xs[:2], norms, w_expand, expand_bias)
    order.step(act_a)
    du_a, cacc, eacc, sums = hidden_back(order(me), gs[:2], act_a, slope_a, h2_a, w_contract)
    order.step(sums)
    xs = finish(xs[0], xs[1], order(xs[2]))
    act_b, slope_b, h1_b, h2_b, n_b = hidden(xs[2:], norms, w_expand, expand_bias)
    order.step(act_b)
    h1, n, act = (h1_a, h1_b), (n_a, n_b), (act_a, act_b)
    biases = (query_bias, shared_bias)
    saved0 = attend(
        0, order(rank), doc_ends, h1, w_query.T, w_shared, *biases, cs, sn, heads, 0
    )
    order.step(saved0[0])
    gs = finish(gs[0], gs[1], order(gs[2]))
    du_b, c_keep, c_send, e_keep, e_send, sums = hidden_back(
        order(me), gs[2:], act_b, slope_b, h2_b, w_contract, (cacc, eacc, sums)
    )
    order.step(sums)
    weights = (w_query.T, w_shared, w_output, w_contract, w_expand, first_gain, second_gain)
    inputs = (gs, h1, act, (du_a, du_b), n, *weights, cs, sn, heads)
    c = Sum(order, size, c_keep, c_send, ACROSS, ACROSS)
    e = Sum(order, size, e_keep, e_send, EXPAND, BACK)
    *mine0, send0, og, qs, vec = attend_back(0, order(rank), me, saved0, *inputs)
    order.step(vec)
    kept_both(order, c, e)
    rows0 = Rows(order, mine0, send0)
    *mine1, send1, r_keep, r_send = attend_back(
        1, order(rank), me, (doc_ends, *biases), *inputs, True, (og, qs, vec, sums)
    )
    order.step(r_send)
    filled = 2 * (own_q // 8) + LANES // 8 + 8
    rest = Sum(order, size, r_keep, r_send, ACROSS, ACROSS, filled)
    c.near()
    rows0.away()
    rows1 = Rows(order, mine1, send1)
    e.near()
    rest.kept()
    c.own()
    rest.near()
    e.own()
    c.pair()
    rest.own(2 * (own_q // 8))
    rest.over_tp(2 * (own_q // 8))
    e.pair()
    rows0.land()
    rows1.away()
    c.four()
    rest.pair()
    e.four()
    contract_grad = order.step(place(order(me), *c.parts(), ACROSS))
    rest.four()
    rows1.land()
    layer_out, input_grad = order.step(
        final_rows(order(tokens), cotangent, output_bias, (rows0.total, rows1.total))
    )
    expand_grad = order.step(place(order(me), *e.parts(), BACK))
    output_grad, query_grad, shared_grad, *vectors = unpack(
        me, *rest.parts(), own_q, expand_bias.shape[0]
    )
    out_bias, hidden_bias, query_bias, gain1, bias1, gain2, bias2, kv_bias = vectors

    return (
        layer_out,
        input_grad,
        query_grad.T,
        query_bias,
        shared_grad,
        kv_bias,
        output_grad,
        expand_grad,
        hidden_bias,
        contract_grad,
        out_bias,
        gain1,
        bias1,
        gain2,
        bias2,
    )


def final_rows(tokens, cotangent, output_bias, terms):
    joined = lambda which: jnp.stack([t[which] for t in terms])
    x = tokens.astype(F32)
    layer_out = (x + joined(0) + output_bias).astype(BF)
    norm, scale = normalize_rows(x)
    e = joined(1)
    slope_mean = jnp.mean(e * norm, -1, keepdims=True)
    input_grad = cotangent.astype(F32) + scale * (
        e - jnp.mean(e, -1, keepdims=True) - norm * slope_mean
    )
    return layer_out, input_grad


def normalize_rows(x):
    centre = x - jnp.mean(x, -1, keepdims=True)
    scale = lax.rsqrt(jnp.mean(centre * centre, -1, keepdims=True) + 1e-05)
    return centre * scale, scale


def solution(mesh):
    rows = P(None, ("dp", "tp"), None)
    in_specs = (
        rows, rows, P(None, "dp", None), P(None, "dp", None),
        P(), P(), P(), P(),
        P(None, "tp"), P("tp"), P(), P(), P("tp", None),
        P(None, "tp"), P("tp"), P("tp", None), P(),
    )
    out_specs = (
        rows, rows,
        P(None, "tp"), P("tp"), P(), P(), P("tp", None),
        P(None, "tp"), P("tp"), P("tp", None),
        P(), P(), P(), P(), P(),
    )
    return jax.shard_map(
        functools.partial(on_device, mesh.shape["dp"]),
        mesh=mesh,
        in_specs=in_specs,
        out_specs=out_specs,
        check_vma=False,
    )
```
